32 devices in a mesh: seq: 2 (over y), tp: 4 (over z), dp: 4 (over x, core).
Axes of the slice: x: 2, y: 2, z: 4, core: 2. Of those that a mesh axis runs over, the one named last changes fastest.
Arguments:
- query_rows: bfloat16 [4, 256, 2048], P('dp', 'seq', 'tp'), may hold values from -8 to 8
- key_rows: bfloat16 [4, 256, 256], P('dp', 'seq', 'tp'), may hold values from -6 to 6
- value_rows: bfloat16 [4, 256, 256], P('dp', 'seq', 'tp'), may hold values from -6 to 6
- gate_rows: bfloat16 [4, 256, 2048], P('dp', 'seq', 'tp'), may hold values from -6 to 6
- write_vec: bfloat16 [4, 256, 128], P('dp', 'seq'), may hold values from -0.5 to 0.5
- read_vec: bfloat16 [4, 256, 128], P('dp', 'seq'), may hold values from -0.5 to 0.5
- dt_raw: float32 [4, 32, 256], P('dp', 'tp', 'seq'), may hold values from -4 to 4
- a_log: float32 [32], P('tp')
- skip_gain: float32 [32], P('tp'), may hold values from 0.5 to 1.5
- dt_bias: float32 [32], P('tp'), may hold values from -1 to 1
- out_grad: bfloat16 [4, 256, 2048], P('dp', 'seq', 'tp'), may hold values from -6 to 6
Outputs:
- grad_query: float32 [4, 256, 2048], P('dp', 'seq', 'tp')
- grad_key: float32 [4, 256, 256], P('dp', 'seq', 'tp')
- grad_value: float32 [4, 256, 256], P('dp', 'seq', 'tp')
- grad_gate: float32 [4, 256, 2048], P('dp', 'seq', 'tp')
- grad_write: float32 [4, 256, 128], P('dp', 'seq')
- grad_read: float32 [4, 256, 128], P('dp', 'seq')
- grad_dt: float32 [4, 32, 256], P('dp', 'tp', 'seq')
- grad_alog: float32 [32], P('tp')
- grad_skip: float32 [32], P('tp')
- grad_bias: float32 [32], P('tp')
The draws below stay inside these ranges and needn't reach their ends.
All inputs are finite; a program needn't handle non-finite values.
Results may differ from the reference program's by a relative error of at most 0.024.
Values may be sent and summed in bfloat16 or wider, within the bound.
No kernel may reach another device: no remote copies, remote signals or barrier semaphores. Data moves between devices by JAX's collectives and lax.ppermute only.
A program may use at most 64 MiB of HBM per device.

```python
import math
import jax
import jax.numpy as jnp
from jax import lax

HD = 128
MP = 64
NS = 128
QH = 16
KVH = 2
MH = 32
LEN = 256
SEQS = 4


def draw_query_rows(key, part):
    key = jax.random.fold_in(key, 101)
    values = 2.0 * jax.random.truncated_normal(key, -4.0, 4.0, (SEQS, LEN, QH * HD), jnp.float32)
    return values.astype(jnp.bfloat16)


def draw_key_rows(key, part):
    key = jax.random.fold_in(key, 202)
    values = jax.random.truncated_normal(key, -4.0, 4.0, (SEQS, LEN, KVH * HD), jnp.float32)
    return values.astype(jnp.bfloat16)


def draw_a_log(key, part):
    key = jax.random.fold_in(key, 303)
    spread = jax.random.uniform(key, (MH,), jnp.float32)
    lowest = jnp.log(0.05 / LEN)
    highest = jnp.log(0.05)
    return (lowest + spread * (highest - lowest)).astype(jnp.float32)


def block_levels(key, extent, cuts, low, largest):
    factor_of = 1.0
    for axis_at, shards_of in cuts:
        draws = jax.random.uniform(jax.random.fold_in(jax.random.fold_in(key, 6), axis_at), (shards_of,), jnp.float32, low / len(cuts), largest / len(cuts))
        factor_of = factor_of * jnp.repeat(jnp.exp(draws), extent[axis_at] // shards_of).reshape((-1,) + (1,) * (len(extent) - 1 - axis_at))
    return factor_of


def scatter_about(stream_key, dims, scale, most, shards=(), held_as=jnp.bfloat16):
    level = block_levels(stream_key, dims, shards, -0.22, 0.18) if shards else 1.0
    result = jax.random.normal(stream_key, dims, jnp.float32) * scale * level
    return jnp.minimum(jnp.maximum(result, -most), most).astype(held_as)


def setup_inputs(seed: int = 0) -> dict:
    streams_of = jax.random.split(jax.random.key(seed), 12)
    return {
        "query_rows": draw_query_rows(jax.random.fold_in(streams_of[11], 71), 0),
        "key_rows": draw_key_rows(jax.random.fold_in(streams_of[11], 71), 0),
        "value_rows": scatter_about(streams_of[2], (SEQS, LEN, KVH * HD), 1.0, 6.0, ((0, 4), (1, 2), (2, 4))),
        "gate_rows": scatter_about(streams_of[3], (SEQS, LEN, MH * MP), 1.0, 6.0, ((0, 4), (1, 2), (2, 4))),
        "write_vec": scatter_about(streams_of[4], (SEQS, LEN, NS), NS ** -0.5, 0.5, ((0, 4), (1, 2))),
        "read_vec": scatter_about(streams_of[5], (SEQS, LEN, NS), NS ** -0.5, 0.5, ((0, 4), (1, 2))),
        "dt_raw": scatter_about(streams_of[6], (SEQS, MH, LEN), 1.0, 4.0, ((0, 4), (1, 4), (2, 2)), jnp.float32),
        "a_log": draw_a_log(jax.random.fold_in(streams_of[11], 71), 0),
        "skip_gain": jnp.clip(0.5 + 1.0 * jax.random.uniform(streams_of[8], (MH,), jnp.float32) ** block_levels(streams_of[8], (MH,), ((0, 4),), -0.2, 0.2), 0.5, 1.5),
        "dt_bias": jnp.clip(jax.random.uniform(streams_of[9], (MH,), jnp.float32, -1.0, 1.0) * block_levels(streams_of[9], (MH,), ((0, 4),), -0.4, 0.0), -1.0, 1.0),
        "out_grad": scatter_about(streams_of[10], (SEQS, LEN, MH * MP), 1.0, 6.0, ((0, 4), (1, 2), (2, 4))),
    }


NEG_FILL = -1e+30
HIGH = lax.Precision.HIGHEST

def block_scan(inner, gate_in, write_in, read_in, dt_raw, a_log, skip_gain, dt_bias):
    num_rows, num_heads, head_width = inner.shape
    num_states = write_in.shape[1]
    block_len = math.gcd(num_rows, 256)
    block_count = num_rows // block_len
    step_dt = jax.nn.softplus(dt_raw + dt_bias[:, None])
    rate_all = step_dt * jnp.exp(a_log)[:, None]
    rate_blocks = rate_all.reshape(num_heads, block_count, block_len).transpose(1, 0, 2)
    dt_blocks = step_dt.reshape(num_heads, block_count, block_len).transpose(1, 0, 2)
    inner_blocks = inner.reshape(block_count, block_len, num_heads, head_width)
    write_blocks = write_in.reshape(block_count, block_len, num_states)
    read_blocks = read_in.reshape(block_count, block_len, num_states)
    causal = jnp.arange(block_len)[:, None] >= jnp.arange(block_len)[None, :]

    def advance(carried, pieces):
        rate_now, dt_now, inner_now, write_now, read_now = pieces
        cum_rate = jnp.cumsum(rate_now, axis=1)
        intersection = jnp.dot(read_now, write_now.T, precision=HIGH)
        log_gap = cum_rate[:, :, None] - cum_rate[:, None, :]
        weight = jnp.where(causal, jnp.exp(-jnp.maximum(log_gap, 0.0)), 0.0) * intersection[None] * dt_now[:, None, :]
        output = jnp.einsum('hts,shp->thp', weight, inner_now, precision=HIGH)
        output = output + jnp.einsum('tn,hpn->thp', read_now, carried, precision=HIGH) * jnp.exp(-cum_rate).T[:, :, None]
        to_end = jnp.exp(-(cum_rate[:, -1:] - cum_rate)) * dt_now
        next_state = jnp.exp(-cum_rate[:, -1])[:, None, None] * carried + jnp.einsum('hs,shp,sn->hpn', to_end, inner_now, write_now, precision=HIGH)
        return (next_state, output)
    zero_state = jnp.zeros((num_heads, head_width, num_states), jnp.float32)
    end_state, outputs = lax.scan(advance, zero_state, (rate_blocks, dt_blocks, inner_blocks, write_blocks, read_blocks))
    mixed_out = outputs.reshape(num_rows, num_heads, head_width) + skip_gain[None, :, None] * inner
    gated_out = mixed_out.reshape(num_rows, num_heads * head_width) * jax.nn.silu(gate_in)
    return (gated_out, end_state, jnp.exp(-lax.optimization_barrier(jnp.sum(rate_all, axis=1))))

def sequence_grads(query_seq, key_seq, value_seq, gate_seq, write_seq, read_seq, raw_dt, a_log, skip_gain, dt_bias, cotangent):
    scale = HD ** (-0.5)
    group = QH // KVH
    heads_q = query_seq.reshape(LEN, QH, HD).transpose(1, 0, 2)
    heads_k = key_seq.reshape(LEN, KVH, HD).transpose(1, 0, 2)
    heads_v = value_seq.reshape(LEN, KVH, HD).transpose(1, 0, 2)
    position = jnp.arange(LEN)
    allowed = position[:, None] >= position[None, :]

    def head_scores(index):
        raw_scores = jnp.dot(heads_q[index], heads_k[index // group].T, preferred_element_type=jnp.float32) * scale
        return jnp.where(allowed, raw_scores, NEG_FILL)

    def forward_head(index):
        scores = head_scores(index)
        row_max = lax.optimization_barrier(jnp.max(scores, axis=1))
        exp_scores = jnp.exp(scores - row_max[:, None])
        row_total = lax.optimization_barrier(jnp.sum(exp_scores, axis=1))
        attn = jnp.dot(exp_scores.astype(jnp.bfloat16), heads_v[index // group], preferred_element_type=jnp.float32) / row_total[:, None]
        return (attn, row_max + jnp.log(row_total))
    attn, log_sum = lax.map(forward_head, jnp.arange(QH))
    inner = attn.transpose(1, 0, 2).reshape(LEN, MH, MP)
    primal_out, pullback = jax.vjp(block_scan, inner, gate_seq.astype(jnp.float32), write_seq.astype(jnp.float32), read_seq.astype(jnp.float32), raw_dt, a_log, skip_gain, dt_bias)
    zero_state = jnp.zeros((MH, MP, NS), jnp.float32)
    grads = pullback((cotangent.astype(jnp.float32), zero_state, jnp.zeros((MH,), jnp.float32)))
    grad_inner, grad_gate, grad_write, grad_read, grad_dt, grad_alog, grad_skip, grad_bias = grads
    grad_attn = grad_inner.reshape(LEN, QH, HD).transpose(1, 0, 2)
    delta = lax.optimization_barrier(jnp.sum(grad_attn * attn, axis=2))
    grad_low = grad_attn.astype(jnp.bfloat16)

    def backward_head(index):
        scores = head_scores(index)
        probs = jnp.exp(scores - log_sum[index][:, None])
        probs_low = probs.astype(jnp.bfloat16)
        key_one = heads_k[index // group]
        value_one = heads_v[index // group]
        grad_value = jnp.dot(probs_low.T, grad_low[index], preferred_element_type=jnp.float32)
        grad_probs = jnp.dot(grad_low[index], value_one.T, preferred_element_type=jnp.float32)
        grad_scores = (probs * (grad_probs - delta[index][:, None])).astype(jnp.bfloat16)
        grad_query = jnp.dot(grad_scores, key_one, preferred_element_type=jnp.float32) * scale
        grad_key = jnp.dot(grad_scores.T, heads_q[index], preferred_element_type=jnp.float32) * scale
        return (grad_query, grad_key, grad_value)
    grad_query, grad_key, grad_value = lax.map(backward_head, jnp.arange(QH))
    grad_query = grad_query.transpose(1, 0, 2).reshape(LEN, QH * HD)
    grad_key = grad_key.reshape(KVH, group, LEN, HD).sum(axis=1).transpose(1, 0, 2).reshape(LEN, KVH * HD)
    grad_value = grad_value.reshape(KVH, group, LEN, HD).sum(axis=1).transpose(1, 0, 2).reshape(LEN, KVH * HD)
    return (grad_query, grad_key, grad_value, grad_gate, grad_write, grad_read, grad_dt, grad_alog, grad_skip, grad_bias)

def reference(query_rows, key_rows, value_rows, gate_rows, write_vec, read_vec, dt_raw, a_log, skip_gain, dt_bias, out_grad):

    def one_sequence(pieces):
        query_seq, key_seq, value_seq, gate_seq, write_seq, read_seq, raw_dt, cotangent = pieces
        return sequence_grads(query_seq, key_seq, value_seq, gate_seq, write_seq, read_seq, raw_dt, a_log, skip_gain, dt_bias, cotangent)
    results = lax.map(one_sequence, (query_rows, key_rows, value_rows, gate_rows, write_vec, read_vec, dt_raw, out_grad))
    return (results[0], results[1], results[2], results[3], results[4], results[5], results[6], lax.optimization_barrier(jnp.sum(results[7], axis=0)), lax.optimization_barrier(jnp.sum(results[8], axis=0)), lax.optimization_barrier(jnp.sum(results[9], axis=0)))
```

```python
import jax
import jax.numpy as jnp
from jax import lax
from jax.experimental import pallas as pl
from jax.experimental.pallas import tpu as pltpu
from jax.sharding import PartitionSpec as P

NEG_FILL = -1e30
LOG2E = 1.4426950408889634
F32 = jnp.float32
BF16 = jnp.bfloat16
NN = (((1,), (0,)), ((), ()))
NT = (((1,), (1,)), ((), ()))
TN = (((0,), (0,)), ((), ()))


def dot(a, b, dims=NN):
    return lax.dot_general(a.astype(BF16), b.astype(BF16), dims, preferred_element_type=F32)


def parts_of(array, count):
    parts = []
    for _ in range(count):
        parts.append(array.astype(BF16))
        array = array - parts[-1].astype(F32)
    return parts


def dot_flags(arrays, flags, count=3):
    split_up = [parts_of(a, count) for a in arrays]
    left = [parts[i] for i in range(count) for parts in split_up]
    right = jnp.concatenate([jnp.where(f, 1.0, 0.0) for f in flags] * count, axis=0)
    return dot(jnp.concatenate(left, axis=1), right)


def iota(shape, axis):
    return lax.broadcasted_iota(jnp.int32, shape, axis)


def column(ref, width):
    heads = ref.shape[0]
    at = iota((heads, width), 0)
    out = jnp.full((heads, width), ref[0], F32)
    for m in range(1, heads):
        out = jnp.where(at == m, ref[m], out)
    return out


def rates(raw, bias, alog):
    rows = raw.shape[1]
    shifted = raw + bias
    step = jnp.maximum(shifted, 0.0) + jnp.log1p(jnp.exp(-jnp.abs(shifted)))
    rate = step * jnp.exp(alog)
    return step, rate, dot_flags([rate], [iota((rows, rows), 0) <= iota((rows, rows), 1)])


def spread(cols, m, width):
    return jnp.broadcast_to(cols[:, m : m + 1], (cols.shape[0], width))


def widen(factors, channels):
    heads = factors.shape[0]
    shape = (3 * heads, heads * channels)
    pick = (iota(shape, 1) // channels == iota(shape, 0) % heads).astype(BF16)
    return dot(jnp.concatenate(parts_of(factors, 3), axis=0), pick, TN)


def stack(wide, width):
    return jnp.concatenate([wide[:, i : i + width] for i in range(0, wide.shape[1], width)], axis=0)


def unstack(tall, rows):
    return jnp.concatenate([tall[i : i + rows] for i in range(0, tall.shape[0], rows)], axis=1)


def attend(jobs, scale):
    shapes = [(q.shape[0] // m.shape[0],) + m.shape for q, _, _, m in jobs]
    scores = [
        jnp.where(m[None], (dot(q, k) * (scale * LOG2E)).reshape(dims), NEG_FILL)
        for (q, k, _, m), dims in zip(jobs, shapes)
    ]
    tops = [jnp.max(s, axis=2, keepdims=True) for s in scores]
    weights = [
        jnp.exp2(s - top).reshape(dims[0] * dims[1], dims[2])
        for s, top, dims in zip(scores, tops, shapes)
    ]
    both = [
        dot(w, jnp.concatenate([v, jnp.ones_like(v)], axis=0), NT)
        for w, (_, _, v, _) in zip(weights, jobs)
    ]
    width = jobs[0][2].shape[0]
    shares = [1.0 / b[:, width:] for b in both]
    return [(b[:, :width] * share, w, share) for b, w, share in zip(both, weights, shares)]


def _fold(join, parts):
    out = parts[0]
    for part in parts[1:]:
        out = join(out, part)
    return out


def slot_mask(here, query_slot, slots, rows):
    masks = []
    for slot in slots:
        if slot == query_slot:
            masks.append(iota((rows, rows), 0) >= iota((rows, rows), 1))
        else:
            seen = jnp.bitwise_xor(here, slot) < jnp.bitwise_xor(here, query_slot)
            masks.append(jnp.broadcast_to(seen, (rows, rows)))
    return jnp.concatenate(masks, axis=1)


def share_kernel(*refs):
    sources, (pack, message), held, arrived = refs[:10], refs[10:12], refs[12:22], refs[22]
    copies = [
        pltpu.make_async_copy(source, here, arrived.at[i])
        for i, (source, here) in enumerate(zip(sources, held))
    ]
    for copy in copies:
        copy.start()
    raw, alog, bias, gate, cotangent, read, query, key, value, write = held
    for copy in copies[:3]:
        copy.wait()
    here = lax.axis_index("seq")
    heads, rows = raw.shape[1:]
    wide, states = gate.shape[2], read.shape[2]
    half = key.shape[1]
    step, _, cum = rates(raw[0], column(bias, rows), column(alog, rows))
    decay = widen(jnp.exp(-cum), wide // heads)
    to_end = jnp.exp(cum - cum[:, rows - 1 :]) * step
    whole = jnp.broadcast_to(jnp.exp(-cum[:, rows - 1 :]), (heads, rows))
    tail = jnp.concatenate([to_end, whole], axis=0).astype(BF16)
    for copy in copies[3:]:
        copy.wait()
    pack[:half] = key[0]
    pack[half:] = value[0]
    gate_f = gate[0].astype(F32)
    grad_mixed = cotangent[0].astype(F32) * gate_f * jax.nn.sigmoid(gate_f)
    entry = dot(read[0], grad_mixed * decay, TN).astype(BF16)
    for bit in range(message.shape[0]):
        is_early = jnp.bitwise_and(lax.shift_right_logical(here, bit), 1) == 0
        for at in range(0, wide, states):
            message[bit, at : at + rows] = jnp.where(
                is_early, query[0, :, at : at + states], entry[:, at : at + states]
            )
        message[bit, wide : wide + half] = key[0]
        message[bit, wide + half : wide + 2 * half] = value[0]
        message[bit, wide + rows : wide + 2 * rows] = write[0]
        message[bit, wide + 2 * rows :] = tail


def prepare_kernel(gate, cotangent, write, read, raw, alog, skip, bias, *outs):
    mixed_out, slope_out, step_out, in_out, out_out, own_out, fall_out, back_out = outs[:8]
    ahead_out, split_out, rates_out, skip_out = outs[8:]
    heads, rows = raw.shape[1:]
    wide = gate.shape[2]
    channels = wide // heads
    pair = 2 * channels
    alog_c, bias_c = column(alog, rows), column(bias, rows)
    step, rate, cum = rates(raw[0], bias_c, alog_c)
    for i, table in enumerate((step, rate, cum, jnp.exp(alog_c), jax.nn.sigmoid(raw[0] + bias_c))):
        rates_out[i * heads : (i + 1) * heads] = table
    head_of = iota(skip_out.shape, 1) // channels
    skip_w = jnp.full(skip_out.shape, skip[0], F32)
    for m in range(1, heads):
        skip_w = jnp.where(head_of == m, skip[m], skip_w)
    skip_out[...] = skip_w
    gate_f = gate[0].astype(F32)
    sig = jax.nn.sigmoid(gate_f)
    cot = cotangent[0].astype(F32)
    grad_mixed = cot * gate_f * sig
    mixed_out[...] = grad_mixed
    slope_out[...] = cot * sig * (1.0 + gate_f * (1.0 - sig))
    cum_cols = cum.T
    step_out[...] = widen(step, channels)
    in_out[...] = widen(jnp.exp(-cum), channels)
    out_out[...] = widen(jnp.exp(cum - cum[:, rows - 1 :]), channels)
    read_b, write_b = read[0], write[0]
    upper = iota((rows, rows), 0) <= iota((rows, rows), 1)
    lower = iota((rows, rows), 0) >= iota((rows, rows), 1)
    cross = jnp.where(lower, dot(read_b, write_b, NT), 0.0)
    cross_t = jnp.where(upper, dot(write_b, read_b, NT), 0.0)
    low = iota((rows, pair), 1) < channels
    for m in range(0, heads, 2):
        block = slice(m * channels, (m + 2) * channels)
        grad_p = grad_mixed[:, block]
        grad_d = jnp.concatenate(
            [jnp.where(low, grad_p, 0.0), jnp.where(low, 0.0, grad_p)], axis=0
        ).astype(BF16)
        split_out[m * rows : (m + 2) * rows] = grad_d
        backs = []
        for k in range(m, m + 2):
            gap = spread(cum_cols, k, rows) - cum[k : k + 1, :]
            fall = jnp.exp(-jnp.abs(gap))
            back = fall * cross_t
            at = slice(k * rows, (k + 1) * rows)
            fall_out[at] = fall
            back_out[at] = back
            ahead_out[:, at] = (fall * cross).astype(BF16)
            backs.append(back.astype(BF16))
        own_out[:, block] = dot(jnp.concatenate(backs, axis=1), grad_d)


def state_kernel(slots, scale, query, write, read, partner, *refs):
    mixed_in, step_in, in_in, out_in, own_in, fall_in, split_in, skip_in = refs[:8]
    refs = refs[8:]
    far, sources, refs = refs[: slots - 1], refs[slots - 1 : 2 * slots - 1], refs[2 * slots - 1 :]
    kept, sent, scores_out, keys_out, scaled_out, base_out, products_out = refs[:7]
    (pack, *messages), arrived = refs[7 : 7 + slots], refs[7 + slots]
    copies = [
        pltpu.make_async_copy(source, held, arrived.at[i])
        for i, (source, held) in enumerate(zip(sources, (pack, *messages)))
    ]
    for copy in copies:
        copy.start()
    here = lax.axis_index("seq")
    parity = lax.axis_index("tp") % 2
    rows, wide = query.shape[1:]
    heads = fall_in.shape[0] // rows
    channels = wide // heads
    states, head_dim = write.shape[2], pack.shape[0]
    half, pair, count = head_dim // 2, 2 * channels, wide // head_dim
    for copy in copies:
        copy.wait()

    key_parts, value_parts = [], []
    for slot in range(slots):
        near = messages[slot - 1][wide : wide + head_dim] if slot else pack[...]
        paired = far[slot - 1][...] if slot else partner[...]
        first = jnp.where(parity == 0, near, paired)
        second = jnp.where(parity == 0, paired, near)
        key_parts.append(jnp.concatenate([first[:half], second[:half]], axis=0))
        value_parts.append(jnp.concatenate([first[half:], second[half:]], axis=0))
    keys, values = jnp.concatenate(key_parts, axis=1), jnp.concatenate(value_parts, axis=1)
    keys_out[...] = keys

    grad_mixed, step_w, decay_in, decay_out = mixed_in[...], step_in[...], in_in[...], out_in[...]
    skip_w = skip_in[:1]
    read_b, write_b = read[0], write[0]
    tails = [m[wide + 2 * rows :].astype(F32) for m in messages]
    exit_t = jnp.zeros((states, wide), F32)
    early, to_ends = [], []
    for slot in range(1, slots):
        block = jnp.bitwise_xor(here, slot)
        early.append(block < here)
        between = jnp.ones((heads, rows), F32)
        for third in range(1, slots):
            if third != slot:
                at = jnp.bitwise_xor(here, third)
                inside = jnp.logical_and(
                    at > jnp.minimum(block, here), at < jnp.maximum(block, here)
                )
                between = between * jnp.where(inside, tails[third - 1][heads:], 1.0)
        later = unstack(messages[slot - 1][:wide], rows).astype(F32)
        if slots > 2:
            later = later * widen(between, channels)
        exit_t = exit_t + jnp.where(early[-1], 0.0, later)
        to_ends.append(widen(tails[slot - 1][:heads] * between, channels))
    exit_b = exit_t.astype(BF16)
    from_exit = decay_out * dot(write_b, exit_b)
    grad_scaled = own_in[...] + from_exit
    grad_inner = step_w * grad_scaled + skip_w * grad_mixed
    grads = stack(grad_inner, head_dim)
    grads_b = grads.astype(BF16)

    queries = stack(query[0], head_dim)
    jobs = [(queries, keys, values, slot_mask(here, 0, range(slots), rows))]
    for slot in range(1, slots):
        whole = slots > 2
        mask = slot_mask(here, slot, range(slots) if whole else [slot], rows)
        some = (keys, values) if whole else (key_parts[slot], value_parts[slot])
        jobs.append((messages[slot - 1][:wide], *some, mask))
    (attn, weights, share), *before = attend(jobs, scale)
    grad_probs = dot(grads_b, values)
    inner = unstack(attn, rows)
    scaled = inner * step_w
    scaled_b = scaled.astype(BF16)
    scaled_out[...] = scaled_b
    entry_t = jnp.zeros((states, wide), F32)
    for message, is_early, to_end, (attn_o, _, _) in zip(messages, early, to_ends, before):
        carried = unstack(attn_o, rows) * to_end
        end_state = dot(message[wide + rows : wide + 2 * rows], carried, TN)
        entry_t = entry_t + jnp.where(is_early, end_state, 0.0)
    entry_b = entry_t.astype(BF16)
    from_entry = decay_in * dot(read_b, entry_b)
    base_out[...] = from_entry + skip_w * inner

    product = grads * attn
    ones = jnp.ones((2 * head_dim, head_dim), BF16)
    delta = dot(jnp.concatenate(parts_of(product, 2), axis=1), ones)
    probs = weights * jnp.concatenate([share] * slots, axis=1)
    grad_scores = (probs * (grad_probs - jnp.concatenate([delta] * slots, axis=1))).astype(BF16)
    scores_out[...] = grad_scores
    key_t = (dot(queries, grad_scores, TN) * scale).astype(BF16)
    value_t = dot(grads_b, probs, TN).astype(BF16)
    for slot in range(slots):
        block = slice(slot * rows, (slot + 1) * rows)
        first = jnp.concatenate([key_t[:half, block], value_t[:half, block]], axis=0)
        second = jnp.concatenate([key_t[half:, block], value_t[half:, block]], axis=0)
        kept[slot] = jnp.where(parity == 0, first, second)
        sent[slot * head_dim : (slot + 1) * head_dim] = jnp.where(parity == 0, second, first)

    upper = iota((rows, rows), 0) <= iota((rows, rows), 1)
    grad_cross_t = jnp.zeros((rows, rows), F32)
    for m in range(0, heads, 2):
        outer = dot(
            scaled_b[:, m * channels : (m + 2) * channels], split_in[m * rows : (m + 2) * rows], NT
        )
        grad_cross_t = grad_cross_t + outer[:, :rows] * fall_in[m * rows : (m + 1) * rows]
        grad_cross_t = grad_cross_t + outer[:, rows:] * fall_in[(m + 1) * rows : (m + 2) * rows]
    grad_cross_t = jnp.where(upper, grad_cross_t, 0.0)
    grad_write = dot(grad_cross_t, read_b) + dot(scaled * decay_out, exit_b, NT)
    grad_read = dot(grad_cross_t, write_b, TN) + dot(grad_mixed * decay_in, entry_b, NT)
    sent[slots * head_dim : slots * head_dim + rows] = grad_write.astype(BF16)
    sent[slots * head_dim + rows :] = grad_read.astype(BF16)
    products = (
        inner * grad_scaled,
        inner * from_exit,
        grad_mixed * from_entry,
        grad_mixed * inner,
        exit_t * entry_t,
    )
    for i, product in enumerate(products):
        products_out[i * rows : (i + 1) * rows] = product.astype(BF16)


def rates_kernel(products, scaled, halves, back, tables, grad_raw, params):
    heads, rows = grad_raw.shape[1:]
    wide = products.shape[1]
    channels = wide // heads
    step, rate, cum, grow, slope = [tables[i * heads : (i + 1) * heads] for i in range(5)]
    strict = iota((rows, rows), 0) < iota((rows, rows), 1)
    lower = iota((rows, rows), 0) >= iota((rows, rows), 1)
    terms = []
    for m in range(0, heads, 2):
        outer = dot(
            scaled[:, m * channels : (m + 2) * channels], halves[m * rows : (m + 2) * rows], NT
        )
        terms.append((outer[:, :rows] * back[m * rows : (m + 1) * rows]).astype(BF16))
        terms.append((outer[:, rows:] * back[(m + 1) * rows : (m + 2) * rows]).astype(BF16))
    later = dot(jnp.concatenate(terms, axis=0), jnp.where(lower, 1.0, 0.0))
    rate_rows = [
        jnp.sum(jnp.where(strict, later[m * rows : (m + 1) * rows], 0.0), axis=0, keepdims=True)
        for m in range(heads)
    ]
    pick = (iota((heads, wide), 1) // channels == iota((heads, wide), 0)).astype(BF16)
    sums = dot(pick, products[...], NT)
    grad_step = sums[:, :rows]
    exit_sum = sums[:, rows : 2 * rows] * step
    entry_sum = sums[:, 2 * rows : 3 * rows]
    skip_sum = sums[:, 3 * rows : 4 * rows]
    carry_sum = jnp.sum(sums[:, 4 * rows :], axis=1, keepdims=True) * jnp.exp(-cum[:, rows - 1 :])
    grad_rate = -(
        jnp.concatenate(rate_rows, axis=0)
        + dot_flags([entry_sum, exit_sum], [lower, strict])
        + carry_sum
    )
    grad_shift = (grad_step + grad_rate * grow) * slope
    grad_raw[0] = grad_shift
    terms = jnp.concatenate([grad_rate * rate, skip_sum, grad_shift], axis=0)
    summed = jnp.concatenate(parts_of(terms, 3), axis=1)
    params[:, : 3 * heads] = dot(jnp.ones((8, 3 * rows), F32), summed, NT)
    params[:, 3 * heads :] = jnp.zeros((8, params.shape[1] - 3 * heads), F32)


def output_kernel(scale, ahead, scaled, base, slope, scores, keys, grad_gate, grad_query):
    rows, wide = base.shape
    channels = wide * rows // ahead.shape[1]
    pair = 2 * channels
    low = iota((rows, pair), 1) < channels
    for at in range(0, wide, pair):
        block = slice(at, at + pair)
        scaled_p = scaled[:, block].astype(F32)
        scaled_d = jnp.concatenate(
            [jnp.where(low, scaled_p, 0.0), jnp.where(low, 0.0, scaled_p)], axis=0
        )
        m = at // channels
        mixed = dot(ahead[:, m * rows : (m + 2) * rows], scaled_d) + base[:, block]
        grad_gate[0, :, block] = mixed * slope[:, block]
    grad_query[0] = unstack(dot(scores[...], keys[...], NT) * scale, rows)


def finish_kernel(count, *refs):
    arrived, (mine, other, tail, shared, got) = refs[:count], refs[count : count + 5]
    grad_key, grad_value, grad_write, grad_read, grad_alog, grad_skip, grad_bias = refs[count + 5 :]
    half, rows = grad_key.shape[1:]
    total = mine[0].astype(F32) + other[: 2 * half].astype(F32)
    for term in arrived:
        total = total + term[: 2 * half].astype(F32)
    grad_key[0] = total[:half]
    grad_value[0] = total[half:]
    both = shared[...].astype(F32) + got[...].astype(F32)
    grad_write[0] = both[:rows]
    grad_read[0] = both[rows:]
    heads = grad_alog.shape[0]
    params = joined(tail[...]) + joined(arrived[-1][2 * half :])
    grad_alog[...] = params[0, :heads]
    grad_skip[...] = params[0, heads : 2 * heads]
    grad_bias[...] = params[0, 2 * heads : 3 * heads]


def split(sums):
    high = lax.reduce_precision(sums, 8, 7)
    return jnp.concatenate([high.astype(BF16), (sums - high).astype(BF16)], axis=0)


def joined(tail):
    tail = tail.astype(F32)
    count = tail.shape[0] // 2
    return tail[:count] + tail[count:]


def flip(axis, distance):
    return [(i, i ^ distance) for i in range(lax.axis_size(axis))]


def shape(dims, dtype):
    return jax.ShapeDtypeStruct(tuple(dims), dtype)


VMEM = pl.BlockSpec(memory_space=pltpu.VMEM)
SMEM = pl.BlockSpec(memory_space=pltpu.SMEM)
HBM = pl.BlockSpec(memory_space=pltpu.HBM)
PARAMS = pltpu.CompilerParams(vmem_limit_bytes=48 * 1024 * 1024)


def call(kernel, outs, args, specs=None, scratch=(), flops=0):
    return pl.pallas_call(
        kernel,
        out_shape=outs,
        in_specs=[(specs or {}).get(i, VMEM) for i in range(len(args))],
        out_specs=jax.tree.map(lambda _: VMEM, outs),
        scratch_shapes=scratch,
        compiler_params=PARAMS,
        cost_estimate=pl.CostEstimate(flops=flops, bytes_accessed=0, transcendentals=0),
    )(*args)


def swap(array, seq_bits, tp_bits, to_later=None):
    n_seq, n_tp = lax.axis_size("seq"), lax.axis_size("tp")
    pairs = [
        (s * n_tp + t, (s ^ seq_bits) * n_tp + (t ^ tp_bits))
        for s in range(n_seq)
        for t in range(n_tp)
        if to_later is None or ((s ^ seq_bits) > s) == to_later
    ]
    return lax.ppermute(array, ("seq", "tp"), pairs)


def body(
    query_rows,
    key_rows,
    value_rows,
    gate_rows,
    write_vec,
    read_vec,
    dt_raw,
    a_log,
    skip_gain,
    dt_bias,
    out_grad,
):
    slots = lax.axis_size("seq")
    rows, wide = query_rows.shape[1:]
    head_dim = 2 * key_rows.shape[2]
    states = write_vec.shape[2]
    heads = a_log.shape[0]
    scale = head_dim ** (-0.5)

    bits = slots.bit_length() - 1
    key_t, value_t = key_rows.swapaxes(1, 2), value_rows.swapaxes(1, 2)
    sources = (
        dt_raw,
        a_log,
        dt_bias,
        gate_rows,
        out_grad,
        read_vec,
        query_rows,
        key_t,
        value_t,
        write_vec,
    )
    pack, message = pl.pallas_call(
        share_kernel,
        out_shape=(
            shape((head_dim, rows), BF16),
            shape((bits, wide + 2 * rows + 2 * heads, head_dim), BF16),
        ),
        in_specs=[HBM] * len(sources),
        out_specs=(VMEM, VMEM),
        scratch_shapes=[
            pltpu.SMEM(a.shape, a.dtype) if a.ndim == 1 else pltpu.VMEM(a.shape, a.dtype)
            for a in sources
        ]
        + [pltpu.SemaphoreType.DMA((len(sources),))],
        compiler_params=PARAMS,
    )(*[pltpu.with_memory_space_constraint(a, pltpu.HBM) for a in sources])
    messages = [swap(message[slot.bit_length() - 1], slot, 0) for slot in range(1, slots)]
    partner = swap(pack, 0, 1)
    far = [swap(pack, slot, 1, True) for slot in range(1, slots)]

    wide_f, wide_b = shape((rows, wide), F32), shape((rows, wide), BF16)
    tall_f = shape((heads * rows, rows), F32)
    prepared = call(
        prepare_kernel,
        (wide_f,) * 6
        + (tall_f, tall_f)
        + (shape((rows, heads * rows), BF16), shape((heads * rows, 2 * wide // heads), BF16))
        + (shape((5 * heads, rows), F32), shape((8, wide), F32)),
        (gate_rows, out_grad, write_vec, read_vec, dt_raw, a_log, skip_gain, dt_bias),
        {5: SMEM, 6: SMEM, 7: SMEM},
    )
    grad_mixed, slope, step_w, decay_in, decay_out, own, fall, back = prepared[:8]
    ahead, halves, tables, skip_w = prepared[8:]
    mine, other, scores, keys, scaled, base, products = call(
        lambda *refs: state_kernel(slots, scale, *refs),
        (
            shape((slots, head_dim, rows), BF16),
            shape((slots * head_dim + 2 * rows, states), BF16),
            shape((wide // head_dim * rows, slots * rows), BF16),
            shape((head_dim, slots * rows), BF16),
            wide_b,
            wide_f,
            shape((5 * rows, wide), BF16),
        ),
        (
            query_rows,
            write_vec,
            read_vec,
            partner,
            grad_mixed,
            step_w,
            decay_in,
            decay_out,
            own,
            fall,
            halves,
            skip_w,
            *far,
            pack,
            *messages,
        ),
        {11 + slots + i: HBM for i in range(slots)},
        [pltpu.VMEM(m.shape, m.dtype) for m in (pack, *messages)]
        + [pltpu.SemaphoreType.DMA((slots,))],
    )
    got = swap(other, 0, 1)
    grad_dt, params = call(
        rates_kernel,
        (shape((1, heads, rows), F32), shape((8, states), F32)),
        (products, scaled, halves, back, tables),
    )
    reach = 1
    while reach < lax.axis_size("dp"):
        near = [params] + [lax.ppermute(params, "dp", flip("dp", k * reach)) for k in (1, 2, 3)]
        got, *near = lax.optimization_barrier((got, *near))
        params = (near[0] + near[1]) + (near[2] + near[3])
        reach *= 4
    sent = [
        (mine[slot].astype(F32) + got[slot * head_dim : (slot + 1) * head_dim].astype(F32)).astype(BF16)
        for slot in range(1, slots)
    ]
    arrived = [swap(sent[slot - 1], slot, 0, False) for slot in range(1, slots) if slot & (slot - 1)]
    slot = 1
    while slot < slots:
        tail = split(params)
        arrived.append(swap(jnp.concatenate([sent[slot - 1], tail], axis=0), slot, 0))
        slot *= 2
        if slot < slots:
            params = joined(tail) + joined(arrived[-1][head_dim:])
    shared, got_shared = other[slots * head_dim :], got[slots * head_dim :]
    reach = 2
    while reach < lax.axis_size("tp"):
        shared = (shared.astype(F32) + got_shared.astype(F32)).astype(BF16)
        got_shared = swap(shared, 0, reach)
        reach *= 2
    scores, shared = lax.optimization_barrier((scores, shared))
    grad_gate, grad_query = call(
        lambda *refs: output_kernel(scale, *refs),
        (shape((1, rows, wide), F32), shape((1, rows, wide), F32)),
        (ahead, scaled, base, slope, scores, keys),
    )
    vector = shape((heads,), F32)
    half = shape((1, head_dim // 2, rows), F32)
    full = shape((1, rows, states), F32)
    grad_key, grad_value, grad_write, grad_read, grad_alog, grad_skip, grad_bias = call(
        lambda *refs: finish_kernel(len(arrived), *refs),
        (half, half, full, full, vector, vector, vector),
        (*arrived, mine, got, tail, shared, got_shared),
    )
    grad_key, grad_value = grad_key.swapaxes(1, 2), grad_value.swapaxes(1, 2)
    return (
        grad_query,
        grad_key,
        grad_value,
        grad_gate,
        grad_write,
        grad_read,
        grad_dt,
        grad_alog,
        grad_skip,
        grad_bias,
    )


def solution(mesh):
    in_specs = (
        P("dp", "seq", "tp"),
        P("dp", "seq", "tp"),
        P("dp", "seq", "tp"),
        P("dp", "seq", "tp"),
        P("dp", "seq", None),
        P("dp", "seq", None),
        P("dp", "tp", "seq"),
        P("tp"),
        P("tp"),
        P("tp"),
        P("dp", "seq", "tp"),
    )
    out_specs = (
        P("dp", "seq", "tp"),
        P("dp", "seq", "tp"),
        P("dp", "seq", "tp"),
        P("dp", "seq", "tp"),
        P("dp", "seq", None),
        P("dp", "seq", None),
        P("dp", "tp", "seq"),
        P("tp"),
        P("tp"),
        P("tp"),
    )
    return jax.shard_map(body, mesh=mesh, in_specs=in_specs, out_specs=out_specs, check_vma=False)
```

```python
import jax
import jax.numpy as jnp
from jax import lax
from jax.experimental import pallas as pl
from jax.experimental.pallas import tpu as pltpu
from jax.sharding import PartitionSpec as P

NEG_FILL = -1e30
LOG2E = 1.4426950408889634
F32 = jnp.float32
BF16 = jnp.bfloat16
NN = (((1,), (0,)), ((), ()))
NT = (((1,), (1,)), ((), ()))
TN = (((0,), (0,)), ((), ()))


def dot(a, b, dims=NN):
    return lax.dot_general(a.astype(BF16), b.astype(BF16), dims, preferred_element_type=F32)


def parts_of(array, count):
    parts = []
    for _ in range(count):
        parts.append(array.astype(BF16))
        array = array - parts[-1].astype(F32)
    return parts


def dot_flags(arrays, flags, count=3):
    split_up = [parts_of(a, count) for a in arrays]
    left = [parts[i] for i in range(count) for parts in split_up]
    right = jnp.concatenate([jnp.where(f, 1.0, 0.0) for f in flags] * count, axis=0)
    return dot(jnp.concatenate(left, axis=1), right)


def iota(shape, axis):
    return lax.broadcasted_iota(jnp.int32, shape, axis)


def column(ref, width):
    heads = ref.shape[0]
    at = iota((heads, width), 0)
    out = jnp.full((heads, width), ref[0], F32)
    for m in range(1, heads):
        out = jnp.where(at == m, ref[m], out)
    return out


def rates(raw, bias, alog):
    rows = raw.shape[1]
    shifted = raw + bias
    step = jnp.maximum(shifted, 0.0) + jnp.log1p(jnp.exp(-jnp.abs(shifted)))
    rate = step * jnp.exp(alog)
    return step, rate, dot_flags([rate], [iota((rows, rows), 0) <= iota((rows, rows), 1)])


def spread(cols, m, width):
    return jnp.broadcast_to(cols[:, m : m + 1], (cols.shape[0], width))


def widen(factors, channels):
    heads = factors.shape[0]
    shape = (3 * heads, heads * channels)
    pick = (iota(shape, 1) // channels == iota(shape, 0) % heads).astype(BF16)
    return dot(jnp.concatenate(parts_of(factors, 3), axis=0), pick, TN)


def stack(wide, width):
    return jnp.concatenate([wide[:, i : i + width] for i in range(0, wide.shape[1], width)], axis=0)


def unstack(tall, rows):
    return jnp.concatenate([tall[i : i + rows] for i in range(0, tall.shape[0], rows)], axis=1)


def attend(jobs, scale):
    shapes = [(q.shape[0] // m.shape[0],) + m.shape for q, _, _, m in jobs]
    scores = [
        jnp.where(m[None], (dot(q, k) * (scale * LOG2E)).reshape(dims), NEG_FILL)
        for (q, k, _, m), dims in zip(jobs, shapes)
    ]
    tops = [jnp.max(s, axis=2, keepdims=True) for s in scores]
    weights = [
        jnp.exp2(s - top).reshape(dims[0] * dims[1], dims[2])
        for s, top, dims in zip(scores, tops, shapes)
    ]
    both = [
        dot(w, jnp.concatenate([v, jnp.ones_like(v)], axis=0), NT)
        for w, (_, _, v, _) in zip(weights, jobs)
    ]
    width = jobs[0][2].shape[0]
    shares = [1.0 / b[:, width:] for b in both]
    return [(b[:, :width] * share, w, share) for b, w, share in zip(both, weights, shares)]


def _fold(join, parts):
    out = parts[0]
    for part in parts[1:]:
        out = join(out, part)
    return out


def slot_mask(here, query_slot, slots, rows):
    masks = []
    for slot in slots:
        if slot == query_slot:
            masks.append(iota((rows, rows), 0) >= iota((rows, rows), 1))
        else:
            seen = jnp.bitwise_xor(here, slot) < jnp.bitwise_xor(here, query_slot)
            masks.append(jnp.broadcast_to(seen, (rows, rows)))
    return jnp.concatenate(masks, axis=1)


def share_kernel(*refs):
    sources, (pack, message), held, arrived = refs[:10], refs[10:12], refs[12:22], refs[22]
    copies = [
        pltpu.make_async_copy(source, here, arrived.at[i])
        for i, (source, here) in enumerate(zip(sources, held))
    ]
    for copy in copies:
        copy.start()
    raw, alog, bias, gate, cotangent, read, query, key, value, write = held
    for copy in copies[:3]:
        copy.wait()
    here = lax.axis_index("seq")
    heads, rows = raw.shape[1:]
    wide, states = gate.shape[2], read.shape[2]
    half = key.shape[1]
    step, _, cum = rates(raw[0], column(bias, rows), column(alog, rows))
    decay = widen(jnp.exp(-cum), wide // heads)
    to_end = jnp.exp(cum - cum[:, rows - 1 :]) * step
    whole = jnp.broadcast_to(jnp.exp(-cum[:, rows - 1 :]), (heads, rows))
    tail = jnp.concatenate([to_end, whole], axis=0).astype(BF16)
    for copy in copies[3:]:
        copy.wait()
    pack[:half] = key[0]
    pack[half:] = value[0]
    gate_f = gate[0].astype(F32)
    grad_mixed = cotangent[0].astype(F32) * gate_f * jax.nn.sigmoid(gate_f)
    entry = dot(read[0], grad_mixed * decay, TN).astype(BF16)
    for bit in range(message.shape[0]):
        is_early = jnp.bitwise_and(lax.shift_right_logical(here, bit), 1) == 0
        for at in range(0, wide, states):
            message[bit, at : at + rows] = jnp.where(
                is_early, query[0, :, at : at + states], entry[:, at : at + states]
            )
        message[bit, wide : wide + half] = key[0]
        message[bit, wide + half : wide + 2 * half] = value[0]
        message[bit, wide + rows : wide + 2 * rows] = write[0]
        message[bit, wide + 2 * rows :] = tail


def prepare_kernel(gate, cotangent, write, read, raw, alog, skip, bias, *outs):
    mixed_out, slope_out, step_out, in_out, out_out, own_out, fall_out, back_out = outs[:8]
    ahead_out, split_out, rates_out, skip_out = outs[8:]
    heads, rows = raw.shape[1:]
    wide = gate.shape[2]
    channels = wide // heads
    pair = 2 * channels
    alog_c, bias_c = column(alog, rows), column(bias, rows)
    step, rate, cum = rates(raw[0], bias_c, alog_c)
    for i, table in enumerate((step, rate, cum, jnp.exp(alog_c), jax.nn.sigmoid(raw[0] + bias_c))):
        rates_out[i * heads : (i + 1) * heads] = table
    head_of = iota(skip_out.shape, 1) // channels
    skip_w = jnp.full(skip_out.shape, skip[0], F32)
    for m in range(1, heads):
        skip_w = jnp.where(head_of == m, skip[m], skip_w)
    skip_out[...] = skip_w
    gate_f = gate[0].astype(F32)
    sig = jax.nn.sigmoid(gate_f)
    cot = cotangent[0].astype(F32)
    grad_mixed = cot * gate_f * sig
    mixed_out[...] = grad_mixed
    slope_out[...] = cot * sig * (1.0 + gate_f * (1.0 - sig))
    cum_cols = cum.T
    step_out[...] = widen(step, channels)
    in_out[...] = widen(jnp.exp(-cum), channels)
    out_out[...] = widen(jnp.exp(cum - cum[:, rows - 1 :]), channels)
    read_b, write_b = read[0], write[0]
    upper = iota((rows, rows), 0) <= iota((rows, rows), 1)
    lower = iota((rows, rows), 0) >= iota((rows, rows), 1)
    cross = jnp.where(lower, dot(read_b, write_b, NT), 0.0)
    cross_t = jnp.where(upper, dot(write_b, read_b, NT), 0.0)
    low = iota((rows, pair), 1) < channels
    for m in range(0, heads, 2):
        block = slice(m * channels, (m + 2) * channels)
        grad_p = grad_mixed[:, block]
        grad_d = jnp.concatenate(
            [jnp.where(low, grad_p, 0.0), jnp.where(low, 0.0, grad_p)], axis=0
        ).astype(BF16)
        split_out[m * rows : (m + 2) * rows] = grad_d
        backs = []
        for k in range(m, m + 2):
            gap = spread(cum_cols, k, rows) - cum[k : k + 1, :]
            fall = jnp.exp(-jnp.abs(gap))
            back = fall * cross_t
            at = slice(k * rows, (k + 1) * rows)
            fall_out[at] = fall
            back_out[at] = back
            ahead_out[:, at] = (fall * cross).astype(BF16)
            backs.append(back.astype(BF16))
        own_out[:, block] = dot(jnp.concatenate(backs, axis=1), grad_d)


def state_kernel(slots, scale, query, write, read, partner, *refs):
    mixed_in, step_in, in_in, out_in, own_in, fall_in, split_in, skip_in = refs[:8]
    refs = refs[8:]
    far, sources, refs = refs[: slots - 1], refs[slots - 1 : 2 * slots - 1], refs[2 * slots - 1 :]
    kept, sent, scores_out, keys_out, scaled_out, base_out, products_out = refs[:7]
    (pack, *messages), arrived = refs[7 : 7 + slots], refs[7 + slots]
    copies = [
        pltpu.make_async_copy(source, held, arrived.at[i])
        for i, (source, held) in enumerate(zip(sources, (pack, *messages)))
    ]
    for copy in copies:
        copy.start()
    here = lax.axis_index("seq")
    parity = lax.axis_index("tp") % 2
    rows, wide = query.shape[1:]
    heads = fall_in.shape[0] // rows
    channels = wide // heads
    states, head_dim = write.shape[2], pack.shape[0]
    half, pair, count = head_dim // 2, 2 * channels, wide // head_dim
    for copy in copies:
        copy.wait()

    key_parts, value_parts = [], []
    for slot in range(slots):
        near = messages[slot - 1][wide : wide + head_dim] if slot else pack[...]
        paired = far[slot - 1][...] if slot else partner[...]
        first = jnp.where(parity == 0, near, paired)
        second = jnp.where(parity == 0, paired, near)
        key_parts.append(jnp.concatenate([first[:half], second[:half]], axis=0))
        value_parts.append(jnp.concatenate([first[half:], second[half:]], axis=0))
    keys, values = jnp.concatenate(key_parts, axis=1), jnp.concatenate(value_parts, axis=1)
    keys_out[...] = keys

    grad_mixed, step_w, decay_in, decay_out = mixed_in[...], step_in[...], in_in[...], out_in[...]
    skip_w = skip_in[:1]
    read_b, write_b = read[0], write[0]
    tails = [m[wide + 2 * rows :].astype(F32) for m in messages]
    exit_t = jnp.zeros((states, wide), F32)
    early, to_ends = [], []
    for slot in range(1, slots):
        block = jnp.bitwise_xor(here, slot)
        early.append(block < here)
        between = jnp.ones((heads, rows), F32)
        for third in range(1, slots):
            if third != slot:
                at = jnp.bitwise_xor(here, third)
                inside = jnp.logical_and(
                    at > jnp.minimum(block, here), at < jnp.maximum(block, here)
                )
                between = between * jnp.where(inside, tails[third - 1][heads:], 1.0)
        later = unstack(messages[slot - 1][:wide], rows).astype(F32)
        if slots > 2:
            later = later * widen(between, channels)
        exit_t = exit_t + jnp.where(early[-1], 0.0, later)
        to_ends.append(widen(tails[slot - 1][:heads] * between, channels))
    exit_b = exit_t.astype(BF16)
    from_exit = decay_out * dot(write_b, exit_b)
    grad_scaled = own_in[...] + from_exit
    grad_inner = step_w * grad_scaled + skip_w * grad_mixed
    grads = stack(grad_inner, head_dim)
    grads_b = grads.astype(BF16)

    queries = stack(query[0], head_dim)
    jobs = [(queries, keys, values, slot_mask(here, 0, range(slots), rows))]
    for slot in range(1, slots):
        whole = slots > 2
        mask = slot_mask(here, slot, range(slots) if whole else [slot], rows)
        some = (keys, values) if whole else (key_parts[slot], value_parts[slot])
        jobs.append((messages[slot - 1][:wide], *some, mask))
    (attn, weights, share), *before = attend(jobs, scale)
    grad_probs = dot(grads_b, values)
    inner = unstack(attn, rows)
    scaled = inner * step_w
    scaled_b = scaled.astype(BF16)
    scaled_out[...] = scaled_b
    entry_t = jnp.zeros((states, wide), F32)
    for message, is_early, to_end, (attn_o, _, _) in zip(messages, early, to_ends, before):
        carried = unstack(attn_o, rows) * to_end
        end_state = dot(message[wide + rows : wide + 2 * rows], carried, TN)
        entry_t = entry_t + jnp.where(is_early, end_state, 0.0)
    entry_b = entry_t.astype(BF16)
    from_entry = decay_in * dot(read_b, entry_b)
    base_out[...] = from_entry + skip_w * inner

    product = grads * attn
    ones = jnp.ones((2 * head_dim, head_dim), BF16)
    delta = dot(jnp.concatenate(parts_of(product, 2), axis=1), ones)
    probs = weights * jnp.concatenate([share] * slots, axis=1)
    grad_scores = (probs * (grad_probs - jnp.concatenate([delta] * slots, axis=1))).astype(BF16)
    scores_out[...] = grad_scores
    key_t = (dot(queries, grad_scores, TN) * scale).astype(BF16)
    value_t = dot(grads_b, probs, TN).astype(BF16)
    for slot in range(slots):
        block = slice(slot * rows, (slot + 1) * rows)
        first = jnp.concatenate([key_t[:half, block], value_t[:half, block]], axis=0)
        second = jnp.concatenate([key_t[half:, block], value_t[half:, block]], axis=0)
        kept[slot] = jnp.where(parity == 0, first, second)
        sent[slot * head_dim : (slot + 1) * head_dim] = jnp.where(parity == 0, second, first)

    upper = iota((rows, rows), 0) <= iota((rows, rows), 1)
    grad_cross_t = jnp.zeros((rows, rows), F32)
    for m in range(0, heads, 2):
        outer = dot(
            scaled_b[:, m * channels : (m + 2) * channels], split_in[m * rows : (m + 2) * rows], NT
        )
        grad_cross_t = grad_cross_t + outer[:, :rows] * fall_in[m * rows : (m + 1) * rows]
        grad_cross_t = grad_cross_t + outer[:, rows:] * fall_in[(m + 1) * rows : (m + 2) * rows]
    grad_cross_t = jnp.where(upper, grad_cross_t, 0.0)
    grad_write = dot(grad_cross_t, read_b) + dot(scaled * decay_out, exit_b, NT)
    grad_read = dot(grad_cross_t, write_b, TN) + dot(grad_mixed * decay_in, entry_b, NT)
    sent[slots * head_dim : slots * head_dim + rows] = grad_write.astype(BF16)
    sent[slots * head_dim + rows :] = grad_read.astype(BF16)
    products = (
        inner * grad_scaled,
        inner * from_exit,
        grad_mixed * from_entry,
        grad_mixed * inner,
        exit_t * entry_t,
    )
    for i, product in enumerate(products):
        products_out[i * rows : (i + 1) * rows] = product.astype(BF16)


def rates_kernel(products, scaled, halves, back, tables, grad_raw, params):
    heads, rows = grad_raw.shape[1:]
    wide = products.shape[1]
    channels = wide // heads
    step, rate, cum, grow, slope = [tables[i * heads : (i + 1) * heads] for i in range(5)]
    strict = iota((rows, rows), 0) < iota((rows, rows), 1)
    lower = iota((rows, rows), 0) >= iota((rows, rows), 1)
    terms = []
    for m in range(0, heads, 2):
        outer = dot(
            scaled[:, m * channels : (m + 2) * channels], halves[m * rows : (m + 2) * rows], NT
        )
        terms.append((outer[:, :rows] * back[m * rows : (m + 1) * rows]).astype(BF16))
        terms.append((outer[:, rows:] * back[(m + 1) * rows : (m + 2) * rows]).astype(BF16))
    later = dot(jnp.concatenate(terms, axis=0), jnp.where(lower, 1.0, 0.0))
    rate_rows = [
        jnp.sum(jnp.where(strict, later[m * rows : (m + 1) * rows], 0.0), axis=0, keepdims=True)
        for m in range(heads)
    ]
    pick = (iota((heads, wide), 1) // channels == iota((heads, wide), 0)).astype(BF16)
    sums = dot(pick, products[...], NT)
    grad_step = sums[:, :rows]
    exit_sum = sums[:, rows : 2 * rows] * step
    entry_sum = sums[:, 2 * rows : 3 * rows]
    skip_sum = sums[:, 3 * rows : 4 * rows]
    carry_sum = jnp.sum(sums[:, 4 * rows :], axis=1, keepdims=True) * jnp.exp(-cum[:, rows - 1 :])
    grad_rate = -(
        jnp.concatenate(rate_rows, axis=0)
        + dot_flags([entry_sum, exit_sum], [lower, strict])
        + carry_sum
    )
    grad_shift = (grad_step + grad_rate * grow) * slope
    grad_raw[0] = grad_shift
    terms = jnp.concatenate([grad_rate * rate, skip_sum, grad_shift], axis=0)
    summed = jnp.concatenate(parts_of(terms, 3), axis=1)
    params[:, : 3 * heads] = dot(jnp.ones((8, 3 * rows), F32), summed, NT)
    params[:, 3 * heads :] = jnp.zeros((8, params.shape[1] - 3 * heads), F32)


def output_kernel(scale, ahead, scaled, base, slope, scores, keys, grad_gate, grad_query):
    rows, wide = base.shape
    channels = wide * rows // ahead.shape[1]
    pair = 2 * channels
    low = iota((rows, pair), 1) < channels
    for at in range(0, wide, pair):
        block = slice(at, at + pair)
        scaled_p = scaled[:, block].astype(F32)
        scaled_d = jnp.concatenate(
            [jnp.where(low, scaled_p, 0.0), jnp.where(low, 0.0, scaled_p)], axis=0
        )
        m = at // channels
        mixed = dot(ahead[:, m * rows : (m + 2) * rows], scaled_d) + base[:, block]
        grad_gate[0, :, block] = mixed * slope[:, block]
    grad_query[0] = unstack(dot(scores[...], keys[...], NT) * scale, rows)


def vectors_kernel(mine, other, grad_write, grad_read):
    rows = grad_write.shape[1]
    both = mine[...].astype(F32) + other[...].astype(F32)
    grad_write[0] = both[:rows]
    grad_read[0] = both[rows:]


def finish_kernel(count, *refs):
    arrived, (mine, other, tail) = refs[:count], refs[count : count + 3]
    grad_key, grad_value, grad_alog, grad_skip, grad_bias = refs[count + 3 :]
    half, rows = grad_key.shape[1:]
    total = mine[0].astype(F32) + other[: 2 * half].astype(F32)
    for term in arrived:
        total = total + term[: 2 * half].astype(F32)
    grad_key[0] = total[:half]
    grad_value[0] = total[half:]
    heads = grad_alog.shape[0]
    params = joined(tail[...]) + joined(arrived[-1][2 * half :])
    grad_alog[...] = params[0, :heads]
    grad_skip[...] = params[0, heads : 2 * heads]
    grad_bias[...] = params[0, 2 * heads : 3 * heads]


def split(sums):
    high = lax.reduce_precision(sums, 8, 7)
    return jnp.concatenate([high.astype(BF16), (sums - high).astype(BF16)], axis=0)


def joined(tail):
    tail = tail.astype(F32)
    count = tail.shape[0] // 2
    return tail[:count] + tail[count:]


def flip(axis, distance):
    return [(i, i ^ distance) for i in range(lax.axis_size(axis))]


def shape(dims, dtype):
    return jax.ShapeDtypeStruct(tuple(dims), dtype)


VMEM = pl.BlockSpec(memory_space=pltpu.VMEM)
SMEM = pl.BlockSpec(memory_space=pltpu.SMEM)
HBM = pl.BlockSpec(memory_space=pltpu.HBM)
PARAMS = pltpu.CompilerParams(vmem_limit_bytes=48 * 1024 * 1024)


def call(kernel, outs, args, specs=None, scratch=(), flops=0):
    return pl.pallas_call(
        kernel,
        out_shape=outs,
        in_specs=[(specs or {}).get(i, VMEM) for i in range(len(args))],
        out_specs=jax.tree.map(lambda _: VMEM, outs),
        scratch_shapes=scratch,
        compiler_params=PARAMS,
        cost_estimate=pl.CostEstimate(flops=flops, bytes_accessed=0, transcendentals=0),
    )(*args)


def swap(array, seq_bits, tp_bits, to_later=None):
    n_seq, n_tp = lax.axis_size("seq"), lax.axis_size("tp")
    pairs = [
        (s * n_tp + t, (s ^ seq_bits) * n_tp + (t ^ tp_bits))
        for s in range(n_seq)
        for t in range(n_tp)
        if to_later is None or ((s ^ seq_bits) > s) == to_later
    ]
    return lax.ppermute(array, ("seq", "tp"), pairs)


def body(
    query_rows,
    key_rows,
    value_rows,
    gate_rows,
    write_vec,
    read_vec,
    dt_raw,
    a_log,
    skip_gain,
    dt_bias,
    out_grad,
):
    slots = lax.axis_size("seq")
    rows, wide = query_rows.shape[1:]
    head_dim = 2 * key_rows.shape[2]
    states = write_vec.shape[2]
    heads = a_log.shape[0]
    scale = head_dim ** (-0.5)

    bits = slots.bit_length() - 1
    key_t, value_t = key_rows.swapaxes(1, 2), value_rows.swapaxes(1, 2)
    sources = (
        dt_raw,
        a_log,
        dt_bias,
        gate_rows,
        out_grad,
        read_vec,
        query_rows,
        key_t,
        value_t,
        write_vec,
    )
    pack, message = pl.pallas_call(
        share_kernel,
        out_shape=(
            shape((head_dim, rows), BF16),
            shape((bits, wide + 2 * rows + 2 * heads, head_dim), BF16),
        ),
        in_specs=[HBM] * len(sources),
        out_specs=(VMEM, VMEM),
        scratch_shapes=[
            pltpu.SMEM(a.shape, a.dtype) if a.ndim == 1 else pltpu.VMEM(a.shape, a.dtype)
            for a in sources
        ]
        + [pltpu.SemaphoreType.DMA((len(sources),))],
        compiler_params=PARAMS,
    )(*[pltpu.with_memory_space_constraint(a, pltpu.HBM) for a in sources])
    messages = [swap(message[slot.bit_length() - 1], slot, 0) for slot in range(1, slots)]
    partner = swap(pack, 0, 1)
    far = [swap(pack, slot, 1, True) for slot in range(1, slots)]

    wide_f, wide_b = shape((rows, wide), F32), shape((rows, wide), BF16)
    tall_f = shape((heads * rows, rows), F32)
    prepared = call(
        prepare_kernel,
        (wide_f,) * 6
        + (tall_f, tall_f)
        + (shape((rows, heads * rows), BF16), shape((heads * rows, 2 * wide // heads), BF16))
        + (shape((5 * heads, rows), F32), shape((8, wide), F32)),
        (gate_rows, out_grad, write_vec, read_vec, dt_raw, a_log, skip_gain, dt_bias),
        {5: SMEM, 6: SMEM, 7: SMEM},
    )
    grad_mixed, slope, step_w, decay_in, decay_out, own, fall, back = prepared[:8]
    ahead, halves, tables, skip_w = prepared[8:]
    mine, other, scores, keys, scaled, base, products = call(
        lambda *refs: state_kernel(slots, scale, *refs),
        (
            shape((slots, head_dim, rows), BF16),
            shape((slots * head_dim + 2 * rows, states), BF16),
            shape((wide // head_dim * rows, slots * rows), BF16),
            shape((head_dim, slots * rows), BF16),
            wide_b,
            wide_f,
            shape((5 * rows, wide), BF16),
        ),
        (
            query_rows,
            write_vec,
            read_vec,
            partner,
            grad_mixed,
            step_w,
            decay_in,
            decay_out,
            own,
            fall,
            halves,
            skip_w,
            *far,
            pack,
            *messages,
        ),
        {11 + slots + i: HBM for i in range(slots)},
        [pltpu.VMEM(m.shape, m.dtype) for m in (pack, *messages)]
        + [pltpu.SemaphoreType.DMA((slots,))],
    )
    got = swap(other, 0, 1)
    grad_dt, params = call(
        rates_kernel,
        (shape((1, heads, rows), F32), shape((8, states), F32)),
        (products, scaled, halves, back, tables),
    )
    shared, got_shared = other[slots * head_dim :], got[slots * head_dim :]
    reach = 2
    while reach < lax.axis_size("tp"):
        shared = (shared.astype(F32) + got_shared.astype(F32)).astype(BF16)
        got_shared = swap(shared, 0, reach)
        reach *= 2
    reach = 1
    while reach < lax.axis_size("dp"):
        near = [params] + [lax.ppermute(params, "dp", flip("dp", k * reach)) for k in (1, 2, 3)]
        shared, *near = lax.optimization_barrier((shared, *near))
        params = (near[0] + near[1]) + (near[2] + near[3])
        reach *= 4
    sent = [
        (mine[slot].astype(F32) + got[slot * head_dim : (slot + 1) * head_dim].astype(F32)).astype(BF16)
        for slot in range(1, slots)
    ]
    arrived = [swap(sent[slot - 1], slot, 0, False) for slot in range(1, slots) if slot & (slot - 1)]
    slot = 1
    while slot < slots:
        tail = split(params)
        arrived.append(swap(jnp.concatenate([sent[slot - 1], tail], axis=0), slot, 0))
        slot *= 2
        if slot < slots:
            params = joined(tail) + joined(arrived[-1][head_dim:])
    scores, shared = lax.optimization_barrier((scores, shared))
    grad_gate, grad_query = call(
        lambda *refs: output_kernel(scale, *refs),
        (shape((1, rows, wide), F32), shape((1, rows, wide), F32)),
        (ahead, scaled, base, slope, scores, keys),
    )
    vector = shape((heads,), F32)
    half = shape((1, head_dim // 2, rows), F32)
    full = shape((1, rows, states), F32)
    grad_write, grad_read = call(vectors_kernel, (full, full), (shared, got_shared))
    grad_write, *arrived = lax.optimization_barrier((grad_write, *arrived))
    grad_key, grad_value, grad_alog, grad_skip, grad_bias = call(
        lambda *refs: finish_kernel(len(arrived), *refs),
        (half, half, vector, vector, vector),
        (*arrived, mine, got, tail),
    )
    grad_key, grad_value = grad_key.swapaxes(1, 2), grad_value.swapaxes(1, 2)
    return (
        grad_query,
        grad_key,
        grad_value,
        grad_gate,
        grad_write,
        grad_read,
        grad_dt,
        grad_alog,
        grad_skip,
        grad_bias,
    )


def solution(mesh):
    in_specs = (
        P("dp", "seq", "tp"),
        P("dp", "seq", "tp"),
        P("dp", "seq", "tp"),
        P("dp", "seq", "tp"),
        P("dp", "seq", None),
        P("dp", "seq", None),
        P("dp", "tp", "seq"),
        P("tp"),
        P("tp"),
        P("tp"),
        P("dp", "seq", "tp"),
    )
    out_specs = (
        P("dp", "seq", "tp"),
        P("dp", "seq", "tp"),
        P("dp", "seq", "tp"),
        P("dp", "seq", "tp"),
        P("dp", "seq", None),
        P("dp", "seq", None),
        P("dp", "tp", "seq"),
        P("tp"),
        P("tp"),
        P("tp"),
    )
    return jax.shard_map(body, mesh=mesh, in_specs=in_specs, out_specs=out_specs, check_vma=False)
```

```python
import jax
import jax.numpy as jnp
from jax import lax
from jax.experimental import pallas as pl
from jax.experimental.pallas import tpu as pltpu
from jax.sharding import PartitionSpec as P

NEG_FILL = -1e30
LOG2E = 1.4426950408889634
F32 = jnp.float32
BF16 = jnp.bfloat16
NN = (((1,), (0,)), ((), ()))
NT = (((1,), (1,)), ((), ()))
TN = (((0,), (0,)), ((), ()))


def dot(a, b, dims=NN):
    return lax.dot_general(a.astype(BF16), b.astype(BF16), dims, preferred_element_type=F32)


def parts_of(array, count):
    parts = []
    for _ in range(count):
        parts.append(array.astype(BF16))
        array = array - parts[-1].astype(F32)
    return parts


def dot_flags(arrays, flags, count=3):
    split_up = [parts_of(a, count) for a in arrays]
    left = [parts[i] for i in range(count) for parts in split_up]
    right = jnp.concatenate([jnp.where(f, 1.0, 0.0) for f in flags] * count, axis=0)
    return dot(jnp.concatenate(left, axis=1), right)


def iota(shape, axis):
    return lax.broadcasted_iota(jnp.int32, shape, axis)


def column(ref, width):
    heads = ref.shape[0]
    at = iota((heads, width), 0)
    out = jnp.full((heads, width), ref[0], F32)
    for m in range(1, heads):
        out = jnp.where(at == m, ref[m], out)
    return out


def rates(raw, bias, alog):
    rows = raw.shape[1]
    shifted = raw + bias
    step = jnp.maximum(shifted, 0.0) + jnp.log1p(jnp.exp(-jnp.abs(shifted)))
    rate = step * jnp.exp(alog)
    return step, rate, dot_flags([rate], [iota((rows, rows), 0) <= iota((rows, rows), 1)])


def spread(cols, m, width):
    return jnp.broadcast_to(cols[:, m : m + 1], (cols.shape[0], width))


def widen(factors, channels):
    heads = factors.shape[0]
    shape = (3 * heads, heads * channels)
    pick = (iota(shape, 1) // channels == iota(shape, 0) % heads).astype(BF16)
    return dot(jnp.concatenate(parts_of(factors, 3), axis=0), pick, TN)


def stack(wide, width):
    return jnp.concatenate([wide[:, i : i + width] for i in range(0, wide.shape[1], width)], axis=0)


def unstack(tall, rows):
    return jnp.concatenate([tall[i : i + rows] for i in range(0, tall.shape[0], rows)], axis=1)


def attend(jobs, scale):
    shapes = [(q.shape[0] // m.shape[0],) + m.shape for q, _, _, m in jobs]
    scores = [
        jnp.where(m[None], (dot(q, k) * (scale * LOG2E)).reshape(dims), NEG_FILL)
        for (q, k, _, m), dims in zip(jobs, shapes)
    ]
    tops = [jnp.max(s, axis=2, keepdims=True) for s in scores]
    weights = [
        jnp.exp2(s - top).reshape(dims[0] * dims[1], dims[2])
        for s, top, dims in zip(scores, tops, shapes)
    ]
    both = [
        dot(w, jnp.concatenate([v, jnp.ones_like(v)], axis=0), NT)
        for w, (_, _, v, _) in zip(weights, jobs)
    ]
    width = jobs[0][2].shape[0]
    shares = [1.0 / b[:, width:] for b in both]
    return [(b[:, :width] * share, w, share) for b, w, share in zip(both, weights, shares)]


def slot_mask(here, query_slot, slots, rows):
    masks = []
    for slot in slots:
        if slot == query_slot:
            masks.append(iota((rows, rows), 0) >= iota((rows, rows), 1))
        else:
            seen = jnp.bitwise_xor(here, slot) < jnp.bitwise_xor(here, query_slot)
            masks.append(jnp.broadcast_to(seen, (rows, rows)))
    return jnp.concatenate(masks, axis=1)


def share_kernel(*refs):
    sources, (pack, message), held, arrived = refs[:10], refs[10:12], refs[12:22], refs[22]
    copies = [
        pltpu.make_async_copy(source, here, arrived.at[i])
        for i, (source, here) in enumerate(zip(sources, held))
    ]
    for copy in copies:
        copy.start()
    raw, alog, bias, gate, cotangent, read, query, key, value, write = held
    for copy in copies[:3]:
        copy.wait()
    here = lax.axis_index("seq")
    heads, rows = raw.shape[1:]
    wide, states = gate.shape[2], read.shape[2]
    half = key.shape[1]
    step, _, cum = rates(raw[0], column(bias, rows), column(alog, rows))
    decay = widen(jnp.exp(-cum), wide // heads)
    to_end = jnp.exp(cum - cum[:, rows - 1 :]) * step
    whole = jnp.broadcast_to(jnp.exp(-cum[:, rows - 1 :]), (heads, rows))
    tail = jnp.concatenate([to_end, whole], axis=0).astype(BF16)
    for copy in copies[3:]:
        copy.wait()
    pack[:half] = key[0]
    pack[half:] = value[0]
    gate_f = gate[0].astype(F32)
    grad_mixed = cotangent[0].astype(F32) * gate_f * jax.nn.sigmoid(gate_f)
    entry = dot(read[0], grad_mixed * decay, TN).astype(BF16)
    for bit in range(message.shape[0]):
        is_early = jnp.bitwise_and(lax.shift_right_logical(here, bit), 1) == 0
        for at in range(0, wide, states):
            message[bit, at : at + rows] = jnp.where(
                is_early, query[0, :, at : at + states], entry[:, at : at + states]
            )
        message[bit, wide : wide + half] = key[0]
        message[bit, wide + half : wide + 2 * half] = value[0]
        message[bit, wide + rows : wide + 2 * rows] = write[0]
        message[bit, wide + 2 * rows :] = tail


def prepare_kernel(gate, cotangent, write, read, raw, alog, skip, bias, *outs):
    mixed_out, slope_out, step_out, in_out, out_out, own_out, fall_out, back_out = outs[:8]
    ahead_out, split_out, rates_out, skip_out = outs[8:]
    heads, rows = raw.shape[1:]
    wide = gate.shape[2]
    channels = wide // heads
    pair = 2 * channels
    alog_c, bias_c = column(alog, rows), column(bias, rows)
    step, rate, cum = rates(raw[0], bias_c, alog_c)
    for i, table in enumerate((step, rate, cum, jnp.exp(alog_c), jax.nn.sigmoid(raw[0] + bias_c))):
        rates_out[i * heads : (i + 1) * heads] = table
    head_of = iota(skip_out.shape, 1) // channels
    skip_w = jnp.full(skip_out.shape, skip[0], F32)
    for m in range(1, heads):
        skip_w = jnp.where(head_of == m, skip[m], skip_w)
    skip_out[...] = skip_w
    gate_f = gate[0].astype(F32)
    sig = jax.nn.sigmoid(gate_f)
    cot = cotangent[0].astype(F32)
    grad_mixed = cot * gate_f * sig
    mixed_out[...] = grad_mixed
    slope_out[...] = cot * sig * (1.0 + gate_f * (1.0 - sig))
    cum_cols = cum.T
    step_out[...] = widen(step, channels)
    in_out[...] = widen(jnp.exp(-cum), channels)
    out_out[...] = widen(jnp.exp(cum - cum[:, rows - 1 :]), channels)
    read_b, write_b = read[0], write[0]
    upper = iota((rows, rows), 0) <= iota((rows, rows), 1)
    lower = iota((rows, rows), 0) >= iota((rows, rows), 1)
    cross = jnp.where(lower, dot(read_b, write_b, NT), 0.0)
    cross_t = jnp.where(upper, dot(write_b, read_b, NT), 0.0)
    low = iota((rows, pair), 1) < channels
    for m in range(0, heads, 2):
        block = slice(m * channels, (m + 2) * channels)
        grad_p = grad_mixed[:, block]
        grad_d = jnp.concatenate(
            [jnp.where(low, grad_p, 0.0), jnp.where(low, 0.0, grad_p)], axis=0
        ).astype(BF16)
        split_out[m * rows : (m + 2) * rows] = grad_d
        backs = []
        for k in range(m, m + 2):
            gap = spread(cum_cols, k, rows) - cum[k : k + 1, :]
            fall = jnp.exp(-jnp.abs(gap))
            back = fall * cross_t
            at = slice(k * rows, (k + 1) * rows)
            fall_out[at] = fall
            back_out[at] = back
            ahead_out[:, at] = (fall * cross).astype(BF16)
            backs.append(back.astype(BF16))
        own_out[:, block] = dot(jnp.concatenate(backs, axis=1), grad_d)


def state_kernel(slots, scale, query, write, read, partner, *refs):
    mixed_in, step_in, in_in, out_in, own_in, fall_in, split_in, skip_in = refs[:8]
    refs = refs[8:]
    far, sources, refs = refs[: slots - 1], refs[slots - 1 : 2 * slots - 1], refs[2 * slots - 1 :]
    kept, sent, scores_out, keys_out, scaled_out, base_out, products_out = refs[:7]
    (pack, *messages), arrived = refs[7 : 7 + slots], refs[7 + slots]
    copies = [
        pltpu.make_async_copy(source, held, arrived.at[i])
        for i, (source, held) in enumerate(zip(sources, (pack, *messages)))
    ]
    for copy in copies:
        copy.start()
    here = lax.axis_index("seq")
    parity = lax.axis_index("tp") % 2
    rows, wide = query.shape[1:]
    heads = fall_in.shape[0] // rows
    channels = wide // heads
    states, head_dim = write.shape[2], pack.shape[0]
    half, pair, count = head_dim // 2, 2 * channels, wide // head_dim
    for copy in copies:
        copy.wait()

    key_parts, value_parts = [], []
    for slot in range(slots):
        near = messages[slot - 1][wide : wide + head_dim] if slot else pack[...]
        paired = far[slot - 1][...] if slot else partner[...]
        first = jnp.where(parity == 0, near, paired)
        second = jnp.where(parity == 0, paired, near)
        key_parts.append(jnp.concatenate([first[:half], second[:half]], axis=0))
        value_parts.append(jnp.concatenate([first[half:], second[half:]], axis=0))
    keys, values = jnp.concatenate(key_parts, axis=1), jnp.concatenate(value_parts, axis=1)
    keys_out[...] = keys

    grad_mixed, step_w, decay_in, decay_out = mixed_in[...], step_in[...], in_in[...], out_in[...]
    skip_w = skip_in[:1]
    read_b, write_b = read[0], write[0]
    tails = [m[wide + 2 * rows :].astype(F32) for m in messages]
    exit_t = jnp.zeros((states, wide), F32)
    early, to_ends = [], []
    for slot in range(1, slots):
        block = jnp.bitwise_xor(here, slot)
        early.append(block < here)
        between = jnp.ones((heads, rows), F32)
        for third in range(1, slots):
            if third != slot:
                at = jnp.bitwise_xor(here, third)
                inside = jnp.logical_and(
                    at > jnp.minimum(block, here), at < jnp.maximum(block, here)
                )
                between = between * jnp.where(inside, tails[third - 1][heads:], 1.0)
        later = unstack(messages[slot - 1][:wide], rows).astype(F32)
        if slots > 2:
            later = later * widen(between, channels)
        exit_t = exit_t + jnp.where(early[-1], 0.0, later)
        to_ends.append(widen(tails[slot - 1][:heads] * between, channels))
    exit_b = exit_t.astype(BF16)
    from_exit = decay_out * dot(write_b, exit_b)
    grad_scaled = own_in[...] + from_exit
    grad_inner = step_w * grad_scaled + skip_w * grad_mixed
    grads = stack(grad_inner, head_dim)
    grads_b = grads.astype(BF16)

    queries = stack(query[0], head_dim)
    jobs = [(queries, keys, values, slot_mask(here, 0, range(slots), rows))]
    for slot in range(1, slots):
        whole = slots > 2
        mask = slot_mask(here, slot, range(slots) if whole else [slot], rows)
        some = (keys, values) if whole else (key_parts[slot], value_parts[slot])
        jobs.append((messages[slot - 1][:wide], *some, mask))
    (attn, weights, share), *before = attend(jobs, scale)
    grad_probs = dot(grads_b, values)
    inner = unstack(attn, rows)
    scaled = inner * step_w
    scaled_b = scaled.astype(BF16)
    scaled_out[...] = scaled_b
    entry_t = jnp.zeros((states, wide), F32)
    for message, is_early, to_end, (attn_o, _, _) in zip(messages, early, to_ends, before):
        carried = unstack(attn_o, rows) * to_end
        end_state = dot(message[wide + rows : wide + 2 * rows], carried, TN)
        entry_t = entry_t + jnp.where(is_early, end_state, 0.0)
    entry_b = entry_t.astype(BF16)
    from_entry = decay_in * dot(read_b, entry_b)
    base_out[...] = from_entry + skip_w * inner

    product = grads * attn
    ones = jnp.ones((2 * head_dim, head_dim), BF16)
    delta = dot(jnp.concatenate(parts_of(product, 2), axis=1), ones)
    probs = weights * jnp.concatenate([share] * slots, axis=1)
    grad_scores = (probs * (grad_probs - jnp.concatenate([delta] * slots, axis=1))).astype(BF16)
    scores_out[...] = grad_scores
    key_t = (dot(queries, grad_scores, TN) * scale).astype(BF16)
    value_t = dot(grads_b, probs, TN).astype(BF16)
    for slot in range(slots):
        block = slice(slot * rows, (slot + 1) * rows)
        first = jnp.concatenate([key_t[:half, block], value_t[:half, block]], axis=0)
        second = jnp.concatenate([key_t[half:, block], value_t[half:, block]], axis=0)
        kept[slot] = jnp.where(parity == 0, first, second)
        sent[slot * head_dim : (slot + 1) * head_dim] = jnp.where(parity == 0, second, first)

    upper = iota((rows, rows), 0) <= iota((rows, rows), 1)
    grad_cross_t = jnp.zeros((rows, rows), F32)
    for m in range(0, heads, 2):
        outer = dot(
            scaled_b[:, m * channels : (m + 2) * channels], split_in[m * rows : (m + 2) * rows], NT
        )
        grad_cross_t = grad_cross_t + outer[:, :rows] * fall_in[m * rows : (m + 1) * rows]
        grad_cross_t = grad_cross_t + outer[:, rows:] * fall_in[(m + 1) * rows : (m + 2) * rows]
    grad_cross_t = jnp.where(upper, grad_cross_t, 0.0)
    grad_write = dot(grad_cross_t, read_b) + dot(scaled * decay_out, exit_b, NT)
    grad_read = dot(grad_cross_t, write_b, TN) + dot(grad_mixed * decay_in, entry_b, NT)
    sent[slots * head_dim : slots * head_dim + rows] = grad_write.astype(BF16)
    sent[slots * head_dim + rows :] = grad_read.astype(BF16)
    products = (
        inner * grad_scaled,
        inner * from_exit,
        grad_mixed * from_entry,
        grad_mixed * inner,
        exit_t * entry_t,
    )
    for i, product in enumerate(products):
        products_out[i * rows : (i + 1) * rows] = product.astype(BF16)


def rates_kernel(products, scaled, halves, back, tables, grad_raw, params):
    heads, rows = grad_raw.shape[1:]
    wide = products.shape[1]
    channels = wide // heads
    step, rate, cum, grow, slope = [tables[i * heads : (i + 1) * heads] for i in range(5)]
    strict = iota((rows, rows), 0) < iota((rows, rows), 1)
    lower = iota((rows, rows), 0) >= iota((rows, rows), 1)
    terms = []
    for m in range(0, heads, 2):
        outer = dot(
            scaled[:, m * channels : (m + 2) * channels], halves[m * rows : (m + 2) * rows], NT
        )
        terms.append((outer[:, :rows] * back[m * rows : (m + 1) * rows]).astype(BF16))
        terms.append((outer[:, rows:] * back[(m + 1) * rows : (m + 2) * rows]).astype(BF16))
    later = dot(jnp.concatenate(terms, axis=0), jnp.where(lower, 1.0, 0.0))
    rate_rows = [
        jnp.sum(jnp.where(strict, later[m * rows : (m + 1) * rows], 0.0), axis=0, keepdims=True)
        for m in range(heads)
    ]
    pick = (iota((heads, wide), 1) // channels == iota((heads, wide), 0)).astype(BF16)
    sums = dot(pick, products[...], NT)
    grad_step = sums[:, :rows]
    exit_sum = sums[:, rows : 2 * rows] * step
    entry_sum = sums[:, 2 * rows : 3 * rows]
    skip_sum = sums[:, 3 * rows : 4 * rows]
    carry_sum = jnp.sum(sums[:, 4 * rows :], axis=1, keepdims=True) * jnp.exp(-cum[:, rows - 1 :])
    grad_rate = -(
        jnp.concatenate(rate_rows, axis=0)
        + dot_flags([entry_sum, exit_sum], [lower, strict])
        + carry_sum
    )
    grad_shift = (grad_step + grad_rate * grow) * slope
    grad_raw[0] = grad_shift
    terms = jnp.concatenate([grad_rate * rate, skip_sum, grad_shift], axis=0)
    summed = jnp.concatenate(parts_of(terms, 3), axis=1)
    params[:, : 3 * heads] = dot(jnp.ones((8, 3 * rows), F32), summed, NT)
    params[:, 3 * heads :] = jnp.zeros((8, params.shape[1] - 3 * heads), F32)


def output_kernel(scale, ahead, scaled, base, slope, scores, keys, grad_gate, grad_query):
    rows, wide = base.shape
    channels = wide * rows // ahead.shape[1]
    pair = 2 * channels
    low = iota((rows, pair), 1) < channels
    for at in range(0, wide, pair):
        block = slice(at, at + pair)
        scaled_p = scaled[:, block].astype(F32)
        scaled_d = jnp.concatenate(
            [jnp.where(low, scaled_p, 0.0), jnp.where(low, 0.0, scaled_p)], axis=0
        )
        m = at // channels
        mixed = dot(ahead[:, m * rows : (m + 2) * rows], scaled_d) + base[:, block]
        grad_gate[0, :, block] = mixed * slope[:, block]
    grad_query[0] = unstack(dot(scores[...], keys[...], NT) * scale, rows)


def vectors_kernel(mine, other, grad_write, grad_read):
    rows = grad_write.shape[1]
    both = mine[...].astype(F32) + other[...].astype(F32)
    grad_write[0] = both[:rows]
    grad_read[0] = both[rows:]


def finish_kernel(count, *refs):
    arrived, (mine, other, tail) = refs[:count], refs[count : count + 3]
    grad_key, grad_value, grad_alog, grad_skip, grad_bias = refs[count + 3 :]
    half, rows = grad_key.shape[1:]
    total = mine[0].astype(F32) + other[: 2 * half].astype(F32)
    for term in arrived:
        total = total + term[: 2 * half].astype(F32)
    grad_key[0] = total[:half]
    grad_value[0] = total[half:]
    heads = grad_alog.shape[0]
    params = joined(tail[...]) + joined(arrived[-1][2 * half :])
    grad_alog[...] = params[0, :heads]
    grad_skip[...] = params[0, heads : 2 * heads]
    grad_bias[...] = params[0, 2 * heads : 3 * heads]


def split(sums):
    high = lax.reduce_precision(sums, 8, 7)
    return jnp.concatenate([high.astype(BF16), (sums - high).astype(BF16)], axis=0)


def joined(tail):
    tail = tail.astype(F32)
    count = tail.shape[0] // 2
    return tail[:count] + tail[count:]


def flip(axis, distance):
    return [(i, i ^ distance) for i in range(lax.axis_size(axis))]


def shape(dims, dtype):
    return jax.ShapeDtypeStruct(tuple(dims), dtype)


VMEM = pl.BlockSpec(memory_space=pltpu.VMEM)
SMEM = pl.BlockSpec(memory_space=pltpu.SMEM)
HBM = pl.BlockSpec(memory_space=pltpu.HBM)
PARAMS = pltpu.CompilerParams(vmem_limit_bytes=48 * 1024 * 1024)


def call(kernel, outs, args, specs=None, scratch=(), flops=0):
    return pl.pallas_call(
        kernel,
        out_shape=outs,
        in_specs=[(specs or {}).get(i, VMEM) for i in range(len(args))],
        out_specs=jax.tree.map(lambda _: VMEM, outs),
        scratch_shapes=scratch,
        compiler_params=PARAMS,
        cost_estimate=pl.CostEstimate(flops=flops, bytes_accessed=0, transcendentals=0),
    )(*args)


def swap(array, seq_bits, tp_bits):
    n_seq, n_tp = lax.axis_size("seq"), lax.axis_size("tp")
    pairs = [
        (s * n_tp + t, (s ^ seq_bits) * n_tp + (t ^ tp_bits))
        for s in range(n_seq)
        for t in range(n_tp)
    ]
    return lax.ppermute(array, ("seq", "tp"), pairs)


def body(
    query_rows,
    key_rows,
    value_rows,
    gate_rows,
    write_vec,
    read_vec,
    dt_raw,
    a_log,
    skip_gain,
    dt_bias,
    out_grad,
):
    slots = lax.axis_size("seq")
    rows, wide = query_rows.shape[1:]
    head_dim = 2 * key_rows.shape[2]
    states = write_vec.shape[2]
    heads = a_log.shape[0]
    scale = head_dim ** (-0.5)

    bits = slots.bit_length() - 1
    key_t, value_t = key_rows.swapaxes(1, 2), value_rows.swapaxes(1, 2)
    sources = (
        dt_raw,
        a_log,
        dt_bias,
        gate_rows,
        out_grad,
        read_vec,
        query_rows,
        key_t,
        value_t,
        write_vec,
    )
    pack, message = pl.pallas_call(
        share_kernel,
        out_shape=(
            shape((head_dim, rows), BF16),
            shape((bits, wide + 2 * rows + 2 * heads, head_dim), BF16),
        ),
        in_specs=[HBM] * len(sources),
        out_specs=(VMEM, VMEM),
        scratch_shapes=[
            pltpu.SMEM(a.shape, a.dtype) if a.ndim == 1 else pltpu.VMEM(a.shape, a.dtype)
            for a in sources
        ]
        + [pltpu.SemaphoreType.DMA((len(sources),))],
        compiler_params=PARAMS,
    )(*[pltpu.with_memory_space_constraint(a, pltpu.HBM) for a in sources])
    messages = [swap(message[slot.bit_length() - 1], slot, 0) for slot in range(1, slots)]
    partner = swap(pack, 0, 1)
    far = [swap(pack, slot, 1) for slot in range(1, slots)]

    wide_f, wide_b = shape((rows, wide), F32), shape((rows, wide), BF16)
    tall_f = shape((heads * rows, rows), F32)
    prepared = call(
        prepare_kernel,
        (wide_f,) * 6
        + (tall_f, tall_f)
        + (shape((rows, heads * rows), BF16), shape((heads * rows, 2 * wide // heads), BF16))
        + (shape((5 * heads, rows), F32), shape((8, wide), F32)),
        (gate_rows, out_grad, write_vec, read_vec, dt_raw, a_log, skip_gain, dt_bias),
        {5: SMEM, 6: SMEM, 7: SMEM},
    )
    grad_mixed, slope, step_w, decay_in, decay_out, own, fall, back = prepared[:8]
    ahead, halves, tables, skip_w = prepared[8:]
    mine, other, scores, keys, scaled, base, products = call(
        lambda *refs: state_kernel(slots, scale, *refs),
        (
            shape((slots, head_dim, rows), BF16),
            shape((slots * head_dim + 2 * rows, states), BF16),
            shape((wide // head_dim * rows, slots * rows), BF16),
            shape((head_dim, slots * rows), BF16),
            wide_b,
            wide_f,
            shape((5 * rows, wide), BF16),
        ),
        (
            query_rows,
            write_vec,
            read_vec,
            partner,
            grad_mixed,
            step_w,
            decay_in,
            decay_out,
            own,
            fall,
            halves,
            skip_w,
            *far,
            pack,
            *messages,
        ),
        {11 + slots + i: HBM for i in range(slots)},
        [pltpu.VMEM(m.shape, m.dtype) for m in (pack, *messages)]
        + [pltpu.SemaphoreType.DMA((slots,))],
    )
    got = swap(other, 0, 1)
    grad_dt, params = call(
        rates_kernel,
        (shape((1, heads, rows), F32), shape((8, states), F32)),
        (products, scaled, halves, back, tables),
    )
    shared, got_shared = other[slots * head_dim :], got[slots * head_dim :]
    reach = 2
    while reach < lax.axis_size("tp"):
        shared = (shared.astype(F32) + got_shared.astype(F32)).astype(BF16)
        got_shared = swap(shared, 0, reach)
        reach *= 2
    reach = 1
    while reach < lax.axis_size("dp"):
        near = [params] + [lax.ppermute(params, "dp", flip("dp", k * reach)) for k in (1, 2, 3)]
        shared, *near = lax.optimization_barrier((shared, *near))
        params = (near[0] + near[1]) + (near[2] + near[3])
        reach *= 4
    sent = [
        (mine[slot].astype(F32) + got[slot * head_dim : (slot + 1) * head_dim].astype(F32)).astype(BF16)
        for slot in range(1, slots)
    ]
    arrived = [swap(sent[slot - 1], slot, 0) for slot in range(1, slots) if slot & (slot - 1)]
    slot = 1
    while slot < slots:
        tail = split(params)
        arrived.append(swap(jnp.concatenate([sent[slot - 1], tail], axis=0), slot, 0))
        slot *= 2
        if slot < slots:
            params = joined(tail) + joined(arrived[-1][head_dim:])
    scores, shared = lax.optimization_barrier((scores, shared))
    grad_gate, grad_query = call(
        lambda *refs: output_kernel(scale, *refs),
        (shape((1, rows, wide), F32), shape((1, rows, wide), F32)),
        (ahead, scaled, base, slope, scores, keys),
    )
    vector = shape((heads,), F32)
    half = shape((1, head_dim // 2, rows), F32)
    full = shape((1, rows, states), F32)
    grad_write, grad_read = call(vectors_kernel, (full, full), (shared, got_shared))
    grad_write, *arrived = lax.optimization_barrier((grad_write, *arrived))
    grad_key, grad_value, grad_alog, grad_skip, grad_bias = call(
        lambda *refs: finish_kernel(len(arrived), *refs),
        (half, half, vector, vector, vector),
        (*arrived, mine, got, tail),
    )
    grad_key, grad_value = grad_key.swapaxes(1, 2), grad_value.swapaxes(1, 2)
    return (
        grad_query,
        grad_key,
        grad_value,
        grad_gate,
        grad_write,
        grad_read,
        grad_dt,
        grad_alog,
        grad_skip,
        grad_bias,
    )


def solution(mesh):
    in_specs = (
        P("dp", "seq", "tp"),
        P("dp", "seq", "tp"),
        P("dp", "seq", "tp"),
        P("dp", "seq", "tp"),
        P("dp", "seq", None),
        P("dp", "seq", None),
        P("dp", "tp", "seq"),
        P("tp"),
        P("tp"),
        P("tp"),
        P("dp", "seq", "tp"),
    )
    out_specs = (
        P("dp", "seq", "tp"),
        P("dp", "seq", "tp"),
        P("dp", "seq", "tp"),
        P("dp", "seq", "tp"),
        P("dp", "seq", None),
        P("dp", "seq", None),
        P("dp", "tp", "seq"),
        P("tp"),
        P("tp"),
        P("tp"),
    )
    return jax.shard_map(body, mesh=mesh, in_specs=in_specs, out_specs=out_specs, check_vma=False)
```

```python
import jax
import jax.numpy as jnp
from jax import lax
from jax.experimental import pallas as pl
from jax.experimental.pallas import tpu as pltpu
from jax.sharding import PartitionSpec as P

NEG_FILL = -1e30
LOG2E = 1.4426950408889634
F32 = jnp.float32
BF16 = jnp.bfloat16
NN = (((1,), (0,)), ((), ()))
NT = (((1,), (1,)), ((), ()))
TN = (((0,), (0,)), ((), ()))


def dot(a, b, dims=NN):
    return lax.dot_general(a.astype(BF16), b.astype(BF16), dims, preferred_element_type=F32)


def parts_of(array, count):
    parts = []
    for _ in range(count):
        parts.append(array.astype(BF16))
        array = array - parts[-1].astype(F32)
    return parts


def dot_flags(arrays, flags, count=3):
    split_up = [parts_of(a, count) for a in arrays]
    left = [parts[i] for i in range(count) for parts in split_up]
    right = jnp.concatenate([jnp.where(f, 1.0, 0.0) for f in flags] * count, axis=0)
    return dot(jnp.concatenate(left, axis=1), right)


def iota(shape, axis):
    return lax.broadcasted_iota(jnp.int32, shape, axis)


def column(ref, width):
    heads = ref.shape[0]
    at = iota((heads, width), 0)
    out = jnp.full((heads, width), ref[0], F32)
    for m in range(1, heads):
        out = jnp.where(at == m, ref[m], out)
    return out


def rates(raw, bias, alog):
    rows = raw.shape[1]
    shifted = raw + bias
    step = jnp.maximum(shifted, 0.0) + jnp.log1p(jnp.exp(-jnp.abs(shifted)))
    rate = step * jnp.exp(alog)
    return step, rate, dot_flags([rate], [iota((rows, rows), 0) <= iota((rows, rows), 1)])


def spread(cols, m, width):
    return jnp.broadcast_to(cols[:, m : m + 1], (cols.shape[0], width))


def widen(factors, channels):
    heads = factors.shape[0]
    shape = (3 * heads, heads * channels)
    pick = (iota(shape, 1) // channels == iota(shape, 0) % heads).astype(BF16)
    return dot(jnp.concatenate(parts_of(factors, 3), axis=0), pick, TN)


def stack(wide, width):
    return jnp.concatenate([wide[:, i : i + width] for i in range(0, wide.shape[1], width)], axis=0)


def unstack(tall, rows):
    return jnp.concatenate([tall[i : i + rows] for i in range(0, tall.shape[0], rows)], axis=1)


def attend(jobs, scale):
    shapes = [(q.shape[0] // m.shape[0],) + m.shape for q, _, _, m in jobs]
    scores = [
        jnp.where(m[None], (dot(q, k) * (scale * LOG2E)).reshape(dims), NEG_FILL)
        for (q, k, _, m), dims in zip(jobs, shapes)
    ]
    tops = [jnp.max(s, axis=2, keepdims=True) for s in scores]
    weights = [
        jnp.exp2(s - top).reshape(dims[0] * dims[1], dims[2])
        for s, top, dims in zip(scores, tops, shapes)
    ]
    both = [
        dot(w, jnp.concatenate([v, jnp.ones_like(v)], axis=0), NT)
        for w, (_, _, v, _) in zip(weights, jobs)
    ]
    width = jobs[0][2].shape[0]
    shares = [1.0 / b[:, width:] for b in both]
    return [(b[:, :width] * share, w, share) for b, w, share in zip(both, weights, shares)]


def slot_mask(here, query_slot, slots, rows):
    masks = []
    for slot in slots:
        if slot == query_slot:
            masks.append(iota((rows, rows), 0) >= iota((rows, rows), 1))
        else:
            seen = jnp.bitwise_xor(here, slot) < jnp.bitwise_xor(here, query_slot)
            masks.append(jnp.broadcast_to(seen, (rows, rows)))
    return jnp.concatenate(masks, axis=1)


def share_kernel(*refs):
    sources, (pack, message), held, arrived = refs[:10], refs[10:12], refs[12:22], refs[22]
    copies = [
        pltpu.make_async_copy(source, here, arrived.at[i])
        for i, (source, here) in enumerate(zip(sources, held))
    ]
    for copy in copies:
        copy.start()
    raw, alog, bias, gate, cotangent, read, query, key, value, write = held
    for copy in copies[:6]:
        copy.wait()
    here = lax.axis_index("seq")
    heads, rows = raw.shape[1:]
    wide, states = gate.shape[2], read.shape[2]
    half = key.shape[1]
    gate_f = gate[0].astype(F32)
    grad_mixed = cotangent[0].astype(F32) * gate_f * jax.nn.sigmoid(gate_f)
    step, _, cum = rates(raw[0], column(bias, rows), column(alog, rows))
    decay = widen(jnp.exp(-cum), wide // heads)
    to_end = jnp.exp(cum - cum[:, rows - 1 :]) * step
    whole = jnp.broadcast_to(jnp.exp(-cum[:, rows - 1 :]), (heads, rows))
    tail = jnp.concatenate([to_end, whole], axis=0).astype(BF16)
    entry = dot(read[0], grad_mixed * decay, TN).astype(BF16)
    for copy in copies[6:]:
        copy.wait()
    pack[:half] = key[0]
    pack[half:] = value[0]
    for bit in range(message.shape[0]):
        is_early = jnp.bitwise_and(lax.shift_right_logical(here, bit), 1) == 0
        for at in range(0, wide, states):
            message[bit, at : at + rows] = jnp.where(
                is_early, query[0, :, at : at + states], entry[:, at : at + states]
            )
        message[bit, wide : wide + half] = key[0]
        message[bit, wide + half : wide + 2 * half] = value[0]
        message[bit, wide + rows : wide + 2 * rows] = write[0]
        message[bit, wide + 2 * rows :] = tail


def prepare_kernel(gate, cotangent, write, read, raw, alog, skip, bias, *outs):
    mixed_out, slope_out, step_out, in_out, out_out, own_out, fall_out, back_out = outs[:8]
    ahead_out, split_out, rates_out, skip_out = outs[8:]
    heads, rows = raw.shape[1:]
    wide = gate.shape[2]
    channels = wide // heads
    pair = 2 * channels
    alog_c, bias_c = column(alog, rows), column(bias, rows)
    step, rate, cum = rates(raw[0], bias_c, alog_c)
    for i, table in enumerate((step, rate, cum, jnp.exp(alog_c), jax.nn.sigmoid(raw[0] + bias_c))):
        rates_out[i * heads : (i + 1) * heads] = table
    head_of = iota(skip_out.shape, 1) // channels
    skip_w = jnp.full(skip_out.shape, skip[0], F32)
    for m in range(1, heads):
        skip_w = jnp.where(head_of == m, skip[m], skip_w)
    skip_out[...] = skip_w
    gate_f = gate[0].astype(F32)
    sig = jax.nn.sigmoid(gate_f)
    cot = cotangent[0].astype(F32)
    grad_mixed = cot * gate_f * sig
    mixed_out[...] = grad_mixed
    slope_out[...] = cot * sig * (1.0 + gate_f * (1.0 - sig))
    cum_cols = cum.T
    step_out[...] = widen(step, channels)
    in_out[...] = widen(jnp.exp(-cum), channels)
    out_out[...] = widen(jnp.exp(cum - cum[:, rows - 1 :]), channels)
    read_b, write_b = read[0], write[0]
    upper = iota((rows, rows), 0) <= iota((rows, rows), 1)
    lower = iota((rows, rows), 0) >= iota((rows, rows), 1)
    cross = jnp.where(lower, dot(read_b, write_b, NT), 0.0)
    cross_t = jnp.where(upper, dot(write_b, read_b, NT), 0.0)
    low = iota((rows, pair), 1) < channels
    for m in range(0, heads, 2):
        block = slice(m * channels, (m + 2) * channels)
        grad_p = grad_mixed[:, block]
        grad_d = jnp.concatenate(
            [jnp.where(low, grad_p, 0.0), jnp.where(low, 0.0, grad_p)], axis=0
        ).astype(BF16)
        split_out[m * rows : (m + 2) * rows] = grad_d
        backs = []
        for k in range(m, m + 2):
            gap = spread(cum_cols, k, rows) - cum[k : k + 1, :]
            fall = jnp.exp(-jnp.abs(gap))
            back = fall * cross_t
            at = slice(k * rows, (k + 1) * rows)
            fall_out[at] = fall
            back_out[at] = back
            ahead_out[:, at] = (fall * cross).astype(BF16)
            backs.append(back.astype(BF16))
        own_out[:, block] = dot(jnp.concatenate(backs, axis=1), grad_d)


def state_kernel(slots, scale, query, write, read, partner, *refs):
    mixed_in, step_in, in_in, out_in, own_in, fall_in, split_in, skip_in = refs[:8]
    refs = refs[8:]
    far, sources, refs = refs[: slots - 1], refs[slots - 1 : 2 * slots - 1], refs[2 * slots - 1 :]
    kept, sent, shared, scores_out, keys_out, scaled_out, base_out, products_out = refs[:8]
    (pack, *messages), arrived = refs[8 : 8 + slots], refs[8 + slots]
    copies = [
        pltpu.make_async_copy(source, held, arrived.at[i])
        for i, (source, held) in enumerate(zip(sources, (pack, *messages)))
    ]
    for copy in copies:
        copy.start()
    here = lax.axis_index("seq")
    parity = lax.axis_index("tp") % 2
    rows, wide = query.shape[1:]
    heads = fall_in.shape[0] // rows
    channels = wide // heads
    states, head_dim = write.shape[2], pack.shape[0]
    half, pair, count = head_dim // 2, 2 * channels, wide // head_dim
    for copy in copies:
        copy.wait()

    key_parts, value_parts = [], []
    for slot in range(slots):
        near = messages[slot - 1][wide : wide + head_dim] if slot else pack[...]
        paired = far[slot - 1][...] if slot else partner[...]
        first = jnp.where(parity == 0, near, paired)
        second = jnp.where(parity == 0, paired, near)
        key_parts.append(jnp.concatenate([first[:half], second[:half]], axis=0))
        value_parts.append(jnp.concatenate([first[half:], second[half:]], axis=0))
    keys, values = jnp.concatenate(key_parts, axis=1), jnp.concatenate(value_parts, axis=1)
    keys_out[...] = keys

    grad_mixed, step_w, decay_in, decay_out = mixed_in[...], step_in[...], in_in[...], out_in[...]
    skip_w = skip_in[:1]
    read_b, write_b = read[0], write[0]
    tails = [m[wide + 2 * rows :].astype(F32) for m in messages]
    exit_t = jnp.zeros((states, wide), F32)
    early, to_ends = [], []
    for slot in range(1, slots):
        block = jnp.bitwise_xor(here, slot)
        early.append(block < here)
        between = jnp.ones((heads, rows), F32)
        for third in range(1, slots):
            if third != slot:
                at = jnp.bitwise_xor(here, third)
                inside = jnp.logical_and(
                    at > jnp.minimum(block, here), at < jnp.maximum(block, here)
                )
                between = between * jnp.where(inside, tails[third - 1][heads:], 1.0)
        later = unstack(messages[slot - 1][:wide], rows).astype(F32)
        if slots > 2:
            later = later * widen(between, channels)
        exit_t = exit_t + jnp.where(early[-1], 0.0, later)
        to_ends.append(widen(tails[slot - 1][:heads] * between, channels))
    exit_b = exit_t.astype(BF16)
    from_exit = decay_out * dot(write_b, exit_b)
    grad_scaled = own_in[...] + from_exit
    grad_inner = step_w * grad_scaled + skip_w * grad_mixed
    grads = stack(grad_inner, head_dim)
    grads_b = grads.astype(BF16)

    queries = stack(query[0], head_dim)
    jobs = [(queries, keys, values, slot_mask(here, 0, range(slots), rows))]
    for slot in range(1, slots):
        whole = slots > 2
        mask = slot_mask(here, slot, range(slots) if whole else [slot], rows)
        some = (keys, values) if whole else (key_parts[slot], value_parts[slot])
        jobs.append((messages[slot - 1][:wide], *some, mask))
    (attn, weights, share), *before = attend(jobs, scale)
    grad_probs = dot(grads_b, values)
    inner = unstack(attn, rows)
    scaled = inner * step_w
    scaled_b = scaled.astype(BF16)
    scaled_out[...] = scaled_b
    entry_t = jnp.zeros((states, wide), F32)
    for message, is_early, to_end, (attn_o, _, _) in zip(messages, early, to_ends, before):
        carried = unstack(attn_o, rows) * to_end
        end_state = dot(message[wide + rows : wide + 2 * rows], carried, TN)
        entry_t = entry_t + jnp.where(is_early, end_state, 0.0)
    entry_b = entry_t.astype(BF16)
    from_entry = decay_in * dot(read_b, entry_b)
    base_out[...] = from_entry + skip_w * inner

    product = grads * attn
    ones = jnp.ones((2 * head_dim, head_dim), BF16)
    delta = dot(jnp.concatenate(parts_of(product, 2), axis=1), ones)
    probs = weights * jnp.concatenate([share] * slots, axis=1)
    grad_scores = (probs * (grad_probs - jnp.concatenate([delta] * slots, axis=1))).astype(BF16)
    scores_out[...] = grad_scores
    key_t = (dot(queries, grad_scores, TN) * scale).astype(BF16)
    value_t = dot(grads_b, probs, TN).astype(BF16)
    for slot in range(slots):
        block = slice(slot * rows, (slot + 1) * rows)
        first = jnp.concatenate([key_t[:half, block], value_t[:half, block]], axis=0)
        second = jnp.concatenate([key_t[half:, block], value_t[half:, block]], axis=0)
        kept[slot] = jnp.where(parity == 0, first, second)
        sent[slot * head_dim : (slot + 1) * head_dim] = jnp.where(parity == 0, second, first)

    upper = iota((rows, rows), 0) <= iota((rows, rows), 1)
    grad_cross_t = jnp.zeros((rows, rows), F32)
    for m in range(0, heads, 2):
        outer = dot(
            scaled_b[:, m * channels : (m + 2) * channels], split_in[m * rows : (m + 2) * rows], NT
        )
        grad_cross_t = grad_cross_t + outer[:, :rows] * fall_in[m * rows : (m + 1) * rows]
        grad_cross_t = grad_cross_t + outer[:, rows:] * fall_in[(m + 1) * rows : (m + 2) * rows]
    grad_cross_t = jnp.where(upper, grad_cross_t, 0.0)
    grad_write = dot(grad_cross_t, read_b) + dot(scaled * decay_out, exit_b, NT)
    grad_read = dot(grad_cross_t, write_b, TN) + dot(grad_mixed * decay_in, entry_b, NT)
    shared[:rows] = grad_write.astype(BF16)
    shared[rows:] = grad_read.astype(BF16)
    products = (
        inner * grad_scaled,
        inner * from_exit,
        grad_mixed * from_entry,
        grad_mixed * inner,
        exit_t * entry_t,
    )
    for i, product in enumerate(products):
        products_out[i * rows : (i + 1) * rows] = product.astype(BF16)


def rates_kernel(products, scaled, halves, back, tables, grad_raw, params):
    heads, rows = grad_raw.shape[1:]
    wide = products.shape[1]
    channels = wide // heads
    step, rate, cum, grow, slope = [tables[i * heads : (i + 1) * heads] for i in range(5)]
    strict = iota((rows, rows), 0) < iota((rows, rows), 1)
    lower = iota((rows, rows), 0) >= iota((rows, rows), 1)
    terms = []
    for m in range(0, heads, 2):
        outer = dot(
            scaled[:, m * channels : (m + 2) * channels], halves[m * rows : (m + 2) * rows], NT
        )
        terms.append((outer[:, :rows] * back[m * rows : (m + 1) * rows]).astype(BF16))
        terms.append((outer[:, rows:] * back[(m + 1) * rows : (m + 2) * rows]).astype(BF16))
    later = dot(jnp.concatenate(terms, axis=0), jnp.where(lower, 1.0, 0.0))
    rate_rows = [
        jnp.sum(jnp.where(strict, later[m * rows : (m + 1) * rows], 0.0), axis=0, keepdims=True)
        for m in range(heads)
    ]
    pick = (iota((heads, wide), 1) // channels == iota((heads, wide), 0)).astype(BF16)
    sums = dot(pick, products[...], NT)
    grad_step = sums[:, :rows]
    exit_sum = sums[:, rows : 2 * rows] * step
    entry_sum = sums[:, 2 * rows : 3 * rows]
    skip_sum = sums[:, 3 * rows : 4 * rows]
    carry_sum = jnp.sum(sums[:, 4 * rows :], axis=1, keepdims=True) * jnp.exp(-cum[:, rows - 1 :])
    grad_rate = -(
        jnp.concatenate(rate_rows, axis=0)
        + dot_flags([entry_sum, exit_sum], [lower, strict])
        + carry_sum
    )
    grad_shift = (grad_step + grad_rate * grow) * slope
    grad_raw[0] = grad_shift
    terms = jnp.concatenate([grad_rate * rate, skip_sum, grad_shift], axis=0)
    summed = jnp.concatenate(parts_of(terms, 3), axis=1)
    params[:, : 3 * heads] = dot(jnp.ones((8, 3 * rows), F32), summed, NT)
    params[:, 3 * heads :] = jnp.zeros((8, params.shape[1] - 3 * heads), F32)


def output_kernel(scale, ahead, scaled, base, slope, scores, keys, grad_gate, grad_query):
    rows, wide = base.shape
    channels = wide * rows // ahead.shape[1]
    pair = 2 * channels
    low = iota((rows, pair), 1) < channels
    for at in range(0, wide, pair):
        block = slice(at, at + pair)
        scaled_p = scaled[:, block].astype(F32)
        scaled_d = jnp.concatenate(
            [jnp.where(low, scaled_p, 0.0), jnp.where(low, 0.0, scaled_p)], axis=0
        )
        m = at // channels
        mixed = dot(ahead[:, m * rows : (m + 2) * rows], scaled_d) + base[:, block]
        grad_gate[0, :, block] = mixed * slope[:, block]
    grad_query[0] = unstack(dot(scores[...], keys[...], NT) * scale, rows)


def vectors_kernel(mine, other, grad_write, grad_read):
    rows = grad_write.shape[1]
    both = mine[...].astype(F32) + other[...].astype(F32)
    grad_write[0] = both[:rows]
    grad_read[0] = both[rows:]


def finish_kernel(count, *refs):
    arrived, (mine, other, tail) = refs[:count], refs[count : count + 3]
    grad_key, grad_value, grad_alog, grad_skip, grad_bias = refs[count + 3 :]
    half, rows = grad_key.shape[1:]
    total = mine[0].astype(F32) + other[: 2 * half].astype(F32)
    for term in arrived:
        total = total + term[: 2 * half].astype(F32)
    grad_key[0] = total[:half]
    grad_value[0] = total[half:]
    heads = grad_alog.shape[0]
    params = joined(tail[...]) + joined(arrived[-1][2 * half :])
    grad_alog[...] = params[0, :heads]
    grad_skip[...] = params[0, heads : 2 * heads]
    grad_bias[...] = params[0, 2 * heads : 3 * heads]


def split(sums):
    high = lax.reduce_precision(sums, 8, 7)
    return jnp.concatenate([high.astype(BF16), (sums - high).astype(BF16)], axis=0)


def joined(tail):
    tail = tail.astype(F32)
    count = tail.shape[0] // 2
    return tail[:count] + tail[count:]


def flip(axis, distance):
    return [(i, i ^ distance) for i in range(lax.axis_size(axis))]


def shape(dims, dtype):
    return jax.ShapeDtypeStruct(tuple(dims), dtype)


VMEM = pl.BlockSpec(memory_space=pltpu.VMEM)
SMEM = pl.BlockSpec(memory_space=pltpu.SMEM)
HBM = pl.BlockSpec(memory_space=pltpu.HBM)
PARAMS = pltpu.CompilerParams(vmem_limit_bytes=48 * 1024 * 1024)


def call(kernel, outs, args, specs=None, scratch=(), flops=0):
    return pl.pallas_call(
        kernel,
        out_shape=outs,
        in_specs=[(specs or {}).get(i, VMEM) for i in range(len(args))],
        out_specs=jax.tree.map(lambda _: VMEM, outs),
        scratch_shapes=scratch,
        compiler_params=PARAMS,
        cost_estimate=pl.CostEstimate(flops=flops, bytes_accessed=0, transcendentals=0),
    )(*args)


def swap(array, seq_bits, tp_bits):
    n_seq, n_tp = lax.axis_size("seq"), lax.axis_size("tp")
    pairs = [
        (s * n_tp + t, (s ^ seq_bits) * n_tp + (t ^ tp_bits))
        for s in range(n_seq)
        for t in range(n_tp)
    ]
    return lax.ppermute(array, ("seq", "tp"), pairs)


def body(
    query_rows,
    key_rows,
    value_rows,
    gate_rows,
    write_vec,
    read_vec,
    dt_raw,
    a_log,
    skip_gain,
    dt_bias,
    out_grad,
):
    slots = lax.axis_size("seq")
    rows, wide = query_rows.shape[1:]
    head_dim = 2 * key_rows.shape[2]
    states = write_vec.shape[2]
    heads = a_log.shape[0]
    scale = head_dim ** (-0.5)

    bits = slots.bit_length() - 1
    key_t, value_t = key_rows.swapaxes(1, 2), value_rows.swapaxes(1, 2)
    sources = (
        dt_raw,
        a_log,
        dt_bias,
        gate_rows,
        out_grad,
        read_vec,
        query_rows,
        key_t,
        value_t,
        write_vec,
    )
    pack, message = pl.pallas_call(
        share_kernel,
        out_shape=(
            shape((head_dim, rows), BF16),
            shape((bits, wide + 2 * rows + 2 * heads, head_dim), BF16),
        ),
        in_specs=[HBM] * len(sources),
        out_specs=(VMEM, VMEM),
        scratch_shapes=[
            pltpu.SMEM(a.shape, a.dtype) if a.ndim == 1 else pltpu.VMEM(a.shape, a.dtype)
            for a in sources
        ]
        + [pltpu.SemaphoreType.DMA((len(sources),))],
        compiler_params=PARAMS,
    )(*[pltpu.with_memory_space_constraint(a, pltpu.HBM) for a in sources])
    messages = [swap(message[slot.bit_length() - 1], slot, 0) for slot in range(1, slots)]
    partner = swap(pack, 0, 1)
    far = [swap(pack, slot, 1) for slot in range(1, slots)]

    wide_f, wide_b = shape((rows, wide), F32), shape((rows, wide), BF16)
    tall_f = shape((heads * rows, rows), F32)
    prepared = call(
        prepare_kernel,
        (wide_f,) * 6
        + (tall_f, tall_f)
        + (shape((rows, heads * rows), BF16), shape((heads * rows, 2 * wide // heads), BF16))
        + (shape((5 * heads, rows), F32), shape((8, wide), F32)),
        (gate_rows, out_grad, write_vec, read_vec, dt_raw, a_log, skip_gain, dt_bias),
        {5: SMEM, 6: SMEM, 7: SMEM},
    )
    grad_mixed, slope, step_w, decay_in, decay_out, own, fall, back = prepared[:8]
    ahead, halves, tables, skip_w = prepared[8:]
    mine, other, shared, scores, keys, scaled, base, products = call(
        lambda *refs: state_kernel(slots, scale, *refs),
        (
            shape((slots, head_dim, rows), BF16),
            shape((slots * head_dim, rows), BF16),
            shape((2 * rows, states), BF16),
            shape((wide // head_dim * rows, slots * rows), BF16),
            shape((head_dim, slots * rows), BF16),
            wide_b,
            wide_f,
            shape((5 * rows, wide), BF16),
        ),
        (
            query_rows,
            write_vec,
            read_vec,
            partner,
            grad_mixed,
            step_w,
            decay_in,
            decay_out,
            own,
            fall,
            halves,
            skip_w,
            *far,
            pack,
            *messages,
        ),
        {11 + slots + i: HBM for i in range(slots)},
        [pltpu.VMEM(m.shape, m.dtype) for m in (pack, *messages)]
        + [pltpu.SemaphoreType.DMA((slots,))],
    )
    got = swap(other, 0, 1)
    grad_dt, params = call(
        rates_kernel,
        (shape((1, heads, rows), F32), shape((8, states), F32)),
        (products, scaled, halves, back, tables),
    )
    n_tp = lax.axis_size("tp")
    reaches = [1 << bit for bit in range(1, n_tp.bit_length() - 1)] + [1]
    got_shared = swap(shared, 0, reaches[0])
    got, got_shared = lax.optimization_barrier((got, got_shared))
    for reach in reaches[1:]:
        shared = (shared.astype(F32) + got_shared.astype(F32)).astype(BF16)
        got_shared = swap(shared, 0, reach)
    reach = 1
    while reach < lax.axis_size("dp"):
        near = [params] + [lax.ppermute(params, "dp", flip("dp", k * reach)) for k in (1, 2, 3)]
        shared, *near = lax.optimization_barrier((shared, *near))
        params = (near[0] + near[1]) + (near[2] + near[3])
        reach *= 4
    sent = [
        (mine[slot].astype(F32) + got[slot * head_dim : (slot + 1) * head_dim].astype(F32)).astype(BF16)
        for slot in range(1, slots)
    ]
    arrived = [swap(sent[slot - 1], slot, 0) for slot in range(1, slots) if slot & (slot - 1)]
    slot = 1
    while slot < slots:
        tail = split(params)
        arrived.append(swap(jnp.concatenate([sent[slot - 1], tail], axis=0), slot, 0))
        slot *= 2
        if slot < slots:
            params = joined(tail) + joined(arrived[-1][head_dim:])
    scores, shared = lax.optimization_barrier((scores, shared))
    grad_gate, grad_query = call(
        lambda *refs: output_kernel(scale, *refs),
        (shape((1, rows, wide), F32), shape((1, rows, wide), F32)),
        (ahead, scaled, base, slope, scores, keys),
    )
    vector = shape((heads,), F32)
    half = shape((1, head_dim // 2, rows), F32)
    full = shape((1, rows, states), F32)
    grad_write, grad_read = call(vectors_kernel, (full, full), (shared, got_shared))
    grad_write, *arrived = lax.optimization_barrier((grad_write, *arrived))
    grad_key, grad_value, grad_alog, grad_skip, grad_bias = call(
        lambda *refs: finish_kernel(len(arrived), *refs),
        (half, half, vector, vector, vector),
        (*arrived, mine, got, tail),
    )
    grad_key, grad_value = grad_key.swapaxes(1, 2), grad_value.swapaxes(1, 2)
    return (
        grad_query,
        grad_key,
        grad_value,
        grad_gate,
        grad_write,
        grad_read,
        grad_dt,
        grad_alog,
        grad_skip,
        grad_bias,
    )


def solution(mesh):
    in_specs = (
        P("dp", "seq", "tp"),
        P("dp", "seq", "tp"),
        P("dp", "seq", "tp"),
        P("dp", "seq", "tp"),
        P("dp", "seq", None),
        P("dp", "seq", None),
        P("dp", "tp", "seq"),
        P("tp"),
        P("tp"),
        P("tp"),
        P("dp", "seq", "tp"),
    )
    out_specs = (
        P("dp", "seq", "tp"),
        P("dp", "seq", "tp"),
        P("dp", "seq", "tp"),
        P("dp", "seq", "tp"),
        P("dp", "seq", None),
        P("dp", "seq", None),
        P("dp", "tp", "seq"),
        P("tp"),
        P("tp"),
        P("tp"),
    )
    return jax.shard_map(body, mesh=mesh, in_specs=in_specs, out_specs=out_specs, check_vma=False)
```

```python
import jax
import jax.numpy as jnp
from jax import lax
from jax.experimental import pallas as pl
from jax.experimental.pallas import tpu as pltpu
from jax.sharding import PartitionSpec as P

NEG_FILL = -1e30
LOG2E = 1.4426950408889634
F32 = jnp.float32
BF16 = jnp.bfloat16
NN = (((1,), (0,)), ((), ()))
NT = (((1,), (1,)), ((), ()))
TN = (((0,), (0,)), ((), ()))


def dot(a, b, dims=NN):
    return lax.dot_general(a.astype(BF16), b.astype(BF16), dims, preferred_element_type=F32)


def parts_of(array, count):
    parts = []
    for _ in range(count):
        parts.append(array.astype(BF16))
        array = array - parts[-1].astype(F32)
    return parts


def dot_flags(arrays, flags, count=3):
    split_up = [parts_of(a, count) for a in arrays]
    left = [parts[i] for i in range(count) for parts in split_up]
    right = jnp.concatenate([jnp.where(f, 1.0, 0.0) for f in flags] * count, axis=0)
    return dot(jnp.concatenate(left, axis=1), right)


def iota(shape, axis):
    return lax.broadcasted_iota(jnp.int32, shape, axis)


def column(ref, width):
    heads = ref.shape[0]
    at = iota((heads, width), 0)
    out = jnp.full((heads, width), ref[0], F32)
    for m in range(1, heads):
        out = jnp.where(at == m, ref[m], out)
    return out


def rates(raw, bias, alog):
    rows = raw.shape[1]
    shifted = raw + bias
    step = jnp.maximum(shifted, 0.0) + jnp.log1p(jnp.exp(-jnp.abs(shifted)))
    rate = step * jnp.exp(alog)
    return step, rate, dot_flags([rate], [iota((rows, rows), 0) <= iota((rows, rows), 1)])


def spread(cols, m, width):
    return jnp.broadcast_to(cols[:, m : m + 1], (cols.shape[0], width))


def widen(factors, channels):
    heads = factors.shape[0]
    shape = (3 * heads, heads * channels)
    pick = (iota(shape, 1) // channels == iota(shape, 0) % heads).astype(BF16)
    return dot(jnp.concatenate(parts_of(factors, 3), axis=0), pick, TN)


def stack(wide, width):
    return jnp.concatenate([wide[:, i : i + width] for i in range(0, wide.shape[1], width)], axis=0)


def unstack(tall, rows):
    return jnp.concatenate([tall[i : i + rows] for i in range(0, tall.shape[0], rows)], axis=1)


def attend(jobs, scale):
    shapes = [(q.shape[0] // m.shape[0],) + m.shape for q, _, _, m in jobs]
    scores = [
        jnp.where(m[None], (dot(q, k) * (scale * LOG2E)).reshape(dims), NEG_FILL)
        for (q, k, _, m), dims in zip(jobs, shapes)
    ]
    tops = [jnp.max(s, axis=2, keepdims=True) for s in scores]
    weights = [
        jnp.exp2(s - top).reshape(dims[0] * dims[1], dims[2])
        for s, top, dims in zip(scores, tops, shapes)
    ]
    both = [
        dot(w, jnp.concatenate([v, jnp.ones_like(v)], axis=0), NT)
        for w, (_, _, v, _) in zip(weights, jobs)
    ]
    width = jobs[0][2].shape[0]
    shares = [1.0 / b[:, width:] for b in both]
    return [(b[:, :width] * share, w, share) for b, w, share in zip(both, weights, shares)]


def slot_mask(here, query_slot, slots, rows):
    masks = []
    for slot in slots:
        if slot == query_slot:
            masks.append(iota((rows, rows), 0) >= iota((rows, rows), 1))
        else:
            seen = jnp.bitwise_xor(here, slot) < jnp.bitwise_xor(here, query_slot)
            masks.append(jnp.broadcast_to(seen, (rows, rows)))
    return jnp.concatenate(masks, axis=1)


def share_kernel(*refs):
    sources, (pack, message), held, arrived = refs[:10], refs[10:12], refs[12:22], refs[22]
    raw, gate, cotangent, read, query, write, alog, bias, key, value = held
    copies = [
        pltpu.make_async_copy(source, here, arrived.at[i])
        for i, (source, here) in enumerate(zip(sources, held))
    ]
    for place in (0, 6, 7, 1, 2, 3, 4, 8, 9, 5):
        copies[place].start()
    for place in (0, 6, 7):
        copies[place].wait()
    here = lax.axis_index("seq")
    heads, rows = raw.shape[1:]
    wide, states = gate.shape[2], read.shape[2]
    half = key.shape[1]
    step, _, cum = rates(raw[0], column(bias, rows), column(alog, rows))
    decay = widen(jnp.exp(-cum), wide // heads)
    to_end = jnp.exp(cum - cum[:, rows - 1 :]) * step
    whole = jnp.broadcast_to(jnp.exp(-cum[:, rows - 1 :]), (heads, rows))
    tail = jnp.concatenate([to_end, whole], axis=0).astype(BF16)
    for place in (1, 2, 3):
        copies[place].wait()
    gate_f = gate[0].astype(F32)
    grad_mixed = cotangent[0].astype(F32) * gate_f * jax.nn.sigmoid(gate_f)
    entry = dot(read[0], grad_mixed * decay, TN).astype(BF16)
    for place in (4, 5, 8, 9):
        copies[place].wait()
    pack[:half] = key[0]
    pack[half:] = value[0]
    for bit in range(message.shape[0]):
        is_early = jnp.bitwise_and(lax.shift_right_logical(here, bit), 1) == 0
        for at in range(0, wide, states):
            message[bit, at : at + rows] = jnp.where(
                is_early, query[0, :, at : at + states], entry[:, at : at + states]
            )
        message[bit, wide : wide + half] = key[0]
        message[bit, wide + half : wide + 2 * half] = value[0]
        message[bit, wide + rows : wide + 2 * rows] = write[0]
        message[bit, wide + 2 * rows :] = tail


def prepare_kernel(gate, cotangent, write, read, raw, alog, skip, bias, *outs):
    mixed_out, slope_out, step_out, in_out, out_out, own_out, fall_out, back_out = outs[:8]
    ahead_out, split_out, rates_out, skip_out = outs[8:]
    heads, rows = raw.shape[1:]
    wide = gate.shape[2]
    channels = wide // heads
    pair = 2 * channels
    alog_c, bias_c = column(alog, rows), column(bias, rows)
    step, rate, cum = rates(raw[0], bias_c, alog_c)
    for i, table in enumerate((step, rate, cum, jnp.exp(alog_c), jax.nn.sigmoid(raw[0] + bias_c))):
        rates_out[i * heads : (i + 1) * heads] = table
    head_of = iota(skip_out.shape, 1) // channels
    skip_w = jnp.full(skip_out.shape, skip[0], F32)
    for m in range(1, heads):
        skip_w = jnp.where(head_of == m, skip[m], skip_w)
    skip_out[...] = skip_w
    gate_f = gate[0].astype(F32)
    sig = jax.nn.sigmoid(gate_f)
    cot = cotangent[0].astype(F32)
    grad_mixed = cot * gate_f * sig
    mixed_out[...] = grad_mixed
    slope_out[...] = cot * sig * (1.0 + gate_f * (1.0 - sig))
    cum_cols = cum.T
    step_out[...] = widen(step, channels)
    in_out[...] = widen(jnp.exp(-cum), channels)
    out_out[...] = widen(jnp.exp(cum - cum[:, rows - 1 :]), channels)
    read_b, write_b = read[0], write[0]
    upper = iota((rows, rows), 0) <= iota((rows, rows), 1)
    lower = iota((rows, rows), 0) >= iota((rows, rows), 1)
    cross = jnp.where(lower, dot(read_b, write_b, NT), 0.0)
    cross_t = jnp.where(upper, dot(write_b, read_b, NT), 0.0)
    low = iota((rows, pair), 1) < channels
    for m in range(0, heads, 2):
        block = slice(m * channels, (m + 2) * channels)
        grad_p = grad_mixed[:, block]
        grad_d = jnp.concatenate(
            [jnp.where(low, grad_p, 0.0), jnp.where(low, 0.0, grad_p)], axis=0
        ).astype(BF16)
        split_out[m * rows : (m + 2) * rows] = grad_d
        backs = []
        for k in range(m, m + 2):
            gap = spread(cum_cols, k, rows) - cum[k : k + 1, :]
            fall = jnp.exp(-jnp.abs(gap))
            back = fall * cross_t
            at = slice(k * rows, (k + 1) * rows)
            fall_out[at] = fall
            back_out[at] = back
            ahead_out[:, at] = (fall * cross).astype(BF16)
            backs.append(back.astype(BF16))
        own_out[:, block] = dot(jnp.concatenate(backs, axis=1), grad_d)


def state_kernel(slots, scale, query, write, read, partner, *refs):
    mixed_in, step_in, in_in, out_in, own_in, fall_in, split_in, skip_in = refs[:8]
    refs = refs[8:]
    far, (pack, *messages) = refs[: slots - 1], refs[slots - 1 : 2 * slots - 1]
    refs = refs[2 * slots - 1 :]
    kept, sent, scores_out, keys_out, scaled_out, base_out, products_out = refs
    here = lax.axis_index("seq")
    parity = lax.axis_index("tp") % 2
    rows, wide = query.shape[1:]
    heads = fall_in.shape[0] // rows
    channels = wide // heads
    states, head_dim = write.shape[2], pack.shape[0]
    half, pair, count = head_dim // 2, 2 * channels, wide // head_dim
    key_parts, value_parts = [], []
    for slot in range(slots):
        near = messages[slot - 1][wide : wide + head_dim] if slot else pack[...]
        paired = far[slot - 1][...] if slot else partner[...]
        first = jnp.where(parity == 0, near, paired)
        second = jnp.where(parity == 0, paired, near)
        key_parts.append(jnp.concatenate([first[:half], second[:half]], axis=0))
        value_parts.append(jnp.concatenate([first[half:], second[half:]], axis=0))
    keys, values = jnp.concatenate(key_parts, axis=1), jnp.concatenate(value_parts, axis=1)
    keys_out[...] = keys

    grad_mixed, step_w, decay_in, decay_out = mixed_in[...], step_in[...], in_in[...], out_in[...]
    skip_w = skip_in[:1]
    read_b, write_b = read[0], write[0]
    tails = [m[wide + 2 * rows :].astype(F32) for m in messages]
    exit_t = jnp.zeros((states, wide), F32)
    early, to_ends = [], []
    for slot in range(1, slots):
        block = jnp.bitwise_xor(here, slot)
        early.append(block < here)
        between = jnp.ones((heads, rows), F32)
        for third in range(1, slots):
            if third != slot:
                at = jnp.bitwise_xor(here, third)
                inside = jnp.logical_and(
                    at > jnp.minimum(block, here), at < jnp.maximum(block, here)
                )
                between = between * jnp.where(inside, tails[third - 1][heads:], 1.0)
        later = unstack(messages[slot - 1][:wide], rows).astype(F32)
        if slots > 2:
            later = later * widen(between, channels)
        exit_t = exit_t + jnp.where(early[-1], 0.0, later)
        to_ends.append(widen(tails[slot - 1][:heads] * between, channels))
    exit_b = exit_t.astype(BF16)
    from_exit = decay_out * dot(write_b, exit_b)
    grad_scaled = own_in[...] + from_exit
    grad_inner = step_w * grad_scaled + skip_w * grad_mixed
    grads = stack(grad_inner, head_dim)
    grads_b = grads.astype(BF16)

    queries = stack(query[0], head_dim)
    jobs = [(queries, keys, values, slot_mask(here, 0, range(slots), rows))]
    for slot in range(1, slots):
        whole = slots > 2
        mask = slot_mask(here, slot, range(slots) if whole else [slot], rows)
        some = (keys, values) if whole else (key_parts[slot], value_parts[slot])
        jobs.append((messages[slot - 1][:wide], *some, mask))
    (attn, weights, share), *before = attend(jobs, scale)
    grad_probs = dot(grads_b, values)
    inner = unstack(attn, rows)
    scaled = inner * step_w
    scaled_b = scaled.astype(BF16)
    scaled_out[...] = scaled_b
    entry_t = jnp.zeros((states, wide), F32)
    for message, is_early, to_end, (attn_o, _, _) in zip(messages, early, to_ends, before):
        carried = unstack(attn_o, rows) * to_end
        end_state = dot(message[wide + rows : wide + 2 * rows], carried, TN)
        entry_t = entry_t + jnp.where(is_early, end_state, 0.0)
    entry_b = entry_t.astype(BF16)
    from_entry = decay_in * dot(read_b, entry_b)
    base_out[...] = from_entry + skip_w * inner

    product = grads * attn
    ones = jnp.ones((2 * head_dim, head_dim), BF16)
    delta = dot(jnp.concatenate(parts_of(product, 2), axis=1), ones)
    probs = weights * jnp.concatenate([share] * slots, axis=1)
    grad_scores = (probs * (grad_probs - jnp.concatenate([delta] * slots, axis=1))).astype(BF16)
    scores_out[...] = grad_scores
    key_t = (dot(queries, grad_scores, TN) * scale).astype(BF16)
    value_t = dot(grads_b, probs, TN).astype(BF16)
    for slot in range(slots):
        block = slice(slot * rows, (slot + 1) * rows)
        first = jnp.concatenate([key_t[:half, block], value_t[:half, block]], axis=0)
        second = jnp.concatenate([key_t[half:, block], value_t[half:, block]], axis=0)
        kept[slot] = jnp.where(parity == 0, first, second)
        sent[slot * head_dim : (slot + 1) * head_dim] = jnp.where(parity == 0, second, first)

    upper = iota((rows, rows), 0) <= iota((rows, rows), 1)
    grad_cross_t = jnp.zeros((rows, rows), F32)
    for m in range(0, heads, 2):
        outer = dot(
            scaled_b[:, m * channels : (m + 2) * channels], split_in[m * rows : (m + 2) * rows], NT
        )
        grad_cross_t = grad_cross_t + outer[:, :rows] * fall_in[m * rows : (m + 1) * rows]
        grad_cross_t = grad_cross_t + outer[:, rows:] * fall_in[(m + 1) * rows : (m + 2) * rows]
    grad_cross_t = jnp.where(upper, grad_cross_t, 0.0)
    grad_write = dot(grad_cross_t, read_b) + dot(scaled * decay_out, exit_b, NT)
    grad_read = dot(grad_cross_t, write_b, TN) + dot(grad_mixed * decay_in, entry_b, NT)
    sent[slots * head_dim : slots * head_dim + rows] = grad_write.astype(BF16)
    sent[slots * head_dim + rows :] = grad_read.astype(BF16)
    products = (
        inner * grad_scaled,
        inner * from_exit,
        grad_mixed * from_entry,
        grad_mixed * inner,
        exit_t * entry_t,
    )
    for i, product in enumerate(products):
        products_out[i * rows : (i + 1) * rows] = product.astype(BF16)


def rates_kernel(products, scaled, halves, back, tables, grad_raw, params):
    heads, rows = grad_raw.shape[1:]
    wide = products.shape[1]
    channels = wide // heads
    step, rate, cum, grow, slope = [tables[i * heads : (i + 1) * heads] for i in range(5)]
    strict = iota((rows, rows), 0) < iota((rows, rows), 1)
    lower = iota((rows, rows), 0) >= iota((rows, rows), 1)
    terms = []
    for m in range(0, heads, 2):
        outer = dot(
            scaled[:, m * channels : (m + 2) * channels], halves[m * rows : (m + 2) * rows], NT
        )
        terms.append((outer[:, :rows] * back[m * rows : (m + 1) * rows]).astype(BF16))
        terms.append((outer[:, rows:] * back[(m + 1) * rows : (m + 2) * rows]).astype(BF16))
    later = dot(jnp.concatenate(terms, axis=0), jnp.where(lower, 1.0, 0.0))
    rate_rows = [
        jnp.sum(jnp.where(strict, later[m * rows : (m + 1) * rows], 0.0), axis=0, keepdims=True)
        for m in range(heads)
    ]
    pick = (iota((heads, wide), 1) // channels == iota((heads, wide), 0)).astype(BF16)
    sums = dot(pick, products[...], NT)
    grad_step = sums[:, :rows]
    exit_sum = sums[:, rows : 2 * rows] * step
    entry_sum = sums[:, 2 * rows : 3 * rows]
    skip_sum = sums[:, 3 * rows : 4 * rows]
    carry_sum = jnp.sum(sums[:, 4 * rows :], axis=1, keepdims=True) * jnp.exp(-cum[:, rows - 1 :])
    grad_rate = -(
        jnp.concatenate(rate_rows, axis=0)
        + dot_flags([entry_sum, exit_sum], [lower, strict])
        + carry_sum
    )
    grad_shift = (grad_step + grad_rate * grow) * slope
    grad_raw[0] = grad_shift
    terms = jnp.concatenate([grad_rate * rate, skip_sum, grad_shift], axis=0)
    summed = jnp.concatenate(parts_of(terms, 3), axis=1)
    params[:, : 3 * heads] = dot(jnp.ones((8, 3 * rows), F32), summed, NT)
    params[:, 3 * heads :] = jnp.zeros((8, params.shape[1] - 3 * heads), F32)


def output_kernel(scale, ahead, scaled, base, slope, scores, keys, grad_gate, grad_query):
    rows, wide = base.shape
    channels = wide * rows // ahead.shape[1]
    pair = 2 * channels
    low = iota((rows, pair), 1) < channels
    for at in range(0, wide, pair):
        block = slice(at, at + pair)
        scaled_p = scaled[:, block].astype(F32)
        scaled_d = jnp.concatenate(
            [jnp.where(low, scaled_p, 0.0), jnp.where(low, 0.0, scaled_p)], axis=0
        )
        m = at // channels
        mixed = dot(ahead[:, m * rows : (m + 2) * rows], scaled_d) + base[:, block]
        grad_gate[0, :, block] = mixed * slope[:, block]
    grad_query[0] = unstack(dot(scores[...], keys[...], NT) * scale, rows)


def vectors_kernel(mine, other, grad_write, grad_read):
    rows = grad_write.shape[1]
    both = mine[...].astype(F32) + other[...].astype(F32)
    grad_write[0] = both[:rows]
    grad_read[0] = both[rows:]


def finish_kernel(count, *refs):
    arrived, (mine, other, tail) = refs[:count], refs[count : count + 3]
    grad_key, grad_value, grad_alog, grad_skip, grad_bias = refs[count + 3 :]
    half, rows = grad_key.shape[1:]
    total = mine[0].astype(F32) + other[: 2 * half].astype(F32)
    for term in arrived:
        total = total + term[: 2 * half].astype(F32)
    grad_key[0] = total[:half]
    grad_value[0] = total[half:]
    heads = grad_alog.shape[0]
    params = joined(tail[...]) + joined(arrived[-1][2 * half :])
    grad_alog[...] = params[0, :heads]
    grad_skip[...] = params[0, heads : 2 * heads]
    grad_bias[...] = params[0, 2 * heads : 3 * heads]


def split(sums):
    high = lax.reduce_precision(sums, 8, 7)
    return jnp.concatenate([high.astype(BF16), (sums - high).astype(BF16)], axis=0)


def joined(tail):
    tail = tail.astype(F32)
    count = tail.shape[0] // 2
    return tail[:count] + tail[count:]


def flip(axis, distance):
    return [(i, i ^ distance) for i in range(lax.axis_size(axis))]


def shape(dims, dtype):
    return jax.ShapeDtypeStruct(tuple(dims), dtype)


VMEM = pl.BlockSpec(memory_space=pltpu.VMEM)
SMEM = pl.BlockSpec(memory_space=pltpu.SMEM)
HBM = pl.BlockSpec(memory_space=pltpu.HBM)
PARAMS = pltpu.CompilerParams(vmem_limit_bytes=48 * 1024 * 1024)


def call(kernel, outs, args, specs=None):
    return pl.pallas_call(
        kernel,
        out_shape=outs,
        in_specs=[(specs or {}).get(i, VMEM) for i in range(len(args))],
        out_specs=jax.tree.map(lambda _: VMEM, outs),
        compiler_params=PARAMS,
        cost_estimate=pl.CostEstimate(flops=0, bytes_accessed=0, transcendentals=0),
    )(*args)


def swap(array, seq_bits, tp_bits):
    n_seq, n_tp = lax.axis_size("seq"), lax.axis_size("tp")
    pairs = [
        (s * n_tp + t, (s ^ seq_bits) * n_tp + (t ^ tp_bits))
        for s in range(n_seq)
        for t in range(n_tp)
    ]
    return lax.ppermute(array, ("seq", "tp"), pairs)


def body(
    query_rows,
    key_rows,
    value_rows,
    gate_rows,
    write_vec,
    read_vec,
    dt_raw,
    a_log,
    skip_gain,
    dt_bias,
    out_grad,
):
    slots = lax.axis_size("seq")
    rows, wide = query_rows.shape[1:]
    head_dim = 2 * key_rows.shape[2]
    states = write_vec.shape[2]
    heads = a_log.shape[0]
    scale = head_dim ** (-0.5)

    bits = slots.bit_length() - 1
    key_t, value_t = key_rows.swapaxes(1, 2), value_rows.swapaxes(1, 2)
    kept_here = (dt_raw, gate_rows, out_grad, read_vec, query_rows, write_vec)
    sources = kept_here + (a_log, dt_bias, key_t, value_t)
    pack, message, dt_raw, gate_rows, out_grad, read_vec, query_rows, write_vec = pl.pallas_call(
        share_kernel,
        out_shape=(
            shape((head_dim, rows), BF16),
            shape((bits, wide + 2 * rows + 2 * heads, head_dim), BF16),
        )
        + tuple(shape(a.shape, a.dtype) for a in kept_here),
        in_specs=[HBM] * len(sources),
        out_specs=(VMEM,) * (2 + len(kept_here)),
        scratch_shapes=[
            pltpu.SMEM(a.shape, a.dtype) if a.ndim == 1 else pltpu.VMEM(a.shape, a.dtype)
            for a in sources[len(kept_here) :]
        ]
        + [pltpu.SemaphoreType.DMA((len(sources),))],
        compiler_params=PARAMS,
    )(*[pltpu.with_memory_space_constraint(a, pltpu.HBM) for a in sources])
    messages = [swap(message[slot.bit_length() - 1], slot, 0) for slot in range(1, slots)]
    partner = swap(pack, 0, 1)
    far = [swap(pack, slot, 1) for slot in range(1, slots)]

    wide_f, wide_b = shape((rows, wide), F32), shape((rows, wide), BF16)
    tall_f = shape((heads * rows, rows), F32)
    prepared = call(
        prepare_kernel,
        (wide_f,) * 6
        + (tall_f, tall_f)
        + (shape((rows, heads * rows), BF16), shape((heads * rows, 2 * wide // heads), BF16))
        + (shape((5 * heads, rows), F32), shape((8, wide), F32)),
        (gate_rows, out_grad, write_vec, read_vec, dt_raw, a_log, skip_gain, dt_bias),
        {5: SMEM, 6: SMEM, 7: SMEM},
    )
    grad_mixed, slope, step_w, decay_in, decay_out, own, fall, back = prepared[:8]
    ahead, halves, tables, skip_w = prepared[8:]
    mine, other, scores, keys, scaled, base, products = call(
        lambda *refs: state_kernel(slots, scale, *refs),
        (
            shape((slots, head_dim, rows), BF16),
            shape((slots * head_dim + 2 * rows, states), BF16),
            shape((wide // head_dim * rows, slots * rows), BF16),
            shape((head_dim, slots * rows), BF16),
            wide_b,
            wide_f,
            shape((5 * rows, wide), BF16),
        ),
        (
            query_rows,
            write_vec,
            read_vec,
            partner,
            grad_mixed,
            step_w,
            decay_in,
            decay_out,
            own,
            fall,
            halves,
            skip_w,
            *far,
            pack,
            *messages,
        ),
    )
    got = swap(other, 0, 1)
    grad_dt, params = call(
        rates_kernel,
        (shape((1, heads, rows), F32), shape((8, states), F32)),
        (products, scaled, halves, back, tables),
    )
    shared, got_shared = other[slots * head_dim :], got[slots * head_dim :]
    reach = 2
    while reach < lax.axis_size("tp"):
        shared = (shared.astype(F32) + got_shared.astype(F32)).astype(BF16)
        got_shared = swap(shared, 0, reach)
        reach *= 2
    reach = 1
    while reach < lax.axis_size("dp"):
        near = [params] + [lax.ppermute(params, "dp", flip("dp", k * reach)) for k in (1, 2, 3)]
        shared, *near = lax.optimization_barrier((shared, *near))
        params = (near[0] + near[1]) + (near[2] + near[3])
        reach *= 4
    sent = [
        (mine[slot].astype(F32) + got[slot * head_dim : (slot + 1) * head_dim].astype(F32)).astype(BF16)
        for slot in range(1, slots)
    ]
    arrived = [swap(sent[slot - 1], slot, 0) for slot in range(1, slots) if slot & (slot - 1)]
    slot = 1
    while slot < slots:
        tail = split(params)
        arrived.append(swap(jnp.concatenate([sent[slot - 1], tail], axis=0), slot, 0))
        slot *= 2
        if slot < slots:
            params = joined(tail) + joined(arrived[-1][head_dim:])
    scores, shared = lax.optimization_barrier((scores, shared))
    grad_gate, grad_query = call(
        lambda *refs: output_kernel(scale, *refs),
        (shape((1, rows, wide), F32), shape((1, rows, wide), F32)),
        (ahead, scaled, base, slope, scores, keys),
    )
    vector = shape((heads,), F32)
    half = shape((1, head_dim // 2, rows), F32)
    full = shape((1, rows, states), F32)
    grad_write, grad_read = call(vectors_kernel, (full, full), (shared, got_shared))
    grad_write, *arrived = lax.optimization_barrier((grad_write, *arrived))
    grad_key, grad_value, grad_alog, grad_skip, grad_bias = call(
        lambda *refs: finish_kernel(len(arrived), *refs),
        (half, half, vector, vector, vector),
        (*arrived, mine, got, tail),
    )
    grad_key, grad_value = grad_key.swapaxes(1, 2), grad_value.swapaxes(1, 2)
    return (
        grad_query,
        grad_key,
        grad_value,
        grad_gate,
        grad_write,
        grad_read,
        grad_dt,
        grad_alog,
        grad_skip,
        grad_bias,
    )


def solution(mesh):
    in_specs = (
        P("dp", "seq", "tp"),
        P("dp", "seq", "tp"),
        P("dp", "seq", "tp"),
        P("dp", "seq", "tp"),
        P("dp", "seq", None),
        P("dp", "seq", None),
        P("dp", "tp", "seq"),
        P("tp"),
        P("tp"),
        P("tp"),
        P("dp", "seq", "tp"),
    )
    out_specs = (
        P("dp", "seq", "tp"),
        P("dp", "seq", "tp"),
        P("dp", "seq", "tp"),
        P("dp", "seq", "tp"),
        P("dp", "seq", None),
        P("dp", "seq", None),
        P("dp", "tp", "seq"),
        P("tp"),
        P("tp"),
        P("tp"),
    )
    return jax.shard_map(body, mesh=mesh, in_specs=in_specs, out_specs=out_specs, check_vma=False)
```

```python
import jax
import jax.numpy as jnp
from jax import lax
from jax.experimental import pallas as pl
from jax.experimental.pallas import tpu as pltpu
from jax.sharding import PartitionSpec as P

NEG_FILL = -1e30
LOG2E = 1.4426950408889634
F32 = jnp.float32
BF16 = jnp.bfloat16
NN = (((1,), (0,)), ((), ()))
NT = (((1,), (1,)), ((), ()))
TN = (((0,), (0,)), ((), ()))


def dot(a, b, dims=NN):
    return lax.dot_general(a.astype(BF16), b.astype(BF16), dims, preferred_element_type=F32)


def parts_of(array, count):
    parts = []
    for _ in range(count):
        parts.append(array.astype(BF16))
        array = array - parts[-1].astype(F32)
    return parts


def dot_flags(arrays, flags, count=3):
    split_up = [parts_of(a, count) for a in arrays]
    left = [parts[i] for i in range(count) for parts in split_up]
    right = jnp.concatenate([jnp.where(f, 1.0, 0.0) for f in flags] * count, axis=0)
    return dot(jnp.concatenate(left, axis=1), right)


def iota(shape, axis):
    return lax.broadcasted_iota(jnp.int32, shape, axis)


def column(ref, width):
    heads = ref.shape[0]
    at = iota((heads, width), 0)
    out = jnp.full((heads, width), ref[0], F32)
    for m in range(1, heads):
        out = jnp.where(at == m, ref[m], out)
    return out


def upright(vector, width):
    heads = vector.shape[0]
    square = jnp.broadcast_to(vector[...].reshape(1, heads), (heads, heads))
    square = jnp.where(iota((heads, heads), 0) == iota((heads, heads), 1), square, 0.0)
    return jnp.broadcast_to(jnp.sum(square, axis=1, keepdims=True), (heads, width))


def rates(raw, bias, alog):
    rows = raw.shape[1]
    shifted = raw + bias
    step = jnp.maximum(shifted, 0.0) + jnp.log1p(jnp.exp(-jnp.abs(shifted)))
    rate = step * jnp.exp(alog)
    return step, rate, dot_flags([rate], [iota((rows, rows), 0) <= iota((rows, rows), 1)])


def spread(cols, m, width):
    return jnp.broadcast_to(cols[:, m : m + 1], (cols.shape[0], width))


def widen(factors, channels):
    heads = factors.shape[0]
    shape = (3 * heads, heads * channels)
    pick = (iota(shape, 1) // channels == iota(shape, 0) % heads).astype(BF16)
    return dot(jnp.concatenate(parts_of(factors, 3), axis=0), pick, TN)


def stack(wide, width):
    return jnp.concatenate([wide[:, i : i + width] for i in range(0, wide.shape[1], width)], axis=0)


def unstack(tall, rows):
    return jnp.concatenate([tall[i : i + rows] for i in range(0, tall.shape[0], rows)], axis=1)


def attend(jobs, scale):
    shapes = [(q.shape[0] // m.shape[0],) + m.shape for q, _, _, m in jobs]
    scores = [
        jnp.where(m[None], (dot(q, k) * (scale * LOG2E)).reshape(dims), NEG_FILL)
        for (q, k, _, m), dims in zip(jobs, shapes)
    ]
    tops = [jnp.max(s, axis=2, keepdims=True) for s in scores]
    weights = [
        jnp.exp2(s - top).reshape(dims[0] * dims[1], dims[2])
        for s, top, dims in zip(scores, tops, shapes)
    ]
    both = [
        dot(w, jnp.concatenate([v, jnp.ones_like(v)], axis=0), NT)
        for w, (_, _, v, _) in zip(weights, jobs)
    ]
    width = jobs[0][2].shape[0]
    shares = [1.0 / b[:, width:] for b in both]
    return [(b[:, :width] * share, w, share) for b, w, share in zip(both, weights, shares)]


def slot_mask(here, query_slot, slots, rows):
    masks = []
    for slot in slots:
        if slot == query_slot:
            masks.append(iota((rows, rows), 0) >= iota((rows, rows), 1))
        else:
            seen = jnp.bitwise_xor(here, slot) < jnp.bitwise_xor(here, query_slot)
            masks.append(jnp.broadcast_to(seen, (rows, rows)))
    return jnp.concatenate(masks, axis=1)


def share_kernel(*refs):
    sources, (pack, message), held, arrived = refs[:10], refs[10:12], refs[12:22], refs[22]
    raw, gate, cotangent, read, query, write, alog, bias, key, value = held
    copies = [
        pltpu.make_async_copy(source, here, arrived.at[i])
        for i, (source, here) in enumerate(zip(sources, held))
    ]
    for place in (0, 6, 7, 1, 2, 3, 4, 8, 9, 5):
        copies[place].start()
    for place in (0, 6, 7):
        copies[place].wait()
    here = lax.axis_index("seq")
    heads, rows = raw.shape[1:]
    wide, states = gate.shape[2], read.shape[2]
    half = key.shape[1]
    step, _, cum = rates(raw[0], upright(bias, rows), upright(alog, rows))
    decay = widen(jnp.exp(-cum), wide // heads)
    to_end = jnp.exp(cum - cum[:, rows - 1 :]) * step
    whole = jnp.broadcast_to(jnp.exp(-cum[:, rows - 1 :]), (heads, rows))
    tail = jnp.concatenate([to_end, whole], axis=0).astype(BF16)
    for place in (1, 2, 3):
        copies[place].wait()
    gate_f = gate[0].astype(F32)
    grad_mixed = cotangent[0].astype(F32) * gate_f * jax.nn.sigmoid(gate_f)
    entry = dot(read[0], grad_mixed * decay, TN).astype(BF16)
    for place in (4, 5, 8, 9):
        copies[place].wait()
    pack[:half] = key[0]
    pack[half:] = value[0]
    for bit in range(message.shape[0]):
        is_early = jnp.bitwise_and(lax.shift_right_logical(here, bit), 1) == 0
        for at in range(0, wide, states):
            message[bit, at : at + rows] = jnp.where(
                is_early, query[0, :, at : at + states], entry[:, at : at + states]
            )
        message[bit, wide : wide + half] = key[0]
        message[bit, wide + half : wide + 2 * half] = value[0]
        message[bit, wide + rows : wide + 2 * rows] = write[0]
        message[bit, wide + 2 * rows :] = tail


def prepare_kernel(gate, cotangent, write, read, raw, alog, skip, bias, *outs):
    mixed_out, slope_out, step_out, in_out, out_out, own_out, fall_out, back_out = outs[:8]
    ahead_out, split_out, rates_out, skip_out = outs[8:]
    heads, rows = raw.shape[1:]
    wide = gate.shape[2]
    channels = wide // heads
    pair = 2 * channels
    alog_c, bias_c = column(alog, rows), column(bias, rows)
    step, rate, cum = rates(raw[0], bias_c, alog_c)
    for i, table in enumerate((step, rate, cum, jnp.exp(alog_c), jax.nn.sigmoid(raw[0] + bias_c))):
        rates_out[i * heads : (i + 1) * heads] = table
    head_of = iota(skip_out.shape, 1) // channels
    skip_w = jnp.full(skip_out.shape, skip[0], F32)
    for m in range(1, heads):
        skip_w = jnp.where(head_of == m, skip[m], skip_w)
    skip_out[...] = skip_w
    gate_f = gate[0].astype(F32)
    sig = jax.nn.sigmoid(gate_f)
    cot = cotangent[0].astype(F32)
    grad_mixed = cot * gate_f * sig
    mixed_out[...] = grad_mixed
    slope_out[...] = cot * sig * (1.0 + gate_f * (1.0 - sig))
    cum_cols = cum.T
    step_out[...] = widen(step, channels)
    in_out[...] = widen(jnp.exp(-cum), channels)
    out_out[...] = widen(jnp.exp(cum - cum[:, rows - 1 :]), channels)
    read_b, write_b = read[0], write[0]
    upper = iota((rows, rows), 0) <= iota((rows, rows), 1)
    lower = iota((rows, rows), 0) >= iota((rows, rows), 1)
    cross = jnp.where(lower, dot(read_b, write_b, NT), 0.0)
    cross_t = jnp.where(upper, dot(write_b, read_b, NT), 0.0)
    low = iota((rows, pair), 1) < channels
    for m in range(0, heads, 2):
        block = slice(m * channels, (m + 2) * channels)
        grad_p = grad_mixed[:, block]
        grad_d = jnp.concatenate(
            [jnp.where(low, grad_p, 0.0), jnp.where(low, 0.0, grad_p)], axis=0
        ).astype(BF16)
        split_out[m * rows : (m + 2) * rows] = grad_d
        backs = []
        for k in range(m, m + 2):
            gap = spread(cum_cols, k, rows) - cum[k : k + 1, :]
            fall = jnp.exp(-jnp.abs(gap))
            back = fall * cross_t
            at = slice(k * rows, (k + 1) * rows)
            fall_out[at] = fall
            back_out[at] = back
            ahead_out[:, at] = (fall * cross).astype(BF16)
            backs.append(back.astype(BF16))
        own_out[:, block] = dot(jnp.concatenate(backs, axis=1), grad_d)


def state_kernel(slots, scale, query, write, read, partner, *refs):
    mixed_in, step_in, in_in, out_in, own_in, fall_in, split_in, skip_in = refs[:8]
    refs = refs[8:]
    far, (pack, *messages) = refs[: slots - 1], refs[slots - 1 : 2 * slots - 1]
    refs = refs[2 * slots - 1 :]
    kept, sent, scores_out, keys_out, scaled_out, base_out, products_out = refs
    here = lax.axis_index("seq")
    parity = lax.axis_index("tp") % 2
    rows, wide = query.shape[1:]
    heads = fall_in.shape[0] // rows
    channels = wide // heads
    states, head_dim = write.shape[2], pack.shape[0]
    half, pair, count = head_dim // 2, 2 * channels, wide // head_dim
    key_parts, value_parts = [], []
    for slot in range(slots):
        near = messages[slot - 1][wide : wide + head_dim] if slot else pack[...]
        paired = far[slot - 1][...] if slot else partner[...]
        first = jnp.where(parity == 0, near, paired)
        second = jnp.where(parity == 0, paired, near)
        key_parts.append(jnp.concatenate([first[:half], second[:half]], axis=0))
        value_parts.append(jnp.concatenate([first[half:], second[half:]], axis=0))
    keys, values = jnp.concatenate(key_parts, axis=1), jnp.concatenate(value_parts, axis=1)
    keys_out[...] = keys

    grad_mixed, step_w, decay_in, decay_out = mixed_in[...], step_in[...], in_in[...], out_in[...]
    skip_w = skip_in[:1]
    read_b, write_b = read[0], write[0]
    tails = [m[wide + 2 * rows :].astype(F32) for m in messages]
    exit_t = jnp.zeros((states, wide), F32)
    early, to_ends = [], []
    for slot in range(1, slots):
        block = jnp.bitwise_xor(here, slot)
        early.append(block < here)
        between = jnp.ones((heads, rows), F32)
        for third in range(1, slots):
            if third != slot:
                at = jnp.bitwise_xor(here, third)
                inside = jnp.logical_and(
                    at > jnp.minimum(block, here), at < jnp.maximum(block, here)
                )
                between = between * jnp.where(inside, tails[third - 1][heads:], 1.0)
        later = unstack(messages[slot - 1][:wide], rows).astype(F32)
        if slots > 2:
            later = later * widen(between, channels)
        exit_t = exit_t + jnp.where(early[-1], 0.0, later)
        to_ends.append(widen(tails[slot - 1][:heads] * between, channels))
    exit_b = exit_t.astype(BF16)
    from_exit = decay_out * dot(write_b, exit_b)
    grad_scaled = own_in[...] + from_exit
    grad_inner = step_w * grad_scaled + skip_w * grad_mixed
    grads = stack(grad_inner, head_dim)
    grads_b = grads.astype(BF16)

    queries = stack(query[0], head_dim)
    jobs = [(queries, keys, values, slot_mask(here, 0, range(slots), rows))]
    for slot in range(1, slots):
        whole = slots > 2
        mask = slot_mask(here, slot, range(slots) if whole else [slot], rows)
        some = (keys, values) if whole else (key_parts[slot], value_parts[slot])
        jobs.append((messages[slot - 1][:wide], *some, mask))
    (attn, weights, share), *before = attend(jobs, scale)
    grad_probs = dot(grads_b, values)
    inner = unstack(attn, rows)
    scaled = inner * step_w
    scaled_b = scaled.astype(BF16)
    scaled_out[...] = scaled_b
    entry_t = jnp.zeros((states, wide), F32)
    for message, is_early, to_end, (attn_o, _, _) in zip(messages, early, to_ends, before):
        carried = unstack(attn_o, rows) * to_end
        end_state = dot(message[wide + rows : wide + 2 * rows], carried, TN)
        entry_t = entry_t + jnp.where(is_early, end_state, 0.0)
    entry_b = entry_t.astype(BF16)
    from_entry = decay_in * dot(read_b, entry_b)
    base_out[...] = from_entry + skip_w * inner

    product = grads * attn
    ones = jnp.ones((2 * head_dim, head_dim), BF16)
    delta = dot(jnp.concatenate(parts_of(product, 2), axis=1), ones)
    probs = weights * jnp.concatenate([share] * slots, axis=1)
    grad_scores = (probs * (grad_probs - jnp.concatenate([delta] * slots, axis=1))).astype(BF16)
    scores_out[...] = grad_scores
    key_t = (dot(queries, grad_scores, TN) * scale).astype(BF16)
    value_t = dot(grads_b, probs, TN).astype(BF16)
    for slot in range(slots):
        block = slice(slot * rows, (slot + 1) * rows)
        first = jnp.concatenate([key_t[:half, block], value_t[:half, block]], axis=0)
        second = jnp.concatenate([key_t[half:, block], value_t[half:, block]], axis=0)
        kept[slot] = jnp.where(parity == 0, first, second)
        sent[slot * head_dim : (slot + 1) * head_dim] = jnp.where(parity == 0, second, first)

    upper = iota((rows, rows), 0) <= iota((rows, rows), 1)
    grad_cross_t = jnp.zeros((rows, rows), F32)
    for m in range(0, heads, 2):
        outer = dot(
            scaled_b[:, m * channels : (m + 2) * channels], split_in[m * rows : (m + 2) * rows], NT
        )
        grad_cross_t = grad_cross_t + outer[:, :rows] * fall_in[m * rows : (m + 1) * rows]
        grad_cross_t = grad_cross_t + outer[:, rows:] * fall_in[(m + 1) * rows : (m + 2) * rows]
    grad_cross_t = jnp.where(upper, grad_cross_t, 0.0)
    grad_write = dot(grad_cross_t, read_b) + dot(scaled * decay_out, exit_b, NT)
    grad_read = dot(grad_cross_t, write_b, TN) + dot(grad_mixed * decay_in, entry_b, NT)
    sent[slots * head_dim : slots * head_dim + rows] = grad_write.astype(BF16)
    sent[slots * head_dim + rows :] = grad_read.astype(BF16)
    products = (inner * grad_scaled, inner * from_exit, grad_mixed * from_entry)
    for i, product in enumerate(products):
        products_out[i * rows : (i + 1) * rows] = product.astype(BF16)
    totals = [
        jnp.sum(grad_mixed * inner, axis=0, keepdims=True),
        jnp.sum(exit_t * entry_t, axis=0, keepdims=True),
    ]
    totals = jnp.concatenate(totals + [jnp.zeros((6, wide), F32)], axis=0)
    products_out[len(products) * rows :] = jnp.concatenate(parts_of(totals, 2), axis=0)


def rates_kernel(products, scaled, halves, back, tables, grad_raw, params):
    heads, rows = grad_raw.shape[1:]
    wide = products.shape[1]
    channels = wide // heads
    step, rate, cum, grow, slope = [tables[i * heads : (i + 1) * heads] for i in range(5)]
    strict = iota((rows, rows), 0) < iota((rows, rows), 1)
    lower = iota((rows, rows), 0) >= iota((rows, rows), 1)
    terms = []
    for m in range(0, heads, 2):
        outer = dot(
            scaled[:, m * channels : (m + 2) * channels], halves[m * rows : (m + 2) * rows], NT
        )
        terms.append((outer[:, :rows] * back[m * rows : (m + 1) * rows]).astype(BF16))
        terms.append((outer[:, rows:] * back[(m + 1) * rows : (m + 2) * rows]).astype(BF16))
    later = dot(jnp.concatenate(terms, axis=0), jnp.where(lower, 1.0, 0.0))
    rate_rows = [
        jnp.sum(jnp.where(strict, later[m * rows : (m + 1) * rows], 0.0), axis=0, keepdims=True)
        for m in range(heads)
    ]
    pick = (iota((heads, wide), 1) // channels == iota((heads, wide), 0)).astype(BF16)
    sums = dot(pick, products[...], NT)
    grad_step = sums[:, :rows]
    exit_sum = sums[:, rows : 2 * rows] * step
    entry_sum = sums[:, 2 * rows : 3 * rows]
    totals = sums[:, 3 * rows : 3 * rows + 8] + sums[:, 3 * rows + 8 :]
    skip_sum = jnp.where(iota((heads, rows), 1) == 0, totals[:, :1], 0.0)
    carry_sum = totals[:, 1:2] * jnp.exp(-cum[:, rows - 1 :])
    grad_rate = -(
        jnp.concatenate(rate_rows, axis=0)
        + dot_flags([entry_sum, exit_sum], [lower, strict])
        + carry_sum
    )
    grad_shift = (grad_step + grad_rate * grow) * slope
    grad_raw[0] = grad_shift
    terms = jnp.concatenate([grad_rate * rate, skip_sum, grad_shift], axis=0)
    summed = jnp.concatenate(parts_of(terms, 3), axis=1)
    params[:, : 3 * heads] = dot(jnp.ones((8, 3 * rows), F32), summed, NT)
    params[:, 3 * heads :] = jnp.zeros((8, params.shape[1] - 3 * heads), F32)


def output_kernel(scale, ahead, scaled, base, slope, scores, keys, grad_gate, grad_query):
    rows, wide = base.shape
    channels = wide * rows // ahead.shape[1]
    pair = 2 * channels
    low = iota((rows, pair), 1) < channels
    for at in range(0, wide, pair):
        block = slice(at, at + pair)
        scaled_p = scaled[:, block].astype(F32)
        scaled_d = jnp.concatenate(
            [jnp.where(low, scaled_p, 0.0), jnp.where(low, 0.0, scaled_p)], axis=0
        )
        m = at // channels
        mixed = dot(ahead[:, m * rows : (m + 2) * rows], scaled_d) + base[:, block]
        grad_gate[0, :, block] = mixed * slope[:, block]
    grad_query[0] = unstack(dot(scores[...], keys[...], NT) * scale, rows)


def vectors_kernel(mine, other, grad_write, grad_read):
    rows = grad_write.shape[1]
    both = mine[...].astype(F32) + other[...].astype(F32)
    grad_write[0] = both[:rows]
    grad_read[0] = both[rows:]


def finish_kernel(count, *refs):
    arrived, (mine, other, tail) = refs[:count], refs[count : count + 3]
    grad_key, grad_value, grad_alog, grad_skip, grad_bias = refs[count + 3 :]
    half, rows = grad_key.shape[1:]
    total = mine[0].astype(F32) + other[: 2 * half].astype(F32)
    for term in arrived:
        total = total + term[: 2 * half].astype(F32)
    grad_key[0] = total[:half]
    grad_value[0] = total[half:]
    heads = grad_alog.shape[0]
    params = joined(tail[...]) + joined(arrived[-1][2 * half :])
    grad_alog[...] = params[0, :heads]
    grad_skip[...] = params[0, heads : 2 * heads]
    grad_bias[...] = params[0, 2 * heads : 3 * heads]


def split(sums):
    high = lax.reduce_precision(sums, 8, 7)
    return jnp.concatenate([high.astype(BF16), (sums - high).astype(BF16)], axis=0)


def joined(tail):
    tail = tail.astype(F32)
    count = tail.shape[0] // 2
    return tail[:count] + tail[count:]


def flip(axis, distance):
    return [(i, i ^ distance) for i in range(lax.axis_size(axis))]


def shape(dims, dtype):
    return jax.ShapeDtypeStruct(tuple(dims), dtype)


VMEM = pl.BlockSpec(memory_space=pltpu.VMEM)
SMEM = pl.BlockSpec(memory_space=pltpu.SMEM)
HBM = pl.BlockSpec(memory_space=pltpu.HBM)
PARAMS = pltpu.CompilerParams(vmem_limit_bytes=48 * 1024 * 1024)


def call(kernel, outs, args, specs=None):
    return pl.pallas_call(
        kernel,
        out_shape=outs,
        in_specs=[(specs or {}).get(i, VMEM) for i in range(len(args))],
        out_specs=jax.tree.map(lambda _: VMEM, outs),
        compiler_params=PARAMS,
        cost_estimate=pl.CostEstimate(flops=0, bytes_accessed=0, transcendentals=0),
    )(*args)


def swap(array, seq_bits, tp_bits):
    n_seq, n_tp = lax.axis_size("seq"), lax.axis_size("tp")
    pairs = [
        (s * n_tp + t, (s ^ seq_bits) * n_tp + (t ^ tp_bits))
        for s in range(n_seq)
        for t in range(n_tp)
    ]
    return lax.ppermute(array, ("seq", "tp"), pairs)


def body(
    query_rows,
    key_rows,
    value_rows,
    gate_rows,
    write_vec,
    read_vec,
    dt_raw,
    a_log,
    skip_gain,
    dt_bias,
    out_grad,
):
    slots = lax.axis_size("seq")
    rows, wide = query_rows.shape[1:]
    head_dim = 2 * key_rows.shape[2]
    states = write_vec.shape[2]
    heads = a_log.shape[0]
    scale = head_dim ** (-0.5)

    bits = slots.bit_length() - 1
    key_t, value_t = key_rows.swapaxes(1, 2), value_rows.swapaxes(1, 2)
    kept_here = (dt_raw, gate_rows, out_grad, read_vec, query_rows, write_vec)
    sources = kept_here + (a_log, dt_bias, key_t, value_t)
    pack, message, dt_raw, gate_rows, out_grad, read_vec, query_rows, write_vec = pl.pallas_call(
        share_kernel,
        out_shape=(
            shape((head_dim, rows), BF16),
            shape((bits, wide + 2 * rows + 2 * heads, head_dim), BF16),
        )
        + tuple(shape(a.shape, a.dtype) for a in kept_here),
        in_specs=[HBM] * len(sources),
        out_specs=(VMEM,) * (2 + len(kept_here)),
        scratch_shapes=[
            pltpu.VMEM(a.shape, a.dtype) for a in sources[len(kept_here) :]
        ]
        + [pltpu.SemaphoreType.DMA((len(sources),))],
        compiler_params=PARAMS,
    )(*[pltpu.with_memory_space_constraint(a, pltpu.HBM) for a in sources])
    messages = [swap(message[slot.bit_length() - 1], slot, 0) for slot in range(1, slots)]
    partner = swap(pack, 0, 1)
    far = [swap(pack, slot, 1) for slot in range(1, slots)]

    wide_f, wide_b = shape((rows, wide), F32), shape((rows, wide), BF16)
    tall_f = shape((heads * rows, rows), F32)
    prepared = call(
        prepare_kernel,
        (wide_f,) * 6
        + (tall_f, tall_f)
        + (shape((rows, heads * rows), BF16), shape((heads * rows, 2 * wide // heads), BF16))
        + (shape((5 * heads, rows), F32), shape((8, wide), F32)),
        (gate_rows, out_grad, write_vec, read_vec, dt_raw, a_log, skip_gain, dt_bias),
        {5: SMEM, 6: SMEM, 7: SMEM},
    )
    grad_mixed, slope, step_w, decay_in, decay_out, own, fall, back = prepared[:8]
    ahead, halves, tables, skip_w = prepared[8:]
    mine, other, scores, keys, scaled, base, products = call(
        lambda *refs: state_kernel(slots, scale, *refs),
        (
            shape((slots, head_dim, rows), BF16),
            shape((slots * head_dim + 2 * rows, states), BF16),
            shape((wide // head_dim * rows, slots * rows), BF16),
            shape((head_dim, slots * rows), BF16),
            wide_b,
            wide_f,
            shape((3 * rows + 16, wide), BF16),
        ),
        (
            query_rows,
            write_vec,
            read_vec,
            partner,
            grad_mixed,
            step_w,
            decay_in,
            decay_out,
            own,
            fall,
            halves,
            skip_w,
            *far,
            pack,
            *messages,
        ),
    )
    got = swap(other, 0, 1)
    grad_dt, params = call(
        rates_kernel,
        (shape((1, heads, rows), F32), shape((8, states), F32)),
        (products, scaled, halves, back, tables),
    )
    shared, got_shared = other[slots * head_dim :], got[slots * head_dim :]
    reach = 2
    while reach < lax.axis_size("tp"):
        shared = (shared.astype(F32) + got_shared.astype(F32)).astype(BF16)
        got_shared = swap(shared, 0, reach)
        reach *= 2
    reach = 1
    while reach < lax.axis_size("dp"):
        near = [params] + [lax.ppermute(params, "dp", flip("dp", k * reach)) for k in (1, 2, 3)]
        shared, *near = lax.optimization_barrier((shared, *near))
        params = (near[0] + near[1]) + (near[2] + near[3])
        reach *= 4
    sent = [
        (mine[slot].astype(F32) + got[slot * head_dim : (slot + 1) * head_dim].astype(F32)).astype(BF16)
        for slot in range(1, slots)
    ]
    arrived = [swap(sent[slot - 1], slot, 0) for slot in range(1, slots) if slot & (slot - 1)]
    slot = 1
    while slot < slots:
        tail = split(params)
        arrived.append(swap(jnp.concatenate([sent[slot - 1], tail], axis=0), slot, 0))
        slot *= 2
        if slot < slots:
            params = joined(tail) + joined(arrived[-1][head_dim:])
    scores, shared = lax.optimization_barrier((scores, shared))
    grad_gate, grad_query = call(
        lambda *refs: output_kernel(scale, *refs),
        (shape((1, rows, wide), F32), shape((1, rows, wide), F32)),
        (ahead, scaled, base, slope, scores, keys),
    )
    vector = shape((heads,), F32)
    half = shape((1, head_dim // 2, rows), F32)
    full = shape((1, rows, states), F32)
    grad_write, grad_read = call(vectors_kernel, (full, full), (shared, got_shared))
    grad_write, *arrived = lax.optimization_barrier((grad_write, *arrived))
    grad_key, grad_value, grad_alog, grad_skip, grad_bias = call(
        lambda *refs: finish_kernel(len(arrived), *refs),
        (half, half, vector, vector, vector),
        (*arrived, mine, got, tail),
    )
    grad_key, grad_value = grad_key.swapaxes(1, 2), grad_value.swapaxes(1, 2)
    return (
        grad_query,
        grad_key,
        grad_value,
        grad_gate,
        grad_write,
        grad_read,
        grad_dt,
        grad_alog,
        grad_skip,
        grad_bias,
    )


def solution(mesh):
    in_specs = (
        P("dp", "seq", "tp"),
        P("dp", "seq", "tp"),
        P("dp", "seq", "tp"),
        P("dp", "seq", "tp"),
        P("dp", "seq", None),
        P("dp", "seq", None),
        P("dp", "tp", "seq"),
        P("tp"),
        P("tp"),
        P("tp"),
        P("dp", "seq", "tp"),
    )
    out_specs = (
        P("dp", "seq", "tp"),
        P("dp", "seq", "tp"),
        P("dp", "seq", "tp"),
        P("dp", "seq", "tp"),
        P("dp", "seq", None),
        P("dp", "seq", None),
        P("dp", "tp", "seq"),
        P("tp"),
        P("tp"),
        P("tp"),
    )
    return jax.shard_map(body, mesh=mesh, in_specs=in_specs, out_specs=out_specs, check_vma=False)
```

```python
import jax
import jax.numpy as jnp
from jax import lax
from jax.experimental import pallas as pl
from jax.experimental.pallas import tpu as pltpu
from jax.sharding import PartitionSpec as P

NEG_FILL = -1e30
LOG2E = 1.4426950408889634
F32 = jnp.float32
BF16 = jnp.bfloat16
NN = (((1,), (0,)), ((), ()))
NT = (((1,), (1,)), ((), ()))
TN = (((0,), (0,)), ((), ()))


def dot(a, b, dims=NN):
    return lax.dot_general(a.astype(BF16), b.astype(BF16), dims, preferred_element_type=F32)


def parts_of(array, count):
    parts = []
    for _ in range(count):
        parts.append(array.astype(BF16))
        array = array - parts[-1].astype(F32)
    return parts


PARTS = 3


def flag_rows(*flags):
    return jnp.concatenate([jnp.where(f, 1.0, 0.0).astype(BF16) for f in flags] * PARTS, axis=0)


def dot_flags(arrays, rows):
    split_up = [parts_of(a, PARTS) for a in arrays]
    left = [parts[i] for i in range(PARTS) for parts in split_up]
    return dot(jnp.concatenate(left, axis=1), rows)


def over(index, size):
    if size & (size - 1):
        return index // size
    return lax.shift_right_logical(index, size.bit_length() - 1)


def upto_rows(rows):
    return flag_rows(iota((rows, rows), 0) <= iota((rows, rows), 1))


def head_rows(heads, channels):
    shape = (heads, heads * channels)
    one = jnp.where(over(iota(shape, 1), channels) == iota(shape, 0), 1.0, 0.0)
    return jnp.concatenate([one.astype(BF16)] * PARTS, axis=0)


def iota(shape, axis):
    return lax.broadcasted_iota(jnp.int32, shape, axis)


def column(ref, width):
    heads = ref.shape[0]
    at = iota((heads, width), 0)
    out = jnp.full((heads, width), ref[0], F32)
    for m in range(1, heads):
        out = jnp.where(at == m, ref[m], out)
    return out


def upright(vector, width):
    heads = vector.shape[0]
    square = jnp.broadcast_to(vector[...].reshape(1, heads), (heads, heads))
    square = jnp.where(iota((heads, heads), 0) == iota((heads, heads), 1), square, 0.0)
    return jnp.broadcast_to(jnp.sum(square, axis=1, keepdims=True), (heads, width))


def rates(raw, bias, alog, upto):
    shifted = raw + bias
    step = jnp.maximum(shifted, 0.0) + jnp.log1p(jnp.exp(-jnp.abs(shifted)))
    rate = step * jnp.exp(alog)
    return step, rate, dot_flags([rate], upto)


def spread(cols, m, width):
    return jnp.broadcast_to(cols[:, m : m + 1], (cols.shape[0], width))


def widen(factors, channels, picked=None):
    if picked is None:
        picked = head_rows(factors.shape[0], channels)
    return dot(jnp.concatenate(parts_of(factors, PARTS), axis=0), picked, TN)


def stack(wide, width):
    return jnp.concatenate([wide[:, i : i + width] for i in range(0, wide.shape[1], width)], axis=0)


def unstack(tall, rows):
    return jnp.concatenate([tall[i : i + rows] for i in range(0, tall.shape[0], rows)], axis=1)


def attend(jobs, scale):
    shapes = [(q.shape[0] // m.shape[0],) + m.shape for q, _, _, m in jobs]
    scores = [
        jnp.where(m[None], (dot(q, k) * (scale * LOG2E)).reshape(dims), NEG_FILL)
        for (q, k, _, m), dims in zip(jobs, shapes)
    ]
    tops = [jnp.max(s, axis=2, keepdims=True) for s in scores]
    weights = [
        jnp.exp2(s - top).reshape(dims[0] * dims[1], dims[2])
        for s, top, dims in zip(scores, tops, shapes)
    ]
    both = [
        dot(w, jnp.concatenate([v, jnp.ones_like(v)], axis=0), NT)
        for w, (_, _, v, _) in zip(weights, jobs)
    ]
    width = jobs[0][2].shape[0]
    shares = [1.0 / b[:, width:] for b in both]
    return [(b[:, :width] * share, w, share) for b, w, share in zip(both, weights, shares)]


def slot_mask(here, query_slot, slots, rows):
    masks = []
    for slot in slots:
        if slot == query_slot:
            masks.append(iota((rows, rows), 0) >= iota((rows, rows), 1))
        else:
            seen = jnp.bitwise_xor(here, slot) < jnp.bitwise_xor(here, query_slot)
            masks.append(jnp.broadcast_to(seen, (rows, rows)))
    return jnp.concatenate(masks, axis=1)


def share_kernel(*refs):
    sources, (pack, message), held, arrived = refs[:10], refs[10:12], refs[12:22], refs[22]
    raw, gate, cotangent, read, query, write, alog, bias, key, value = held
    copies = [
        pltpu.make_async_copy(source, here, arrived.at[i])
        for i, (source, here) in enumerate(zip(sources, held))
    ]
    for place in (0, 6, 7, 1, 2, 3, 4, 8, 9, 5):
        copies[place].start()
    here = lax.axis_index("seq")
    heads, rows = raw.shape[1:]
    wide, states = gate.shape[2], read.shape[2]
    half = key.shape[1]
    upto, picked = upto_rows(rows), head_rows(heads, wide // heads)
    for place in (0, 6, 7):
        copies[place].wait()
    step, _, cum = rates(raw[0], upright(bias, rows), upright(alog, rows), upto)
    decay = widen(jnp.exp(-cum), wide // heads, picked)
    to_end = jnp.exp(cum - cum[:, rows - 1 :]) * step
    whole = jnp.broadcast_to(jnp.exp(-cum[:, rows - 1 :]), (heads, rows))
    tail = jnp.concatenate([to_end, whole], axis=0).astype(BF16)
    for place in (1, 2, 3):
        copies[place].wait()
    gate_f = gate[0].astype(F32)
    grad_mixed = cotangent[0].astype(F32) * gate_f * jax.nn.sigmoid(gate_f)
    entry = dot(read[0], grad_mixed * decay, TN).astype(BF16)
    for place in (4, 5, 8, 9):
        copies[place].wait()
    pack[:half] = key[0]
    pack[half:] = value[0]
    for bit in range(message.shape[0]):
        is_early = jnp.bitwise_and(lax.shift_right_logical(here, bit), 1) == 0
        for at in range(0, wide, states):
            message[bit, at : at + rows] = jnp.where(
                is_early, query[0, :, at : at + states], entry[:, at : at + states]
            )
        message[bit, wide : wide + half] = key[0]
        message[bit, wide + half : wide + 2 * half] = value[0]
        message[bit, wide + rows : wide + 2 * rows] = write[0]
        message[bit, wide + 2 * rows :] = tail


def prepare_kernel(gate, cotangent, write, read, raw, alog, skip, bias, *outs):
    mixed_out, slope_out, step_out, in_out, out_out, own_out, fall_out, back_out = outs[:8]
    ahead_out, split_out, rates_out, skip_out = outs[8:]
    heads, rows = raw.shape[1:]
    wide = gate.shape[2]
    channels = wide // heads
    pair = 2 * channels
    alog_c, bias_c = column(alog, rows), column(bias, rows)
    step, rate, cum = rates(raw[0], bias_c, alog_c, upto_rows(rows))
    for i, table in enumerate((step, rate, cum, jnp.exp(alog_c), jax.nn.sigmoid(raw[0] + bias_c))):
        rates_out[i * heads : (i + 1) * heads] = table
    head_of = over(iota(skip_out.shape, 1), channels)
    skip_w = jnp.full(skip_out.shape, skip[0], F32)
    for m in range(1, heads):
        skip_w = jnp.where(head_of == m, skip[m], skip_w)
    skip_out[...] = skip_w
    gate_f = gate[0].astype(F32)
    sig = jax.nn.sigmoid(gate_f)
    cot = cotangent[0].astype(F32)
    grad_mixed = cot * gate_f * sig
    mixed_out[...] = grad_mixed
    slope_out[...] = cot * sig * (1.0 + gate_f * (1.0 - sig))
    cum_cols = cum.T
    step_out[...] = widen(step, channels)
    in_out[...] = widen(jnp.exp(-cum), channels)
    out_out[...] = widen(jnp.exp(cum - cum[:, rows - 1 :]), channels)
    read_b, write_b = read[0], write[0]
    upper = iota((rows, rows), 0) <= iota((rows, rows), 1)
    lower = iota((rows, rows), 0) >= iota((rows, rows), 1)
    cross = jnp.where(lower, dot(read_b, write_b, NT), 0.0)
    cross_t = jnp.where(upper, dot(write_b, read_b, NT), 0.0)
    low = iota((rows, pair), 1) < channels
    for m in range(0, heads, 2):
        block = slice(m * channels, (m + 2) * channels)
        grad_p = grad_mixed[:, block]
        grad_d = jnp.concatenate(
            [jnp.where(low, grad_p, 0.0), jnp.where(low, 0.0, grad_p)], axis=0
        ).astype(BF16)
        split_out[m * rows : (m + 2) * rows] = grad_d
        backs = []
        for k in range(m, m + 2):
            gap = spread(cum_cols, k, rows) - cum[k : k + 1, :]
            fall = jnp.exp(-jnp.abs(gap))
            back = fall * cross_t
            at = slice(k * rows, (k + 1) * rows)
            fall_out[at] = fall
            back_out[at] = back
            ahead_out[:, at] = (fall * cross).astype(BF16)
            backs.append(back.astype(BF16))
        own_out[:, block] = dot(jnp.concatenate(backs, axis=1), grad_d)


def state_kernel(slots, scale, query, write, read, partner, *refs):
    mixed_in, step_in, in_in, out_in, own_in, fall_in, split_in, skip_in = refs[:8]
    refs = refs[8:]
    far, (pack, *messages) = refs[: slots - 1], refs[slots - 1 : 2 * slots - 1]
    refs = refs[2 * slots - 1 :]
    kept, sent, scores_out, keys_out, scaled_out, base_out, products_out = refs
    here = lax.axis_index("seq")
    parity = lax.axis_index("tp") % 2
    rows, wide = query.shape[1:]
    heads = fall_in.shape[0] // rows
    channels = wide // heads
    states, head_dim = write.shape[2], pack.shape[0]
    half, pair, count = head_dim // 2, 2 * channels, wide // head_dim
    key_parts, value_parts = [], []
    for slot in range(slots):
        near = messages[slot - 1][wide : wide + head_dim] if slot else pack[...]
        paired = far[slot - 1][...] if slot else partner[...]
        first = jnp.where(parity == 0, near, paired)
        second = jnp.where(parity == 0, paired, near)
        key_parts.append(jnp.concatenate([first[:half], second[:half]], axis=0))
        value_parts.append(jnp.concatenate([first[half:], second[half:]], axis=0))
    keys, values = jnp.concatenate(key_parts, axis=1), jnp.concatenate(value_parts, axis=1)
    keys_out[...] = keys

    grad_mixed, step_w, decay_in, decay_out = mixed_in[...], step_in[...], in_in[...], out_in[...]
    skip_w = skip_in[:1]
    read_b, write_b = read[0], write[0]
    tails = [m[wide + 2 * rows :].astype(F32) for m in messages]
    exit_t = jnp.zeros((states, wide), F32)
    early, to_ends = [], []
    for slot in range(1, slots):
        block = jnp.bitwise_xor(here, slot)
        early.append(block < here)
        between = jnp.ones((heads, rows), F32)
        for third in range(1, slots):
            if third != slot:
                at = jnp.bitwise_xor(here, third)
                inside = jnp.logical_and(
                    at > jnp.minimum(block, here), at < jnp.maximum(block, here)
                )
                between = between * jnp.where(inside, tails[third - 1][heads:], 1.0)
        later = unstack(messages[slot - 1][:wide], rows).astype(F32)
        if slots > 2:
            later = later * widen(between, channels)
        exit_t = exit_t + jnp.where(early[-1], 0.0, later)
        to_ends.append(widen(tails[slot - 1][:heads] * between, channels))
    exit_b = exit_t.astype(BF16)
    from_exit = decay_out * dot(write_b, exit_b)
    grad_scaled = own_in[...] + from_exit
    grad_inner = step_w * grad_scaled + skip_w * grad_mixed
    grads = stack(grad_inner, head_dim)
    grads_b = grads.astype(BF16)

    queries = stack(query[0], head_dim)
    jobs = [(queries, keys, values, slot_mask(here, 0, range(slots), rows))]
    for slot in range(1, slots):
        whole = slots > 2
        mask = slot_mask(here, slot, range(slots) if whole else [slot], rows)
        some = (keys, values) if whole else (key_parts[slot], value_parts[slot])
        jobs.append((messages[slot - 1][:wide], *some, mask))
    (attn, weights, share), *before = attend(jobs, scale)
    grad_probs = dot(grads_b, values)
    inner = unstack(attn, rows)
    scaled = inner * step_w
    scaled_b = scaled.astype(BF16)
    scaled_out[...] = scaled_b
    entry_t = jnp.zeros((states, wide), F32)
    for message, is_early, to_end, (attn_o, _, _) in zip(messages, early, to_ends, before):
        carried = unstack(attn_o, rows) * to_end
        end_state = dot(message[wide + rows : wide + 2 * rows], carried, TN)
        entry_t = entry_t + jnp.where(is_early, end_state, 0.0)
    entry_b = entry_t.astype(BF16)
    from_entry = decay_in * dot(read_b, entry_b)
    base_out[...] = from_entry + skip_w * inner

    product = grads * attn
    ones = jnp.ones((2 * head_dim, head_dim), BF16)
    delta = dot(jnp.concatenate(parts_of(product, 2), axis=1), ones)
    probs = weights * jnp.concatenate([share] * slots, axis=1)
    grad_scores = (probs * (grad_probs - jnp.concatenate([delta] * slots, axis=1))).astype(BF16)
    scores_out[...] = grad_scores
    key_t = (dot(queries, grad_scores, TN) * scale).astype(BF16)
    value_t = dot(grads_b, probs, TN).astype(BF16)
    for slot in range(slots):
        block = slice(slot * rows, (slot + 1) * rows)
        first = jnp.concatenate([key_t[:half, block], value_t[:half, block]], axis=0)
        second = jnp.concatenate([key_t[half:, block], value_t[half:, block]], axis=0)
        kept[slot] = jnp.where(parity == 0, first, second)
        sent[slot * head_dim : (slot + 1) * head_dim] = jnp.where(parity == 0, second, first)

    upper = iota((rows, rows), 0) <= iota((rows, rows), 1)
    grad_cross_t = jnp.zeros((rows, rows), F32)
    for m in range(0, heads, 2):
        outer = dot(
            scaled_b[:, m * channels : (m + 2) * channels], split_in[m * rows : (m + 2) * rows], NT
        )
        grad_cross_t = grad_cross_t + outer[:, :rows] * fall_in[m * rows : (m + 1) * rows]
        grad_cross_t = grad_cross_t + outer[:, rows:] * fall_in[(m + 1) * rows : (m + 2) * rows]
    grad_cross_t = jnp.where(upper, grad_cross_t, 0.0)
    grad_write = dot(grad_cross_t, read_b) + dot(scaled * decay_out, exit_b, NT)
    grad_read = dot(grad_cross_t, write_b, TN) + dot(grad_mixed * decay_in, entry_b, NT)
    sent[slots * head_dim : slots * head_dim + rows] = grad_write.astype(BF16)
    sent[slots * head_dim + rows :] = grad_read.astype(BF16)
    products = (inner * grad_scaled, inner * from_exit, grad_mixed * from_entry)
    for i, product in enumerate(products):
        products_out[i * rows : (i + 1) * rows] = product.astype(BF16)
    totals = [
        jnp.sum(grad_mixed * inner, axis=0, keepdims=True),
        jnp.sum(exit_t * entry_t, axis=0, keepdims=True),
    ]
    totals = jnp.concatenate(totals + [jnp.zeros((6, wide), F32)], axis=0)
    products_out[len(products) * rows :] = jnp.concatenate(parts_of(totals, 2), axis=0)


def rates_kernel(products, scaled, halves, back, tables, grad_raw, params):
    heads, rows = grad_raw.shape[1:]
    wide = products.shape[1]
    channels = wide // heads
    step, rate, cum, grow, slope = [tables[i * heads : (i + 1) * heads] for i in range(5)]
    strict = iota((rows, rows), 0) < iota((rows, rows), 1)
    lower = iota((rows, rows), 0) >= iota((rows, rows), 1)
    terms = []
    for m in range(0, heads, 2):
        outer = dot(
            scaled[:, m * channels : (m + 2) * channels], halves[m * rows : (m + 2) * rows], NT
        )
        terms.append((outer[:, :rows] * back[m * rows : (m + 1) * rows]).astype(BF16))
        terms.append((outer[:, rows:] * back[(m + 1) * rows : (m + 2) * rows]).astype(BF16))
    later = dot(jnp.concatenate(terms, axis=0), jnp.where(lower, 1.0, 0.0))
    rate_rows = [
        jnp.sum(jnp.where(strict, later[m * rows : (m + 1) * rows], 0.0), axis=0, keepdims=True)
        for m in range(heads)
    ]
    pick = (over(iota((heads, wide), 1), channels) == iota((heads, wide), 0)).astype(BF16)
    sums = dot(pick, products[...], NT)
    grad_step = sums[:, :rows]
    exit_sum = sums[:, rows : 2 * rows] * step
    entry_sum = sums[:, 2 * rows : 3 * rows]
    totals = sums[:, 3 * rows : 3 * rows + 8] + sums[:, 3 * rows + 8 :]
    skip_sum = jnp.where(iota((heads, rows), 1) == 0, totals[:, :1], 0.0)
    carry_sum = totals[:, 1:2] * jnp.exp(-cum[:, rows - 1 :])
    grad_rate = -(
        jnp.concatenate(rate_rows, axis=0)
        + dot_flags([entry_sum, exit_sum], flag_rows(lower, strict))
        + carry_sum
    )
    grad_shift = (grad_step + grad_rate * grow) * slope
    grad_raw[0] = grad_shift
    terms = jnp.concatenate([grad_rate * rate, skip_sum, grad_shift], axis=0)
    summed = jnp.concatenate(parts_of(terms, 3), axis=1)
    params[:, : 3 * heads] = dot(jnp.ones((8, 3 * rows), F32), summed, NT)
    params[:, 3 * heads :] = jnp.zeros((8, params.shape[1] - 3 * heads), F32)


def output_kernel(scale, ahead, scaled, base, slope, scores, keys, grad_gate, grad_query):
    rows, wide = base.shape
    channels = wide * rows // ahead.shape[1]
    pair = 2 * channels
    low = iota((rows, pair), 1) < channels
    for at in range(0, wide, pair):
        block = slice(at, at + pair)
        scaled_p = scaled[:, block].astype(F32)
        scaled_d = jnp.concatenate(
            [jnp.where(low, scaled_p, 0.0), jnp.where(low, 0.0, scaled_p)], axis=0
        )
        m = at // channels
        mixed = dot(ahead[:, m * rows : (m + 2) * rows], scaled_d) + base[:, block]
        grad_gate[0, :, block] = mixed * slope[:, block]
    grad_query[0] = unstack(dot(scores[...], keys[...], NT) * scale, rows)


def vectors_kernel(mine, other, grad_write, grad_read):
    rows = grad_write.shape[1]
    both = mine[...].astype(F32) + other[...].astype(F32)
    grad_write[0] = both[:rows]
    grad_read[0] = both[rows:]


def finish_kernel(count, *refs):
    arrived, (mine, other, tail) = refs[:count], refs[count : count + 3]
    grad_key, grad_value, grad_alog, grad_skip, grad_bias = refs[count + 3 :]
    half, rows = grad_key.shape[1:]
    total = mine[0].astype(F32) + other[: 2 * half].astype(F32)
    for term in arrived:
        total = total + term[: 2 * half].astype(F32)
    grad_key[0] = total[:half]
    grad_value[0] = total[half:]
    heads = grad_alog.shape[0]
    params = joined(tail[...]) + joined(arrived[-1][2 * half :])
    grad_alog[...] = params[0, :heads]
    grad_skip[...] = params[0, heads : 2 * heads]
    grad_bias[...] = params[0, 2 * heads : 3 * heads]


def split(sums):
    high = lax.reduce_precision(sums, 8, 7)
    return jnp.concatenate([high.astype(BF16), (sums - high).astype(BF16)], axis=0)


def joined(tail):
    tail = tail.astype(F32)
    count = tail.shape[0] // 2
    return tail[:count] + tail[count:]


def flip(axis, distance):
    return [(i, i ^ distance) for i in range(lax.axis_size(axis))]


def shape(dims, dtype):
    return jax.ShapeDtypeStruct(tuple(dims), dtype)


VMEM = pl.BlockSpec(memory_space=pltpu.VMEM)
SMEM = pl.BlockSpec(memory_space=pltpu.SMEM)
HBM = pl.BlockSpec(memory_space=pltpu.HBM)
PARAMS = pltpu.CompilerParams(vmem_limit_bytes=48 * 1024 * 1024)


def call(kernel, outs, args, specs=None):
    return pl.pallas_call(
        kernel,
        out_shape=outs,
        in_specs=[(specs or {}).get(i, VMEM) for i in range(len(args))],
        out_specs=jax.tree.map(lambda _: VMEM, outs),
        compiler_params=PARAMS,
        cost_estimate=pl.CostEstimate(flops=0, bytes_accessed=0, transcendentals=0),
    )(*args)


def swap(array, seq_bits, tp_bits):
    n_seq, n_tp = lax.axis_size("seq"), lax.axis_size("tp")
    pairs = [
        (s * n_tp + t, (s ^ seq_bits) * n_tp + (t ^ tp_bits))
        for s in range(n_seq)
        for t in range(n_tp)
    ]
    return lax.ppermute(array, ("seq", "tp"), pairs)


def body(
    query_rows,
    key_rows,
    value_rows,
    gate_rows,
    write_vec,
    read_vec,
    dt_raw,
    a_log,
    skip_gain,
    dt_bias,
    out_grad,
):
    slots = lax.axis_size("seq")
    rows, wide = query_rows.shape[1:]
    head_dim = 2 * key_rows.shape[2]
    states = write_vec.shape[2]
    heads = a_log.shape[0]
    scale = head_dim ** (-0.5)

    bits = slots.bit_length() - 1
    key_t, value_t = key_rows.swapaxes(1, 2), value_rows.swapaxes(1, 2)
    kept_here = (dt_raw, gate_rows, out_grad, read_vec, query_rows, write_vec)
    sources = kept_here + (a_log, dt_bias, key_t, value_t)
    pack, message, dt_raw, gate_rows, out_grad, read_vec, query_rows, write_vec = pl.pallas_call(
        share_kernel,
        out_shape=(
            shape((head_dim, rows), BF16),
            shape((bits, wide + 2 * rows + 2 * heads, head_dim), BF16),
        )
        + tuple(shape(a.shape, a.dtype) for a in kept_here),
        in_specs=[HBM] * len(sources),
        out_specs=(VMEM,) * (2 + len(kept_here)),
        scratch_shapes=[
            pltpu.VMEM(a.shape, a.dtype) for a in sources[len(kept_here) :]
        ]
        + [pltpu.SemaphoreType.DMA((len(sources),))],
        compiler_params=PARAMS,
    )(*[pltpu.with_memory_space_constraint(a, pltpu.HBM) for a in sources])
    messages = [swap(message[slot.bit_length() - 1], slot, 0) for slot in range(1, slots)]
    partner = swap(pack, 0, 1)
    far = [swap(pack, slot, 1) for slot in range(1, slots)]

    wide_f, wide_b = shape((rows, wide), F32), shape((rows, wide), BF16)
    tall_f = shape((heads * rows, rows), F32)
    prepared = call(
        prepare_kernel,
        (wide_f,) * 6
        + (tall_f, tall_f)
        + (shape((rows, heads * rows), BF16), shape((heads * rows, 2 * wide // heads), BF16))
        + (shape((5 * heads, rows), F32), shape((8, wide), F32)),
        (gate_rows, out_grad, write_vec, read_vec, dt_raw, a_log, skip_gain, dt_bias),
        {5: SMEM, 6: SMEM, 7: SMEM},
    )
    grad_mixed, slope, step_w, decay_in, decay_out, own, fall, back = prepared[:8]
    ahead, halves, tables, skip_w = prepared[8:]
    mine, other, scores, keys, scaled, base, products = call(
        lambda *refs: state_kernel(slots, scale, *refs),
        (
            shape((slots, head_dim, rows), BF16),
            shape((slots * head_dim + 2 * rows, states), BF16),
            shape((wide // head_dim * rows, slots * rows), BF16),
            shape((head_dim, slots * rows), BF16),
            wide_b,
            wide_f,
            shape((3 * rows + 16, wide), BF16),
        ),
        (
            query_rows,
            write_vec,
            read_vec,
            partner,
            grad_mixed,
            step_w,
            decay_in,
            decay_out,
            own,
            fall,
            halves,
            skip_w,
            *far,
            pack,
            *messages,
        ),
    )
    got = swap(other, 0, 1)
    grad_dt, params = call(
        rates_kernel,
        (shape((1, heads, rows), F32), shape((8, states), F32)),
        (products, scaled, halves, back, tables),
    )
    shared, got_shared = other[slots * head_dim :], got[slots * head_dim :]
    reach = 2
    while reach < lax.axis_size("tp"):
        shared = (shared.astype(F32) + got_shared.astype(F32)).astype(BF16)
        got_shared = swap(shared, 0, reach)
        reach *= 2
    reach = 1
    while reach < lax.axis_size("dp"):
        near = [params] + [lax.ppermute(params, "dp", flip("dp", k * reach)) for k in (1, 2, 3)]
        shared, *near = lax.optimization_barrier((shared, *near))
        params = (near[0] + near[1]) + (near[2] + near[3])
        reach *= 4
    sent = [
        (mine[slot].astype(F32) + got[slot * head_dim : (slot + 1) * head_dim].astype(F32)).astype(BF16)
        for slot in range(1, slots)
    ]
    arrived = [swap(sent[slot - 1], slot, 0) for slot in range(1, slots) if slot & (slot - 1)]
    slot = 1
    while slot < slots:
        tail = split(params)
        arrived.append(swap(jnp.concatenate([sent[slot - 1], tail], axis=0), slot, 0))
        slot *= 2
        if slot < slots:
            params = joined(tail) + joined(arrived[-1][head_dim:])
    scores, shared = lax.optimization_barrier((scores, shared))
    grad_gate, grad_query = call(
        lambda *refs: output_kernel(scale, *refs),
        (shape((1, rows, wide), F32), shape((1, rows, wide), F32)),
        (ahead, scaled, base, slope, scores, keys),
    )
    vector = shape((heads,), F32)
    half = shape((1, head_dim // 2, rows), F32)
    full = shape((1, rows, states), F32)
    grad_write, grad_read = call(vectors_kernel, (full, full), (shared, got_shared))
    grad_write, *arrived = lax.optimization_barrier((grad_write, *arrived))
    grad_key, grad_value, grad_alog, grad_skip, grad_bias = call(
        lambda *refs: finish_kernel(len(arrived), *refs),
        (half, half, vector, vector, vector),
        (*arrived, mine, got, tail),
    )
    grad_key, grad_value = grad_key.swapaxes(1, 2), grad_value.swapaxes(1, 2)
    return (
        grad_query,
        grad_key,
        grad_value,
        grad_gate,
        grad_write,
        grad_read,
        grad_dt,
        grad_alog,
        grad_skip,
        grad_bias,
    )


def solution(mesh):
    in_specs = (
        P("dp", "seq", "tp"),
        P("dp", "seq", "tp"),
        P("dp", "seq", "tp"),
        P("dp", "seq", "tp"),
        P("dp", "seq", None),
        P("dp", "seq", None),
        P("dp", "tp", "seq"),
        P("tp"),
        P("tp"),
        P("tp"),
        P("dp", "seq", "tp"),
    )
    out_specs = (
        P("dp", "seq", "tp"),
        P("dp", "seq", "tp"),
        P("dp", "seq", "tp"),
        P("dp", "seq", "tp"),
        P("dp", "seq", None),
        P("dp", "seq", None),
        P("dp", "tp", "seq"),
        P("tp"),
        P("tp"),
        P("tp"),
    )
    return jax.shard_map(body, mesh=mesh, in_specs=in_specs, out_specs=out_specs, check_vma=False)
```

```python
import jax
import jax.numpy as jnp
from jax import lax
from jax.experimental import pallas as pl
from jax.experimental.pallas import tpu as pltpu
from jax.sharding import PartitionSpec as P

NEG_FILL = -1e30
LOG2E = 1.4426950408889634
F32 = jnp.float32
BF16 = jnp.bfloat16
NN = (((1,), (0,)), ((), ()))
NT = (((1,), (1,)), ((), ()))
TN = (((0,), (0,)), ((), ()))


def dot(a, b, dims=NN):
    return lax.dot_general(a.astype(BF16), b.astype(BF16), dims, preferred_element_type=F32)


def parts_of(array, count):
    parts = []
    for _ in range(count):
        parts.append(array.astype(BF16))
        array = array - parts[-1].astype(F32)
    return parts


PARTS = 3


def flag_rows(*flags, count=PARTS):
    return jnp.concatenate([jnp.where(f, 1.0, 0.0).astype(BF16) for f in flags] * count, axis=0)


def dot_flags(arrays, rows, count=PARTS):
    split_up = [parts_of(a, count) for a in arrays]
    left = [parts[i] for i in range(count) for parts in split_up]
    return dot(jnp.concatenate(left, axis=1), rows)


def over(index, size):
    if size & (size - 1):
        return index // size
    return lax.shift_right_logical(index, size.bit_length() - 1)


def upto_rows(rows, count=PARTS):
    return flag_rows(iota((rows, rows), 0) <= iota((rows, rows), 1), count=count)


def head_rows(heads, channels, count=PARTS):
    shape = (heads, heads * channels)
    one = jnp.where(over(iota(shape, 1), channels) == iota(shape, 0), 1.0, 0.0)
    return jnp.concatenate([one.astype(BF16)] * count, axis=0)


def iota(shape, axis):
    return lax.broadcasted_iota(jnp.int32, shape, axis)


def column(ref, width):
    heads = ref.shape[0]
    at = iota((heads, width), 0)
    out = jnp.full((heads, width), ref[0], F32)
    for m in range(1, heads):
        out = jnp.where(at == m, ref[m], out)
    return out


def upright(vector, width):
    heads = vector.shape[0]
    square = jnp.broadcast_to(vector[...].reshape(1, heads), (heads, heads))
    square = jnp.where(iota((heads, heads), 0) == iota((heads, heads), 1), square, 0.0)
    return jnp.broadcast_to(jnp.sum(square, axis=1, keepdims=True), (heads, width))


def rates(raw, bias, alog, upto, count=PARTS):
    shifted = raw + bias
    small = jnp.exp(-jnp.abs(shifted))
    log_one = jnp.log1p(small) if count == PARTS else jnp.log(1.0 + small)
    step = jnp.maximum(shifted, 0.0) + log_one
    rate = step * jnp.exp(alog)
    return step, rate, dot_flags([rate], upto, count)


def spread(cols, m, width):
    return jnp.broadcast_to(cols[:, m : m + 1], (cols.shape[0], width))


def widen(factors, channels, picked=None, count=PARTS):
    if picked is None:
        picked = head_rows(factors.shape[0], channels)
    return dot(jnp.concatenate(parts_of(factors, count), axis=0), picked, TN)


def stack(wide, width):
    return jnp.concatenate([wide[:, i : i + width] for i in range(0, wide.shape[1], width)], axis=0)


def unstack(tall, rows):
    return jnp.concatenate([tall[i : i + rows] for i in range(0, tall.shape[0], rows)], axis=1)


def attend(jobs, scale):
    shapes = [(q.shape[0] // m.shape[0],) + m.shape for q, _, _, m in jobs]
    scores = [
        jnp.where(m[None], (dot(q, k) * (scale * LOG2E)).reshape(dims), NEG_FILL)
        for (q, k, _, m), dims in zip(jobs, shapes)
    ]
    tops = [jnp.max(s, axis=2, keepdims=True) for s in scores]
    weights = [
        jnp.exp2(s - top).reshape(dims[0] * dims[1], dims[2])
        for s, top, dims in zip(scores, tops, shapes)
    ]
    both = [
        dot(w, jnp.concatenate([v, jnp.ones_like(v)], axis=0), NT)
        for w, (_, _, v, _) in zip(weights, jobs)
    ]
    width = jobs[0][2].shape[0]
    shares = [1.0 / b[:, width:] for b in both]
    return [(b[:, :width] * share, w, share) for b, w, share in zip(both, weights, shares)]


def slot_mask(here, query_slot, slots, rows):
    masks = []
    for slot in slots:
        if slot == query_slot:
            masks.append(iota((rows, rows), 0) >= iota((rows, rows), 1))
        else:
            seen = jnp.bitwise_xor(here, slot) < jnp.bitwise_xor(here, query_slot)
            masks.append(jnp.broadcast_to(seen, (rows, rows)))
    return jnp.concatenate(masks, axis=1)


def share_kernel(*refs):
    sources, (pack, message), held, arrived = refs[:10], refs[10:12], refs[12:22], refs[22]
    raw, gate, cotangent, read, query, write, alog, bias, key, value = held
    copies = [
        pltpu.make_async_copy(source, here, arrived.at[i])
        for i, (source, here) in enumerate(zip(sources, held))
    ]
    for place in (0, 6, 7, 1, 2, 3, 4, 8, 9, 5):
        copies[place].start()
    here = lax.axis_index("seq")
    heads, rows = raw.shape[1:]
    wide, states = gate.shape[2], read.shape[2]
    half = key.shape[1]
    upto, picked = upto_rows(rows, 2), head_rows(heads, wide // heads, 2)
    for place in (0, 6, 7):
        copies[place].wait()
    step, _, cum = rates(raw[0], upright(bias, rows), upright(alog, rows), upto, 2)
    decay = widen(jnp.exp(-cum), wide // heads, picked, 2)
    to_end = jnp.exp(cum - cum[:, rows - 1 :]) * step
    whole = jnp.broadcast_to(jnp.exp(-cum[:, rows - 1 :]), (heads, rows))
    tail = jnp.concatenate([to_end, whole], axis=0).astype(BF16)
    for place in (1, 2, 3):
        copies[place].wait()
    gate_f = gate[0].astype(F32)
    grad_mixed = cotangent[0].astype(F32) * gate_f * jax.nn.sigmoid(gate_f)
    entry = dot(read[0], grad_mixed * decay, TN).astype(BF16)
    for place in (4, 5, 8, 9):
        copies[place].wait()
    pack[:half] = key[0]
    pack[half:] = value[0]
    for bit in range(message.shape[0]):
        is_early = jnp.bitwise_and(lax.shift_right_logical(here, bit), 1) == 0
        for at in range(0, wide, states):
            message[bit, at : at + rows] = jnp.where(
                is_early, query[0, :, at : at + states], entry[:, at : at + states]
            )
        message[bit, wide : wide + half] = key[0]
        message[bit, wide + half : wide + 2 * half] = value[0]
        message[bit, wide + rows : wide + 2 * rows] = write[0]
        message[bit, wide + 2 * rows :] = tail


def prepare_kernel(gate, cotangent, write, read, raw, alog, skip, bias, *outs):
    mixed_out, slope_out, step_out, in_out, out_out, own_out, fall_out, back_out = outs[:8]
    ahead_out, split_out, rates_out, skip_out = outs[8:]
    heads, rows = raw.shape[1:]
    wide = gate.shape[2]
    channels = wide // heads
    pair = 2 * channels
    alog_c, bias_c = column(alog, rows), column(bias, rows)
    step, rate, cum = rates(raw[0], bias_c, alog_c, upto_rows(rows))
    for i, table in enumerate((step, rate, cum, jnp.exp(alog_c), jax.nn.sigmoid(raw[0] + bias_c))):
        rates_out[i * heads : (i + 1) * heads] = table
    head_of = over(iota(skip_out.shape, 1), channels)
    skip_w = jnp.full(skip_out.shape, skip[0], F32)
    for m in range(1, heads):
        skip_w = jnp.where(head_of == m, skip[m], skip_w)
    skip_out[...] = skip_w
    gate_f = gate[0].astype(F32)
    sig = jax.nn.sigmoid(gate_f)
    cot = cotangent[0].astype(F32)
    grad_mixed = cot * gate_f * sig
    mixed_out[...] = grad_mixed
    slope_out[...] = cot * sig * (1.0 + gate_f * (1.0 - sig))
    cum_cols = cum.T
    step_out[...] = widen(step, channels)
    in_out[...] = widen(jnp.exp(-cum), channels)
    out_out[...] = widen(jnp.exp(cum - cum[:, rows - 1 :]), channels)
    read_b, write_b = read[0], write[0]
    upper = iota((rows, rows), 0) <= iota((rows, rows), 1)
    lower = iota((rows, rows), 0) >= iota((rows, rows), 1)
    cross = jnp.where(lower, dot(read_b, write_b, NT), 0.0)
    cross_t = jnp.where(upper, dot(write_b, read_b, NT), 0.0)
    low = iota((rows, pair), 1) < channels
    for m in range(0, heads, 2):
        block = slice(m * channels, (m + 2) * channels)
        grad_p = grad_mixed[:, block]
        grad_d = jnp.concatenate(
            [jnp.where(low, grad_p, 0.0), jnp.where(low, 0.0, grad_p)], axis=0
        ).astype(BF16)
        split_out[m * rows : (m + 2) * rows] = grad_d
        backs = []
        for k in range(m, m + 2):
            gap = spread(cum_cols, k, rows) - cum[k : k + 1, :]
            fall = jnp.exp(-jnp.abs(gap))
            back = fall * cross_t
            at = slice(k * rows, (k + 1) * rows)
            fall_out[at] = fall
            back_out[at] = back
            ahead_out[:, at] = (fall * cross).astype(BF16)
            backs.append(back.astype(BF16))
        own_out[:, block] = dot(jnp.concatenate(backs, axis=1), grad_d)


def state_kernel(slots, scale, query, write, read, partner, *refs):
    mixed_in, step_in, in_in, out_in, own_in, fall_in, split_in, skip_in = refs[:8]
    refs = refs[8:]
    far, (pack, *messages) = refs[: slots - 1], refs[slots - 1 : 2 * slots - 1]
    refs = refs[2 * slots - 1 :]
    kept, sent, scores_out, keys_out, scaled_out, base_out, products_out = refs
    here = lax.axis_index("seq")
    parity = lax.axis_index("tp") % 2
    rows, wide = query.shape[1:]
    heads = fall_in.shape[0] // rows
    channels = wide // heads
    states, head_dim = write.shape[2], pack.shape[0]
    half, pair, count = head_dim // 2, 2 * channels, wide // head_dim
    key_parts, value_parts = [], []
    for slot in range(slots):
        near = messages[slot - 1][wide : wide + head_dim] if slot else pack[...]
        paired = far[slot - 1][...] if slot else partner[...]
        first = jnp.where(parity == 0, near, paired)
        second = jnp.where(parity == 0, paired, near)
        key_parts.append(jnp.concatenate([first[:half], second[:half]], axis=0))
        value_parts.append(jnp.concatenate([first[half:], second[half:]], axis=0))
    keys, values = jnp.concatenate(key_parts, axis=1), jnp.concatenate(value_parts, axis=1)
    keys_out[...] = keys

    grad_mixed, step_w, decay_in, decay_out = mixed_in[...], step_in[...], in_in[...], out_in[...]
    skip_w = skip_in[:1]
    read_b, write_b = read[0], write[0]
    tails = [m[wide + 2 * rows :].astype(F32) for m in messages]
    exit_t = jnp.zeros((states, wide), F32)
    early, to_ends = [], []
    for slot in range(1, slots):
        block = jnp.bitwise_xor(here, slot)
        early.append(block < here)
        between = jnp.ones((heads, rows), F32)
        for third in range(1, slots):
            if third != slot:
                at = jnp.bitwise_xor(here, third)
                inside = jnp.logical_and(
                    at > jnp.minimum(block, here), at < jnp.maximum(block, here)
                )
                between = between * jnp.where(inside, tails[third - 1][heads:], 1.0)
        later = unstack(messages[slot - 1][:wide], rows).astype(F32)
        if slots > 2:
            later = later * widen(between, channels)
        exit_t = exit_t + jnp.where(early[-1], 0.0, later)
        to_ends.append(widen(tails[slot - 1][:heads] * between, channels))
    exit_b = exit_t.astype(BF16)
    from_exit = decay_out * dot(write_b, exit_b)
    grad_scaled = own_in[...] + from_exit
    grad_inner = step_w * grad_scaled + skip_w * grad_mixed
    grads = stack(grad_inner, head_dim)
    grads_b = grads.astype(BF16)

    queries = stack(query[0], head_dim)
    jobs = [(queries, keys, values, slot_mask(here, 0, range(slots), rows))]
    for slot in range(1, slots):
        whole = slots > 2
        mask = slot_mask(here, slot, range(slots) if whole else [slot], rows)
        some = (keys, values) if whole else (key_parts[slot], value_parts[slot])
        jobs.append((messages[slot - 1][:wide], *some, mask))
    (attn, weights, share), *before = attend(jobs, scale)
    grad_probs = dot(grads_b, values)
    inner = unstack(attn, rows)
    scaled = inner * step_w
    scaled_b = scaled.astype(BF16)
    scaled_out[...] = scaled_b
    entry_t = jnp.zeros((states, wide), F32)
    for message, is_early, to_end, (attn_o, _, _) in zip(messages, early, to_ends, before):
        carried = unstack(attn_o, rows) * to_end
        end_state = dot(message[wide + rows : wide + 2 * rows], carried, TN)
        entry_t = entry_t + jnp.where(is_early, end_state, 0.0)
    entry_b = entry_t.astype(BF16)
    from_entry = decay_in * dot(read_b, entry_b)
    base_out[...] = from_entry + skip_w * inner

    product = grads * attn
    ones = jnp.ones((2 * head_dim, head_dim), BF16)
    delta = dot(jnp.concatenate(parts_of(product, 2), axis=1), ones)
    probs = weights * jnp.concatenate([share] * slots, axis=1)
    grad_scores = (probs * (grad_probs - jnp.concatenate([delta] * slots, axis=1))).astype(BF16)
    scores_out[...] = grad_scores
    key_t = (dot(queries, grad_scores, TN) * scale).astype(BF16)
    value_t = dot(grads_b, probs, TN).astype(BF16)
    for slot in range(slots):
        block = slice(slot * rows, (slot + 1) * rows)
        first = jnp.concatenate([key_t[:half, block], value_t[:half, block]], axis=0)
        second = jnp.concatenate([key_t[half:, block], value_t[half:, block]], axis=0)
        kept[slot] = jnp.where(parity == 0, first, second)
        sent[slot * head_dim : (slot + 1) * head_dim] = jnp.where(parity == 0, second, first)

    upper = iota((rows, rows), 0) <= iota((rows, rows), 1)
    grad_cross_t = jnp.zeros((rows, rows), F32)
    for m in range(0, heads, 2):
        outer = dot(
            scaled_b[:, m * channels : (m + 2) * channels], split_in[m * rows : (m + 2) * rows], NT
        )
        grad_cross_t = grad_cross_t + outer[:, :rows] * fall_in[m * rows : (m + 1) * rows]
        grad_cross_t = grad_cross_t + outer[:, rows:] * fall_in[(m + 1) * rows : (m + 2) * rows]
    grad_cross_t = jnp.where(upper, grad_cross_t, 0.0)
    grad_write = dot(grad_cross_t, read_b) + dot(scaled * decay_out, exit_b, NT)
    grad_read = dot(grad_cross_t, write_b, TN) + dot(grad_mixed * decay_in, entry_b, NT)
    sent[slots * head_dim : slots * head_dim + rows] = grad_write.astype(BF16)
    sent[slots * head_dim + rows :] = grad_read.astype(BF16)
    products = (inner * grad_scaled, inner * from_exit, grad_mixed * from_entry)
    for i, product in enumerate(products):
        products_out[i * rows : (i + 1) * rows] = product.astype(BF16)
    totals = [
        jnp.sum(grad_mixed * inner, axis=0, keepdims=True),
        jnp.sum(exit_t * entry_t, axis=0, keepdims=True),
    ]
    totals = jnp.concatenate(totals + [jnp.zeros((6, wide), F32)], axis=0)
    products_out[len(products) * rows :] = jnp.concatenate(parts_of(totals, 2), axis=0)


def rates_kernel(products, scaled, halves, back, tables, grad_raw, params):
    heads, rows = grad_raw.shape[1:]
    wide = products.shape[1]
    channels = wide // heads
    step, rate, cum, grow, slope = [tables[i * heads : (i + 1) * heads] for i in range(5)]
    strict = iota((rows, rows), 0) < iota((rows, rows), 1)
    lower = iota((rows, rows), 0) >= iota((rows, rows), 1)
    terms = []
    for m in range(0, heads, 2):
        outer = dot(
            scaled[:, m * channels : (m + 2) * channels], halves[m * rows : (m + 2) * rows], NT
        )
        terms.append((outer[:, :rows] * back[m * rows : (m + 1) * rows]).astype(BF16))
        terms.append((outer[:, rows:] * back[(m + 1) * rows : (m + 2) * rows]).astype(BF16))
    later = dot(jnp.concatenate(terms, axis=0), jnp.where(lower, 1.0, 0.0))
    rate_rows = [
        jnp.sum(jnp.where(strict, later[m * rows : (m + 1) * rows], 0.0), axis=0, keepdims=True)
        for m in range(heads)
    ]
    pick = (over(iota((heads, wide), 1), channels) == iota((heads, wide), 0)).astype(BF16)
    sums = dot(pick, products[...], NT)
    grad_step = sums[:, :rows]
    exit_sum = sums[:, rows : 2 * rows] * step
    entry_sum = sums[:, 2 * rows : 3 * rows]
    totals = sums[:, 3 * rows : 3 * rows + 8] + sums[:, 3 * rows + 8 :]
    skip_sum = jnp.where(iota((heads, rows), 1) == 0, totals[:, :1], 0.0)
    carry_sum = totals[:, 1:2] * jnp.exp(-cum[:, rows - 1 :])
    grad_rate = -(
        jnp.concatenate(rate_rows, axis=0)
        + dot_flags([entry_sum, exit_sum], flag_rows(lower, strict))
        + carry_sum
    )
    grad_shift = (grad_step + grad_rate * grow) * slope
    grad_raw[0] = grad_shift
    terms = jnp.concatenate([grad_rate * rate, skip_sum, grad_shift], axis=0)
    summed = jnp.concatenate(parts_of(terms, 3), axis=1)
    params[:, : 3 * heads] = dot(jnp.ones((8, 3 * rows), F32), summed, NT)
    params[:, 3 * heads :] = jnp.zeros((8, params.shape[1] - 3 * heads), F32)


def output_kernel(scale, ahead, scaled, base, slope, scores, keys, grad_gate, grad_query):
    rows, wide = base.shape
    channels = wide * rows // ahead.shape[1]
    pair = 2 * channels
    low = iota((rows, pair), 1) < channels
    for at in range(0, wide, pair):
        block = slice(at, at + pair)
        scaled_p = scaled[:, block].astype(F32)
        scaled_d = jnp.concatenate(
            [jnp.where(low, scaled_p, 0.0), jnp.where(low, 0.0, scaled_p)], axis=0
        )
        m = at // channels
        mixed = dot(ahead[:, m * rows : (m + 2) * rows], scaled_d) + base[:, block]
        grad_gate[0, :, block] = mixed * slope[:, block]
    grad_query[0] = unstack(dot(scores[...], keys[...], NT) * scale, rows)


def vectors_kernel(mine, other, grad_write, grad_read):
    rows = grad_write.shape[1]
    both = mine[...].astype(F32) + other[...].astype(F32)
    grad_write[0] = both[:rows]
    grad_read[0] = both[rows:]


def finish_kernel(count, *refs):
    arrived, (mine, other, tail) = refs[:count], refs[count : count + 3]
    grad_key, grad_value, grad_alog, grad_skip, grad_bias = refs[count + 3 :]
    half, rows = grad_key.shape[1:]
    total = mine[0].astype(F32) + other[: 2 * half].astype(F32)
    for term in arrived:
        total = total + term[: 2 * half].astype(F32)
    grad_key[0] = total[:half]
    grad_value[0] = total[half:]
    heads = grad_alog.shape[0]
    params = joined(tail[...]) + joined(arrived[-1][2 * half :])
    grad_alog[...] = params[0, :heads]
    grad_skip[...] = params[0, heads : 2 * heads]
    grad_bias[...] = params[0, 2 * heads : 3 * heads]


def split(sums):
    high = lax.reduce_precision(sums, 8, 7)
    return jnp.concatenate([high.astype(BF16), (sums - high).astype(BF16)], axis=0)


def joined(tail):
    tail = tail.astype(F32)
    count = tail.shape[0] // 2
    return tail[:count] + tail[count:]


def flip(axis, distance):
    return [(i, i ^ distance) for i in range(lax.axis_size(axis))]


def shape(dims, dtype):
    return jax.ShapeDtypeStruct(tuple(dims), dtype)


VMEM = pl.BlockSpec(memory_space=pltpu.VMEM)
SMEM = pl.BlockSpec(memory_space=pltpu.SMEM)
HBM = pl.BlockSpec(memory_space=pltpu.HBM)
PARAMS = pltpu.CompilerParams(vmem_limit_bytes=48 * 1024 * 1024)


def call(kernel, outs, args, specs=None):
    return pl.pallas_call(
        kernel,
        out_shape=outs,
        in_specs=[(specs or {}).get(i, VMEM) for i in range(len(args))],
        out_specs=jax.tree.map(lambda _: VMEM, outs),
        compiler_params=PARAMS,
        cost_estimate=pl.CostEstimate(flops=0, bytes_accessed=0, transcendentals=0),
    )(*args)


def swap(array, seq_bits, tp_bits):
    n_seq, n_tp = lax.axis_size("seq"), lax.axis_size("tp")
    pairs = [
        (s * n_tp + t, (s ^ seq_bits) * n_tp + (t ^ tp_bits))
        for s in range(n_seq)
        for t in range(n_tp)
    ]
    return lax.ppermute(array, ("seq", "tp"), pairs)


def body(
    query_rows,
    key_rows,
    value_rows,
    gate_rows,
    write_vec,
    read_vec,
    dt_raw,
    a_log,
    skip_gain,
    dt_bias,
    out_grad,
):
    slots = lax.axis_size("seq")
    rows, wide = query_rows.shape[1:]
    head_dim = 2 * key_rows.shape[2]
    states = write_vec.shape[2]
    heads = a_log.shape[0]
    scale = head_dim ** (-0.5)

    bits = slots.bit_length() - 1
    key_t, value_t = key_rows.swapaxes(1, 2), value_rows.swapaxes(1, 2)
    kept_here = (dt_raw, gate_rows, out_grad, read_vec, query_rows, write_vec)
    sources = kept_here + (a_log, dt_bias, key_t, value_t)
    pack, message, dt_raw, gate_rows, out_grad, read_vec, query_rows, write_vec = pl.pallas_call(
        share_kernel,
        out_shape=(
            shape((head_dim, rows), BF16),
            shape((bits, wide + 2 * rows + 2 * heads, head_dim), BF16),
        )
        + tuple(shape(a.shape, a.dtype) for a in kept_here),
        in_specs=[HBM] * len(sources),
        out_specs=(VMEM,) * (2 + len(kept_here)),
        scratch_shapes=[
            pltpu.VMEM(a.shape, a.dtype) for a in sources[len(kept_here) :]
        ]
        + [pltpu.SemaphoreType.DMA((len(sources),))],
        compiler_params=PARAMS,
    )(*[pltpu.with_memory_space_constraint(a, pltpu.HBM) for a in sources])
    messages = [swap(message[slot.bit_length() - 1], slot, 0) for slot in range(1, slots)]
    partner = swap(pack, 0, 1)
    far = [swap(pack, slot, 1) for slot in range(1, slots)]

    wide_f, wide_b = shape((rows, wide), F32), shape((rows, wide), BF16)
    tall_f = shape((heads * rows, rows), F32)
    prepared = call(
        prepare_kernel,
        (wide_f,) * 6
        + (tall_f, tall_f)
        + (shape((rows, heads * rows), BF16), shape((heads * rows, 2 * wide // heads), BF16))
        + (shape((5 * heads, rows), F32), shape((8, wide), F32)),
        (gate_rows, out_grad, write_vec, read_vec, dt_raw, a_log, skip_gain, dt_bias),
        {5: SMEM, 6: SMEM, 7: SMEM},
    )
    grad_mixed, slope, step_w, decay_in, decay_out, own, fall, back = prepared[:8]
    ahead, halves, tables, skip_w = prepared[8:]
    mine, other, scores, keys, scaled, base, products = call(
        lambda *refs: state_kernel(slots, scale, *refs),
        (
            shape((slots, head_dim, rows), BF16),
            shape((slots * head_dim + 2 * rows, states), BF16),
            shape((wide // head_dim * rows, slots * rows), BF16),
            shape((head_dim, slots * rows), BF16),
            wide_b,
            wide_f,
            shape((3 * rows + 16, wide), BF16),
        ),
        (
            query_rows,
            write_vec,
            read_vec,
            partner,
            grad_mixed,
            step_w,
            decay_in,
            decay_out,
            own,
            fall,
            halves,
            skip_w,
            *far,
            pack,
            *messages,
        ),
    )
    got = swap(other, 0, 1)
    grad_dt, params = call(
        rates_kernel,
        (shape((1, heads, rows), F32), shape((8, states), F32)),
        (products, scaled, halves, back, tables),
    )
    shared, got_shared = other[slots * head_dim :], got[slots * head_dim :]
    reach = 2
    while reach < lax.axis_size("tp"):
        shared = (shared.astype(F32) + got_shared.astype(F32)).astype(BF16)
        got_shared = swap(shared, 0, reach)
        reach *= 2
    reach = 1
    while reach < lax.axis_size("dp"):
        near = [params] + [lax.ppermute(params, "dp", flip("dp", k * reach)) for k in (1, 2, 3)]
        shared, *near = lax.optimization_barrier((shared, *near))
        params = (near[0] + near[1]) + (near[2] + near[3])
        reach *= 4
    sent = [
        (mine[slot].astype(F32) + got[slot * head_dim : (slot + 1) * head_dim].astype(F32)).astype(BF16)
        for slot in range(1, slots)
    ]
    arrived = [swap(sent[slot - 1], slot, 0) for slot in range(1, slots) if slot & (slot - 1)]
    slot = 1
    while slot < slots:
        tail = split(params)
        arrived.append(swap(jnp.concatenate([sent[slot - 1], tail], axis=0), slot, 0))
        slot *= 2
        if slot < slots:
            params = joined(tail) + joined(arrived[-1][head_dim:])
    scores, shared = lax.optimization_barrier((scores, shared))
    grad_gate, grad_query = call(
        lambda *refs: output_kernel(scale, *refs),
        (shape((1, rows, wide), F32), shape((1, rows, wide), F32)),
        (ahead, scaled, base, slope, scores, keys),
    )
    vector = shape((heads,), F32)
    half = shape((1, head_dim // 2, rows), F32)
    full = shape((1, rows, states), F32)
    grad_write, grad_read = call(vectors_kernel, (full, full), (shared, got_shared))
    grad_write, *arrived = lax.optimization_barrier((grad_write, *arrived))
    grad_key, grad_value, grad_alog, grad_skip, grad_bias = call(
        lambda *refs: finish_kernel(len(arrived), *refs),
        (half, half, vector, vector, vector),
        (*arrived, mine, got, tail),
    )
    grad_key, grad_value = grad_key.swapaxes(1, 2), grad_value.swapaxes(1, 2)
    return (
        grad_query,
        grad_key,
        grad_value,
        grad_gate,
        grad_write,
        grad_read,
        grad_dt,
        grad_alog,
        grad_skip,
        grad_bias,
    )


def solution(mesh):
    in_specs = (
        P("dp", "seq", "tp"),
        P("dp", "seq", "tp"),
        P("dp", "seq", "tp"),
        P("dp", "seq", "tp"),
        P("dp", "seq", None),
        P("dp", "seq", None),
        P("dp", "tp", "seq"),
        P("tp"),
        P("tp"),
        P("tp"),
        P("dp", "seq", "tp"),
    )
    out_specs = (
        P("dp", "seq", "tp"),
        P("dp", "seq", "tp"),
        P("dp", "seq", "tp"),
        P("dp", "seq", "tp"),
        P("dp", "seq", None),
        P("dp", "seq", None),
        P("dp", "tp", "seq"),
        P("tp"),
        P("tp"),
        P("tp"),
    )
    return jax.shard_map(body, mesh=mesh, in_specs=in_specs, out_specs=out_specs, check_vma=False)
```

```python
import jax
import jax.numpy as jnp
from jax import lax
from jax.experimental import pallas as pl
from jax.experimental.pallas import tpu as pltpu
from jax.sharding import PartitionSpec as P

NEG_FILL = -1e30
LOG2E = 1.4426950408889634
F32 = jnp.float32
BF16 = jnp.bfloat16
NN = (((1,), (0,)), ((), ()))
NT = (((1,), (1,)), ((), ()))
TN = (((0,), (0,)), ((), ()))


def dot(a, b, dims=NN):
    return lax.dot_general(a.astype(BF16), b.astype(BF16), dims, preferred_element_type=F32)


def parts_of(array, count):
    parts = []
    for _ in range(count):
        parts.append(array.astype(BF16))
        array = array - parts[-1].astype(F32)
    return parts


PARTS = 3


def flag_rows(*flags, count=PARTS):
    return jnp.concatenate([jnp.where(f, 1.0, 0.0).astype(BF16) for f in flags] * count, axis=0)


def dot_flags(arrays, rows, count=PARTS):
    split_up = [parts_of(a, count) for a in arrays]
    left = [parts[i] for i in range(count) for parts in split_up]
    return dot(jnp.concatenate(left, axis=1), rows)


def over(index, size):
    if size & (size - 1):
        return index // size
    return lax.shift_right_logical(index, size.bit_length() - 1)


def upto_rows(rows, count=PARTS):
    return flag_rows(iota((rows, rows), 0) <= iota((rows, rows), 1), count=count)


def head_rows(heads, channels, count=PARTS):
    shape = (heads, heads * channels)
    one = jnp.where(over(iota(shape, 1), channels) == iota(shape, 0), 1.0, 0.0)
    return jnp.concatenate([one.astype(BF16)] * count, axis=0)


def iota(shape, axis):
    return lax.broadcasted_iota(jnp.int32, shape, axis)


def column(ref, width):
    heads = ref.shape[0]
    at = iota((heads, width), 0)
    out = jnp.full((heads, width), ref[0], F32)
    for m in range(1, heads):
        out = jnp.where(at == m, ref[m], out)
    return out


def upright(vector, width):
    heads = vector.shape[0]
    square = jnp.broadcast_to(vector[...].reshape(1, heads), (heads, heads))
    square = jnp.where(iota((heads, heads), 0) == iota((heads, heads), 1), square, 0.0)
    return jnp.broadcast_to(jnp.sum(square, axis=1, keepdims=True), (heads, width))


def rates(raw, bias, alog, upto, count=PARTS):
    shifted = raw + bias
    step = jnp.maximum(shifted, 0.0) + jnp.log1p(jnp.exp(-jnp.abs(shifted)))
    rate = step * jnp.exp(alog)
    return step, rate, dot_flags([rate], upto, count)


def spread(cols, m, width):
    return jnp.broadcast_to(cols[:, m : m + 1], (cols.shape[0], width))


def widen(factors, channels, picked=None, count=PARTS):
    if picked is None:
        picked = head_rows(factors.shape[0], channels)
    return dot(jnp.concatenate(parts_of(factors, count), axis=0), picked, TN)


def stack(wide, width):
    return jnp.concatenate([wide[:, i : i + width] for i in range(0, wide.shape[1], width)], axis=0)


def unstack(tall, rows):
    return jnp.concatenate([tall[i : i + rows] for i in range(0, tall.shape[0], rows)], axis=1)


def attend(jobs, scale):
    shapes = [(q.shape[0] // m.shape[0],) + m.shape for q, _, _, m in jobs]
    scores = [
        jnp.where(m[None], (dot(q, k) * (scale * LOG2E)).reshape(dims), NEG_FILL)
        for (q, k, _, m), dims in zip(jobs, shapes)
    ]
    tops = [jnp.max(s, axis=2, keepdims=True) for s in scores]
    weights = [
        jnp.exp2(s - top).reshape(dims[0] * dims[1], dims[2])
        for s, top, dims in zip(scores, tops, shapes)
    ]
    both = [
        dot(w, jnp.concatenate([v, jnp.ones_like(v)], axis=0), NT)
        for w, (_, _, v, _) in zip(weights, jobs)
    ]
    width = jobs[0][2].shape[0]
    shares = [1.0 / b[:, width:] for b in both]
    return [(b[:, :width] * share, w, share) for b, w, share in zip(both, weights, shares)]


def slot_mask(here, query_slot, slots, rows):
    masks = []
    for slot in slots:
        if slot == query_slot:
            masks.append(iota((rows, rows), 0) >= iota((rows, rows), 1))
        else:
            seen = jnp.bitwise_xor(here, slot) < jnp.bitwise_xor(here, query_slot)
            masks.append(jnp.broadcast_to(seen, (rows, rows)))
    return jnp.concatenate(masks, axis=1)


def share_kernel(*refs):
    sources, (pack, message), held, arrived = refs[:10], refs[10:12], refs[12:22], refs[22]
    raw, gate, cotangent, read, query, write, alog, bias, key, value = held
    copies = [
        pltpu.make_async_copy(source, here, arrived.at[i])
        for i, (source, here) in enumerate(zip(sources, held))
    ]
    for place in (1, 2, 0, 6, 7, 3, 4, 8, 9, 5):
        copies[place].start()
    here = lax.axis_index("seq")
    heads, rows = raw.shape[1:]
    wide, states = gate.shape[2], read.shape[2]
    half = key.shape[1]
    upto, picked = upto_rows(rows, 2), head_rows(heads, wide // heads, 2)
    for place in (0, 6, 7):
        copies[place].wait()
    step, _, cum = rates(raw[0], upright(bias, rows), upright(alog, rows), upto, 2)
    decay = widen(jnp.exp(-cum), wide // heads, picked, 2)
    to_end = jnp.exp(cum - cum[:, rows - 1 :]) * step
    whole = jnp.broadcast_to(jnp.exp(-cum[:, rows - 1 :]), (heads, rows))
    tail = jnp.concatenate([to_end, whole], axis=0).astype(BF16)
    for place in (1, 2, 3):
        copies[place].wait()
    gate_f = gate[0].astype(F32)
    grad_mixed = cotangent[0].astype(F32) * gate_f * jax.nn.sigmoid(gate_f)
    entry = dot(read[0], grad_mixed * decay, TN).astype(BF16)
    for place in (4, 5, 8, 9):
        copies[place].wait()
    pack[:half] = key[0]
    pack[half:] = value[0]
    for bit in range(message.shape[0]):
        is_early = jnp.bitwise_and(lax.shift_right_logical(here, bit), 1) == 0
        for at in range(0, wide, states):
            message[bit, at : at + rows] = jnp.where(
                is_early, query[0, :, at : at + states], entry[:, at : at + states]
            )
        message[bit, wide : wide + half] = key[0]
        message[bit, wide + half : wide + 2 * half] = value[0]
        message[bit, wide + rows : wide + 2 * rows] = write[0]
        message[bit, wide + 2 * rows :] = tail


def prepare_kernel(gate, cotangent, write, read, raw, alog, skip, bias, *outs):
    mixed_out, slope_out, step_out, in_out, out_out, own_out, fall_out, back_out = outs[:8]
    ahead_out, split_out, rates_out, skip_out = outs[8:]
    heads, rows = raw.shape[1:]
    wide = gate.shape[2]
    channels = wide // heads
    pair = 2 * channels
    alog_c, bias_c = column(alog, rows), column(bias, rows)
    step, rate, cum = rates(raw[0], bias_c, alog_c, upto_rows(rows))
    for i, table in enumerate((step, rate, cum, jnp.exp(alog_c), jax.nn.sigmoid(raw[0] + bias_c))):
        rates_out[i * heads : (i + 1) * heads] = table
    head_of = over(iota(skip_out.shape, 1), channels)
    skip_w = jnp.full(skip_out.shape, skip[0], F32)
    for m in range(1, heads):
        skip_w = jnp.where(head_of == m, skip[m], skip_w)
    skip_out[...] = skip_w
    gate_f = gate[0].astype(F32)
    sig = jax.nn.sigmoid(gate_f)
    cot = cotangent[0].astype(F32)
    grad_mixed = cot * gate_f * sig
    mixed_out[...] = grad_mixed
    slope_out[...] = cot * sig * (1.0 + gate_f * (1.0 - sig))
    cum_cols = cum.T
    step_out[...] = widen(step, channels)
    in_out[...] = widen(jnp.exp(-cum), channels)
    out_out[...] = widen(jnp.exp(cum - cum[:, rows - 1 :]), channels)
    read_b, write_b = read[0], write[0]
    upper = iota((rows, rows), 0) <= iota((rows, rows), 1)
    lower = iota((rows, rows), 0) >= iota((rows, rows), 1)
    cross = jnp.where(lower, dot(read_b, write_b, NT), 0.0)
    cross_t = jnp.where(upper, dot(write_b, read_b, NT), 0.0)
    low = iota((rows, pair), 1) < channels
    for m in range(0, heads, 2):
        block = slice(m * channels, (m + 2) * channels)
        grad_p = grad_mixed[:, block]
        grad_d = jnp.concatenate(
            [jnp.where(low, grad_p, 0.0), jnp.where(low, 0.0, grad_p)], axis=0
        ).astype(BF16)
        split_out[m * rows : (m + 2) * rows] = grad_d
        backs = []
        for k in range(m, m + 2):
            gap = spread(cum_cols, k, rows) - cum[k : k + 1, :]
            fall = jnp.exp(-jnp.abs(gap))
            back = fall * cross_t
            at = slice(k * rows, (k + 1) * rows)
            fall_out[at] = fall
            back_out[at] = back
            ahead_out[:, at] = (fall * cross).astype(BF16)
            backs.append(back.astype(BF16))
        own_out[:, block] = dot(jnp.concatenate(backs, axis=1), grad_d)


def state_kernel(slots, scale, query, write, read, partner, *refs):
    mixed_in, step_in, in_in, out_in, own_in, fall_in, split_in, skip_in = refs[:8]
    refs = refs[8:]
    far, (pack, *messages) = refs[: slots - 1], refs[slots - 1 : 2 * slots - 1]
    refs = refs[2 * slots - 1 :]
    kept, sent, scores_out, keys_out, scaled_out, base_out, products_out = refs
    here = lax.axis_index("seq")
    parity = lax.axis_index("tp") % 2
    rows, wide = query.shape[1:]
    heads = fall_in.shape[0] // rows
    channels = wide // heads
    states, head_dim = write.shape[2], pack.shape[0]
    half, pair, count = head_dim // 2, 2 * channels, wide // head_dim
    key_parts, value_parts = [], []
    for slot in range(slots):
        near = messages[slot - 1][wide : wide + head_dim] if slot else pack[...]
        paired = far[slot - 1][...] if slot else partner[...]
        first = jnp.where(parity == 0, near, paired)
        second = jnp.where(parity == 0, paired, near)
        key_parts.append(jnp.concatenate([first[:half], second[:half]], axis=0))
        value_parts.append(jnp.concatenate([first[half:], second[half:]], axis=0))
    keys, values = jnp.concatenate(key_parts, axis=1), jnp.concatenate(value_parts, axis=1)
    keys_out[...] = keys

    grad_mixed, step_w, decay_in, decay_out = mixed_in[...], step_in[...], in_in[...], out_in[...]
    skip_w = skip_in[:1]
    read_b, write_b = read[0], write[0]
    tails = [m[wide + 2 * rows :].astype(F32) for m in messages]
    exit_t = jnp.zeros((states, wide), F32)
    early, to_ends = [], []
    for slot in range(1, slots):
        block = jnp.bitwise_xor(here, slot)
        early.append(block < here)
        between = jnp.ones((heads, rows), F32)
        for third in range(1, slots):
            if third != slot:
                at = jnp.bitwise_xor(here, third)
                inside = jnp.logical_and(
                    at > jnp.minimum(block, here), at < jnp.maximum(block, here)
                )
                between = between * jnp.where(inside, tails[third - 1][heads:], 1.0)
        later = unstack(messages[slot - 1][:wide], rows).astype(F32)
        if slots > 2:
            later = later * widen(between, channels)
        exit_t = exit_t + jnp.where(early[-1], 0.0, later)
        to_ends.append(widen(tails[slot - 1][:heads] * between, channels))
    exit_b = exit_t.astype(BF16)
    from_exit = decay_out * dot(write_b, exit_b)
    grad_scaled = own_in[...] + from_exit
    grad_inner = step_w * grad_scaled + skip_w * grad_mixed
    grads = stack(grad_inner, head_dim)
    grads_b = grads.astype(BF16)

    queries = stack(query[0], head_dim)
    jobs = [(queries, keys, values, slot_mask(here, 0, range(slots), rows))]
    for slot in range(1, slots):
        whole = slots > 2
        mask = slot_mask(here, slot, range(slots) if whole else [slot], rows)
        some = (keys, values) if whole else (key_parts[slot], value_parts[slot])
        jobs.append((messages[slot - 1][:wide], *some, mask))
    (attn, weights, share), *before = attend(jobs, scale)
    grad_probs = dot(grads_b, values)
    inner = unstack(attn, rows)
    scaled = inner * step_w
    scaled_b = scaled.astype(BF16)
    scaled_out[...] = scaled_b
    entry_t = jnp.zeros((states, wide), F32)
    for message, is_early, to_end, (attn_o, _, _) in zip(messages, early, to_ends, before):
        carried = unstack(attn_o, rows) * to_end
        end_state = dot(message[wide + rows : wide + 2 * rows], carried, TN)
        entry_t = entry_t + jnp.where(is_early, end_state, 0.0)
    entry_b = entry_t.astype(BF16)
    from_entry = decay_in * dot(read_b, entry_b)
    base_out[...] = from_entry + skip_w * inner

    product = grads * attn
    ones = jnp.ones((2 * head_dim, head_dim), BF16)
    delta = dot(jnp.concatenate(parts_of(product, 2), axis=1), ones)
    probs = weights * jnp.concatenate([share] * slots, axis=1)
    grad_scores = (probs * (grad_probs - jnp.concatenate([delta] * slots, axis=1))).astype(BF16)
    scores_out[...] = grad_scores
    key_t = (dot(queries, grad_scores, TN) * scale).astype(BF16)
    value_t = dot(grads_b, probs, TN).astype(BF16)
    for slot in range(slots):
        block = slice(slot * rows, (slot + 1) * rows)
        first = jnp.concatenate([key_t[:half, block], value_t[:half, block]], axis=0)
        second = jnp.concatenate([key_t[half:, block], value_t[half:, block]], axis=0)
        kept[slot] = jnp.where(parity == 0, first, second)
        sent[slot * head_dim : (slot + 1) * head_dim] = jnp.where(parity == 0, second, first)

    upper = iota((rows, rows), 0) <= iota((rows, rows), 1)
    grad_cross_t = jnp.zeros((rows, rows), F32)
    for m in range(0, heads, 2):
        outer = dot(
            scaled_b[:, m * channels : (m + 2) * channels], split_in[m * rows : (m + 2) * rows], NT
        )
        grad_cross_t = grad_cross_t + outer[:, :rows] * fall_in[m * rows : (m + 1) * rows]
        grad_cross_t = grad_cross_t + outer[:, rows:] * fall_in[(m + 1) * rows : (m + 2) * rows]
    grad_cross_t = jnp.where(upper, grad_cross_t, 0.0)
    grad_write = dot(grad_cross_t, read_b) + dot(scaled * decay_out, exit_b, NT)
    grad_read = dot(grad_cross_t, write_b, TN) + dot(grad_mixed * decay_in, entry_b, NT)
    sent[slots * head_dim : slots * head_dim + rows] = grad_write.astype(BF16)
    sent[slots * head_dim + rows :] = grad_read.astype(BF16)
    products = (inner * grad_scaled, inner * from_exit, grad_mixed * from_entry)
    for i, product in enumerate(products):
        products_out[i * rows : (i + 1) * rows] = product.astype(BF16)
    totals = [
        jnp.sum(grad_mixed * inner, axis=0, keepdims=True),
        jnp.sum(exit_t * entry_t, axis=0, keepdims=True),
    ]
    totals = jnp.concatenate(totals + [jnp.zeros((6, wide), F32)], axis=0)
    products_out[len(products) * rows :] = jnp.concatenate(parts_of(totals, 2), axis=0)


def rates_kernel(products, scaled, halves, back, tables, grad_raw, params):
    heads, rows = grad_raw.shape[1:]
    wide = products.shape[1]
    channels = wide // heads
    step, rate, cum, grow, slope = [tables[i * heads : (i + 1) * heads] for i in range(5)]
    strict = iota((rows, rows), 0) < iota((rows, rows), 1)
    lower = iota((rows, rows), 0) >= iota((rows, rows), 1)
    terms = []
    for m in range(0, heads, 2):
        outer = dot(
            scaled[:, m * channels : (m + 2) * channels], halves[m * rows : (m + 2) * rows], NT
        )
        terms.append((outer[:, :rows] * back[m * rows : (m + 1) * rows]).astype(BF16))
        terms.append((outer[:, rows:] * back[(m + 1) * rows : (m + 2) * rows]).astype(BF16))
    later = dot(jnp.concatenate(terms, axis=0), jnp.where(lower, 1.0, 0.0))
    rate_rows = [
        jnp.sum(jnp.where(strict, later[m * rows : (m + 1) * rows], 0.0), axis=0, keepdims=True)
        for m in range(heads)
    ]
    pick = (over(iota((heads, wide), 1), channels) == iota((heads, wide), 0)).astype(BF16)
    sums = dot(pick, products[...], NT)
    grad_step = sums[:, :rows]
    exit_sum = sums[:, rows : 2 * rows] * step
    entry_sum = sums[:, 2 * rows : 3 * rows]
    totals = sums[:, 3 * rows : 3 * rows + 8] + sums[:, 3 * rows + 8 :]
    skip_sum = jnp.where(iota((heads, rows), 1) == 0, totals[:, :1], 0.0)
    carry_sum = totals[:, 1:2] * jnp.exp(-cum[:, rows - 1 :])
    grad_rate = -(
        jnp.concatenate(rate_rows, axis=0)
        + dot_flags([entry_sum, exit_sum], flag_rows(lower, strict))
        + carry_sum
    )
    grad_shift = (grad_step + grad_rate * grow) * slope
    grad_raw[0] = grad_shift
    terms = jnp.concatenate([grad_rate * rate, skip_sum, grad_shift], axis=0)
    summed = jnp.concatenate(parts_of(terms, 3), axis=1)
    params[:, : 3 * heads] = dot(jnp.ones((8, 3 * rows), F32), summed, NT)
    params[:, 3 * heads :] = jnp.zeros((8, params.shape[1] - 3 * heads), F32)


def output_kernel(scale, ahead, scaled, base, slope, scores, keys, grad_gate, grad_query):
    rows, wide = base.shape
    channels = wide * rows // ahead.shape[1]
    pair = 2 * channels
    low = iota((rows, pair), 1) < channels
    for at in range(0, wide, pair):
        block = slice(at, at + pair)
        scaled_p = scaled[:, block].astype(F32)
        scaled_d = jnp.concatenate(
            [jnp.where(low, scaled_p, 0.0), jnp.where(low, 0.0, scaled_p)], axis=0
        )
        m = at // channels
        mixed = dot(ahead[:, m * rows : (m + 2) * rows], scaled_d) + base[:, block]
        grad_gate[0, :, block] = mixed * slope[:, block]
    grad_query[0] = unstack(dot(scores[...], keys[...], NT) * scale, rows)


def vectors_kernel(mine, other, grad_write, grad_read):
    rows = grad_write.shape[1]
    both = mine[...].astype(F32) + other[...].astype(F32)
    grad_write[0] = both[:rows]
    grad_read[0] = both[rows:]


def finish_kernel(count, *refs):
    arrived, (mine, other, tail) = refs[:count], refs[count : count + 3]
    grad_key, grad_value, grad_alog, grad_skip, grad_bias = refs[count + 3 :]
    half, rows = grad_key.shape[1:]
    total = mine[0].astype(F32) + other[: 2 * half].astype(F32)
    for term in arrived:
        total = total + term[: 2 * half].astype(F32)
    grad_key[0] = total[:half]
    grad_value[0] = total[half:]
    heads = grad_alog.shape[0]
    params = joined(tail[...]) + joined(arrived[-1][2 * half :])
    grad_alog[...] = params[0, :heads]
    grad_skip[...] = params[0, heads : 2 * heads]
    grad_bias[...] = params[0, 2 * heads : 3 * heads]


def split(sums):
    high = lax.reduce_precision(sums, 8, 7)
    return jnp.concatenate([high.astype(BF16), (sums - high).astype(BF16)], axis=0)


def joined(tail):
    tail = tail.astype(F32)
    count = tail.shape[0] // 2
    return tail[:count] + tail[count:]


def flip(axis, distance):
    return [(i, i ^ distance) for i in range(lax.axis_size(axis))]


def shape(dims, dtype):
    return jax.ShapeDtypeStruct(tuple(dims), dtype)


VMEM = pl.BlockSpec(memory_space=pltpu.VMEM)
SMEM = pl.BlockSpec(memory_space=pltpu.SMEM)
HBM = pl.BlockSpec(memory_space=pltpu.HBM)
PARAMS = pltpu.CompilerParams(vmem_limit_bytes=48 * 1024 * 1024)


def call(kernel, outs, args, specs=None):
    return pl.pallas_call(
        kernel,
        out_shape=outs,
        in_specs=[(specs or {}).get(i, VMEM) for i in range(len(args))],
        out_specs=jax.tree.map(lambda _: VMEM, outs),
        compiler_params=PARAMS,
        cost_estimate=pl.CostEstimate(flops=0, bytes_accessed=0, transcendentals=0),
    )(*args)


def swap(array, seq_bits, tp_bits):
    n_seq, n_tp = lax.axis_size("seq"), lax.axis_size("tp")
    pairs = [
        (s * n_tp + t, (s ^ seq_bits) * n_tp + (t ^ tp_bits))
        for s in range(n_seq)
        for t in range(n_tp)
    ]
    return lax.ppermute(array, ("seq", "tp"), pairs)


def body(
    query_rows,
    key_rows,
    value_rows,
    gate_rows,
    write_vec,
    read_vec,
    dt_raw,
    a_log,
    skip_gain,
    dt_bias,
    out_grad,
):
    slots = lax.axis_size("seq")
    rows, wide = query_rows.shape[1:]
    head_dim = 2 * key_rows.shape[2]
    states = write_vec.shape[2]
    heads = a_log.shape[0]
    scale = head_dim ** (-0.5)

    bits = slots.bit_length() - 1
    key_t, value_t = key_rows.swapaxes(1, 2), value_rows.swapaxes(1, 2)
    kept_here = (dt_raw, gate_rows, out_grad, read_vec, query_rows, write_vec)
    sources = kept_here + (a_log, dt_bias, key_t, value_t)
    pack, message, dt_raw, gate_rows, out_grad, read_vec, query_rows, write_vec = pl.pallas_call(
        share_kernel,
        out_shape=(
            shape((head_dim, rows), BF16),
            shape((bits, wide + 2 * rows + 2 * heads, head_dim), BF16),
        )
        + tuple(shape(a.shape, a.dtype) for a in kept_here),
        in_specs=[HBM] * len(sources),
        out_specs=(VMEM,) * (2 + len(kept_here)),
        scratch_shapes=[
            pltpu.VMEM(a.shape, a.dtype) for a in sources[len(kept_here) :]
        ]
        + [pltpu.SemaphoreType.DMA((len(sources),))],
        compiler_params=PARAMS,
    )(*[pltpu.with_memory_space_constraint(a, pltpu.HBM) for a in sources])
    messages = [swap(message[slot.bit_length() - 1], slot, 0) for slot in range(1, slots)]
    partner = swap(pack, 0, 1)
    far = [swap(pack, slot, 1) for slot in range(1, slots)]

    wide_f, wide_b = shape((rows, wide), F32), shape((rows, wide), BF16)
    tall_f = shape((heads * rows, rows), F32)
    prepared = call(
        prepare_kernel,
        (wide_f,) * 6
        + (tall_f, tall_f)
        + (shape((rows, heads * rows), BF16), shape((heads * rows, 2 * wide // heads), BF16))
        + (shape((5 * heads, rows), F32), shape((8, wide), F32)),
        (gate_rows, out_grad, write_vec, read_vec, dt_raw, a_log, skip_gain, dt_bias),
        {5: SMEM, 6: SMEM, 7: SMEM},
    )
    grad_mixed, slope, step_w, decay_in, decay_out, own, fall, back = prepared[:8]
    ahead, halves, tables, skip_w = prepared[8:]
    mine, other, scores, keys, scaled, base, products = call(
        lambda *refs: state_kernel(slots, scale, *refs),
        (
            shape((slots, head_dim, rows), BF16),
            shape((slots * head_dim + 2 * rows, states), BF16),
            shape((wide // head_dim * rows, slots * rows), BF16),
            shape((head_dim, slots * rows), BF16),
            wide_b,
            wide_f,
            shape((3 * rows + 16, wide), BF16),
        ),
        (
            query_rows,
            write_vec,
            read_vec,
            partner,
            grad_mixed,
            step_w,
            decay_in,
            decay_out,
            own,
            fall,
            halves,
            skip_w,
            *far,
            pack,
            *messages,
        ),
    )
    got = swap(other, 0, 1)
    grad_dt, params = call(
        rates_kernel,
        (shape((1, heads, rows), F32), shape((8, states), F32)),
        (products, scaled, halves, back, tables),
    )
    shared, got_shared = other[slots * head_dim :], got[slots * head_dim :]
    reach = 2
    while reach < lax.axis_size("tp"):
        shared = (shared.astype(F32) + got_shared.astype(F32)).astype(BF16)
        got_shared = swap(shared, 0, reach)
        reach *= 2
    reach = 1
    while reach < lax.axis_size("dp"):
        near = [params] + [lax.ppermute(params, "dp", flip("dp", k * reach)) for k in (1, 2, 3)]
        shared, *near = lax.optimization_barrier((shared, *near))
        params = (near[0] + near[1]) + (near[2] + near[3])
        reach *= 4
    sent = [
        (mine[slot].astype(F32) + got[slot * head_dim : (slot + 1) * head_dim].astype(F32)).astype(BF16)
        for slot in range(1, slots)
    ]
    arrived = [swap(sent[slot - 1], slot, 0) for slot in range(1, slots) if slot & (slot - 1)]
    slot = 1
    while slot < slots:
        tail = split(params)
        arrived.append(swap(jnp.concatenate([sent[slot - 1], tail], axis=0), slot, 0))
        slot *= 2
        if slot < slots:
            params = joined(tail) + joined(arrived[-1][head_dim:])
    scores, shared = lax.optimization_barrier((scores, shared))
    grad_gate, grad_query = call(
        lambda *refs: output_kernel(scale, *refs),
        (shape((1, rows, wide), F32), shape((1, rows, wide), F32)),
        (ahead, scaled, base, slope, scores, keys),
    )
    vector = shape((heads,), F32)
    half = shape((1, head_dim // 2, rows), F32)
    full = shape((1, rows, states), F32)
    grad_write, grad_read = call(vectors_kernel, (full, full), (shared, got_shared))
    grad_write, *arrived = lax.optimization_barrier((grad_write, *arrived))
    grad_key, grad_value, grad_alog, grad_skip, grad_bias = call(
        lambda *refs: finish_kernel(len(arrived), *refs),
        (half, half, vector, vector, vector),
        (*arrived, mine, got, tail),
    )
    grad_key, grad_value = grad_key.swapaxes(1, 2), grad_value.swapaxes(1, 2)
    return (
        grad_query,
        grad_key,
        grad_value,
        grad_gate,
        grad_write,
        grad_read,
        grad_dt,
        grad_alog,
        grad_skip,
        grad_bias,
    )


def solution(mesh):
    in_specs = (
        P("dp", "seq", "tp"),
        P("dp", "seq", "tp"),
        P("dp", "seq", "tp"),
        P("dp", "seq", "tp"),
        P("dp", "seq", None),
        P("dp", "seq", None),
        P("dp", "tp", "seq"),
        P("tp"),
        P("tp"),
        P("tp"),
        P("dp", "seq", "tp"),
    )
    out_specs = (
        P("dp", "seq", "tp"),
        P("dp", "seq", "tp"),
        P("dp", "seq", "tp"),
        P("dp", "seq", "tp"),
        P("dp", "seq", None),
        P("dp", "seq", None),
        P("dp", "tp", "seq"),
        P("tp"),
        P("tp"),
        P("tp"),
    )
    return jax.shard_map(body, mesh=mesh, in_specs=in_specs, out_specs=out_specs, check_vma=False)
```
